128 devices in a mesh: grp: 2 (over core), row: 16 (over y, x), col: 4 (over z).
Axes of the slice: x: 4, y: 4, z: 4, core: 2. Of those that a mesh axis runs over, the one named last changes fastest.
Arguments:
- channels: bfloat16 [6, 4096, 8192], P('grp', 'row', 'col'), may hold values from -0.06629126 to 0.06629126, as said below
- inverse: float32 [6, 4096, 4096], P('grp', 'row', 'col'), may hold values from -1 to 1, as said below
- arrivals: bfloat16 [6, 3, 192, 8192], P(None, None, ('grp', 'row'), 'col'), may hold values from -0.06629126 to 0.06629126
- arrival_cell: int32 [6, 3, 128, 1], replicated, may hold values from 0 to 31; in each aligned block of 128 rows (0 to 127, 128 to 255, ..., all dimensions but the last counted through in order) at most 6 rows name the same one
- cell_owner: int32 [32], replicated, may hold values from 0 to 31, each once
- slots: int32 [6, 3, 128], replicated, may hold values from 0 to 4095, as said below
- symbols: bfloat16 [6, 4096, 256], P('grp', 'col'), may hold values from -45 to 45
Outputs:
- updated_inverse: float32 [6, 4096, 4096], P('grp', 'row', 'col')
- transmit: float32 [256, 6, 8192], P('row', 'grp', 'col')
The draws below stay inside these ranges and needn't reach their ends.
Inputs may be any that keep to these rules, and one draw needn't show every extreme that they name: In each group the 3 x 128 slots are distinct. `inverse`: Symmetric; in each group the rows and columns at that group's slots are those of the identity. `channels`: rows at a group's slots are zero. `arrival_cell`: in each group and epoch at most 6 arriving users share a cell.
All inputs are finite; a program needn't handle non-finite values.
Results may differ from the reference program's by a relative error of at most 0.0031.
Values may be sent and summed in bfloat16 or wider, within the bound.
No kernel may reach another device: no remote copies, remote signals or barrier semaphores. Data moves between devices by JAX's collectives and lax.ppermute only.
A program may use at most 128 MiB of HBM per device.

```python
import math
import jax
import jax.numpy as jnp
import numpy as np
from jax import lax

USERS = 4096
ANTENNAS = 8192
ARRIVE = 128
EPOCHS = 3
STREAMS = 256
GROUPS = 6
CELLS = 32
CAPACITY = 6


def slot_order(key):
    group_keys = jax.random.split(jax.random.fold_in(key, 101), GROUPS)
    return jax.vmap(lambda single: jax.random.permutation(single, USERS))(group_keys).astype(jnp.int32)


def empty_rows(key):
    ordering = slot_order(key)
    placement_rank = jnp.argsort(ordering, axis=1)
    return placement_rank < EPOCHS * ARRIVE


def antenna_gain():
    return 2.0 ** (jnp.arange(ANTENNAS, dtype=jnp.float32) / ANTENNAS - 0.5)


def draw_channels(key, part):
    emptied = empty_rows(key)
    key = jax.random.fold_in(key, 3)
    first_key = jax.random.fold_in(key, 0)
    base_draw = jax.random.truncated_normal(first_key, -4.0, 4.0, (GROUPS, USERS, ANTENNAS), jnp.float32)
    values = base_draw * antenna_gain() / math.sqrt(ANTENNAS)
    return jnp.where(emptied[:, :, None], 0.0, values).astype(jnp.bfloat16)


def draw_inverse(key, part):
    emptied = empty_rows(key)
    key = jax.random.fold_in(key, 5)
    group_keys = jax.random.split(key, GROUPS)
    eye_mask = jnp.eye(USERS, dtype=bool)
    spread_bound = 0.45 / math.sqrt(USERS)

    def one_block(inputs):
        single, empty_one = inputs
        first_key, second_key = jax.random.split(single)
        diagonal = jnp.exp(jax.random.uniform(first_key, (USERS,), jnp.float32, math.log(0.4), math.log(0.9)))
        spread_part = jax.random.uniform(second_key, (USERS, USERS), jnp.float32, -spread_bound, spread_bound)
        spread_part = 0.5 * (spread_part + spread_part.T)
        block = jnp.where(eye_mask, diagonal[:, None], spread_part)
        cleared = empty_one[:, None] | empty_one[None, :]
        return jnp.where(cleared, jnp.where(eye_mask, 1.0, 0.0), block).astype(jnp.float32)
    return lax.map(one_block, (group_keys, emptied))


def draw_arrivals(key, part):
    key = jax.random.fold_in(key, 7)
    first_key = jax.random.fold_in(key, 0)
    extent = (GROUPS, EPOCHS, CELLS * CAPACITY, ANTENNAS)
    base_draw = jax.random.truncated_normal(first_key, -4.0, 4.0, extent, jnp.float32)
    return (base_draw * antenna_gain() / math.sqrt(ANTENNAS)).astype(jnp.bfloat16)


def draw_slots(key, part):
    ordering = slot_order(key)
    return ordering[:, :EPOCHS * ARRIVE].reshape(GROUPS, EPOCHS, ARRIVE).astype(jnp.int32)


def draw_symbols(key, part):
    key = jax.random.fold_in(key, 11)
    first_key = jax.random.fold_in(key, 0)
    column_scale = 10.0 ** (jnp.arange(STREAMS, dtype=jnp.float32) / STREAMS)
    base_draw = jax.random.truncated_normal(first_key, -4.0, 4.0, (GROUPS, USERS, STREAMS), jnp.float32)
    return (base_draw * column_scale).astype(jnp.bfloat16)


def shared_out(rng, own, number, rows, count, top, most, skew):
    order = jax.random.permutation(rng, count)
    packed, common = shares(count, rows * top, most, skew, True), shares(count, rows * top, most, skew, False)
    places = jnp.arange(count)

    def named(tallies, offset_by):
        used = int((tallies > 0).sum())
        fixed = max(1, used // 4)
        shifted = fixed + (places - fixed + offset_by * (used - fixed)) % max(1, count - fixed)
        return jnp.zeros((count,), jnp.int32).at[order[jnp.where(places < fixed, places, shifted)]].set(jnp.asarray(tallies, jnp.int32))

    tallies = jnp.where(number % 4 == 0, named(packed, number // 4), named(common, number - number // 4 - 1))
    mixed = jax.random.permutation(jax.random.fold_in(own, 3), count)
    source_of, receiver = mixed[0:count // 2 * 2:2], mixed[1:count // 2 * 2:2]
    room = jnp.minimum(tallies[source_of] - 1, most - tallies[receiver]) // 2
    room = jnp.where((source_of == order[0]) | (receiver == order[0]) | (tallies[receiver] == 0), 0, jnp.maximum(room, 0))
    shifted = jax.random.randint(jax.random.fold_in(own, 4), (count // 2,), 0, 1 << 20) % (room + 1)
    tallies = tallies.at[source_of].add(-shifted).at[receiver].add(shifted)
    members = jnp.searchsorted(jnp.cumsum(tallies), jnp.arange(rows * top), side="right").astype(jnp.int32)
    table = members.reshape(top, rows).T
    table = table[jax.random.permutation(jax.random.fold_in(own, 1), rows)]
    offset_by = jax.random.randint(jax.random.fold_in(own, 2), (rows, 1), 0, top)
    return jnp.take_along_axis(table, (jnp.arange(top)[None, :] + offset_by) % top, axis=1)


def shares(count, total, limit, slope, full):
    portions = [(1 << 20) // math.isqrt(grade ** slope) + 1 for grade in range(1, count + 1)]
    largest = limit if full else min(limit, max(-(-total // count), total * portions[0] // sum(portions)))
    least = 1 if total - largest >= count - 1 else 0
    counts, rest = [largest] + [least] * (count - 1), total - largest - least * (count - 1)
    while rest > 0:
        candidates = [i for i in range(1, count) if counts[i] < largest] or [i for i in range(1, count) if counts[i] < limit]
        mass, budget = sum([portions[i] for i in candidates]), rest
        for i in candidates:
            addition = min(limit - counts[i], max(1, budget * portions[i] // mass), rest)
            counts[i] = counts[i] + addition
            rest = rest - addition
    return np.array(counts)


def setup_inputs(seed: int = 0) -> dict:
    key_of = jax.random.split(jax.random.key(seed), 8)
    channels = draw_channels(jax.random.fold_in(key_of[7], 71), 0)
    inverse = draw_inverse(jax.random.fold_in(key_of[7], 71), 0)
    arrivals = draw_arrivals(jax.random.fold_in(key_of[7], 71), 0)
    arrival_cell_keys = jax.random.split(jax.random.fold_in(key_of[3], 1), GROUPS * EPOCHS * ARRIVE // ARRIVE)
    arrival_cell_turns = jax.random.permutation(jax.random.fold_in(key_of[3], 3), GROUPS * EPOCHS * ARRIVE // ARRIVE)
    arrival_cell = jax.vmap(lambda own, number: shared_out(jax.random.fold_in(key_of[3], 2), own, number, ARRIVE, CELLS, 1, CAPACITY, 2))(arrival_cell_keys, arrival_cell_turns).reshape((GROUPS, EPOCHS, ARRIVE, 1))
    cell_owner = jax.random.permutation(key_of[4], CELLS).astype(jnp.int32)
    slots = draw_slots(jax.random.fold_in(key_of[7], 71), 0)
    symbols = draw_symbols(jax.random.fold_in(key_of[7], 71), 0)
    return {"channels": channels, "inverse": inverse, "arrivals": arrivals, "arrival_cell": arrival_cell, "cell_owner": cell_owner, "slots": slots, "symbols": symbols}


loading = 1.0
epsilon = 1e-06
highest = lax.Precision.HIGHEST

def arrival_rows(cells, owners):
    arrival_order = jnp.arange(cells.shape[0], dtype=jnp.int32)
    earlier = (cells[:, None] == cells[None, :]) & (arrival_order[:, None] < arrival_order[None, :])
    ranking = lax.optimization_barrier(jnp.sum(earlier.astype(jnp.int32), axis=0))
    return (owners[cells] * CAPACITY + ranking).astype(jnp.int32)

def one_group(channel, inverse_now, arrive_rows, cells_all, cell_owner, slot_all, symbol):
    for period in range(EPOCHS):
        position = arrival_rows(cells_all[period, :, 0], cell_owner)
        newcomer = arrive_rows[period][position]
        columns = jnp.dot(channel.astype(jnp.float32), newcomer.T.astype(jnp.float32), preferred_element_type=jnp.float32)
        gram_new = jnp.dot(newcomer.astype(jnp.float32), newcomer.T.astype(jnp.float32), preferred_element_type=jnp.float32) + loading * jnp.eye(ARRIVE, dtype=jnp.float32)
        weighted = jnp.dot(inverse_now, columns, precision=highest)
        schur_block = gram_new - jnp.dot(columns.T, weighted, precision=highest)
        factor = jnp.linalg.cholesky(schur_block)
        slot_now = slot_all[period]
        placing = (jnp.arange(USERS, dtype=jnp.int32)[:, None] == slot_now[None, :]).astype(jnp.float32)
        border = weighted - placing
        solved = jax.scipy.linalg.solve_triangular(factor, border.T, lower=True)
        filled = lax.optimization_barrier(jnp.sum(placing, axis=1))
        inverse_now = inverse_now - jnp.diag(filled) / loading + jnp.dot(solved.T, solved, precision=highest)
        channel = channel.at[slot_now].set(newcomer)
    users_side = jnp.dot(inverse_now, symbol.astype(jnp.float32), precision=highest).astype(jnp.bfloat16)
    signal = jnp.dot(users_side.T.astype(jnp.float32), channel.astype(jnp.float32), preferred_element_type=jnp.float32)
    total_power = jnp.mean(signal * signal)
    return (inverse_now, signal * lax.rsqrt(total_power + epsilon))

def reference(channels, inverse, arrivals, arrival_cell, cell_owner, slots, symbols):
    inverses = []
    signals = []
    for member in range(GROUPS):
        updated, signal = one_group(channels[member], inverse[member], arrivals[member], arrival_cell[member], cell_owner, slots[member], symbols[member])
        inverses.append(updated)
        signals.append(signal)
    return (jnp.stack(inverses, axis=0), jnp.stack(signals, axis=1))
```

```python
import jax
import jax.numpy as jnp
from jax import lax
from jax.experimental import pallas as pl
from jax.experimental.pallas import tpu as pltpu
from jax.sharding import PartitionSpec as P

ANTENNAS = 8192
ARRIVE = 128
EPOCHS = 3
STREAMS = 256
TOTAL = ARRIVE * EPOCHS
BLOCK = 128

loading = 1.0
epsilon = 1e-06
highest = lax.Precision.HIGHEST
f32 = jnp.float32
bf16 = jnp.bfloat16


def split_dot(a, b):
    a_hi = a.astype(bf16)
    a_lo = (a - a_hi.astype(f32)).astype(bf16)
    b_hi = b.astype(bf16)
    b_lo = (b - b_hi.astype(f32)).astype(bf16)
    total = jnp.dot(a_hi, b_lo, preferred_element_type=f32)
    total += jnp.dot(a_lo, b_hi, preferred_element_type=f32)
    return total + jnp.dot(a_hi, b_hi, preferred_element_type=f32)


def invert_block(a):
    lane = lax.broadcasted_iota(jnp.int32, (1, BLOCK), 1)
    rows = lax.broadcasted_iota(jnp.int32, (BLOCK, 1), 0)
    for k in range(BLOCK):
        pivot = a[k:k + 1, k:k + 1]
        scaled = jnp.where(lane == k, 1.0, a[k:k + 1, :]) * (1.0 / pivot)
        unit = (rows == k).astype(f32)
        column = a[:, k:k + 1]
        a = jnp.where(lane == k, unit, a) - (column - unit) * scaled
    return a


def inverse_kernel(t_ref, z_ref, inv_ref, e_ref):
    inv_ref[...] = t_ref[...]

    @pl.loop(0, TOTAL // BLOCK)
    def _(b):
        start = pl.multiple_of(b * BLOCK, BLOCK)
        here = pl.ds(start, BLOCK)
        pivot_inv = invert_block(inv_ref[here, here])
        panel = inv_ref[:, here]
        row_id = lax.broadcasted_iota(jnp.int32, (TOTAL, BLOCK), 0)
        lane_id = lax.broadcasted_iota(jnp.int32, (TOTAL, BLOCK), 1)
        unit = (row_id == lane_id + start).astype(f32)
        inv_ref[:, here] = unit
        rows = inv_ref[here, :]
        scaled = split_dot(pivot_inv, rows)
        inside = (row_id >= start) & (row_id < start + BLOCK)
        rest = jnp.where(inside, 0.0, panel)
        inv_ref[here, :] = jnp.zeros((BLOCK, TOTAL), f32)
        inv_ref[...] = inv_ref[...] - split_dot(rest, scaled)
        inv_ref[here, :] = scaled

    e_ref[...] = split_dot(inv_ref[...], z_ref[...])


def invert(t, z):
    return pl.pallas_call(
        inverse_kernel,
        out_shape=(
            jax.ShapeDtypeStruct((TOTAL, TOTAL), f32),
            jax.ShapeDtypeStruct((TOTAL, STREAMS), f32),
        ),
        in_specs=[pl.BlockSpec(memory_space=pltpu.VMEM)] * 2,
        out_specs=(pl.BlockSpec(memory_space=pltpu.VMEM),) * 2,
        compiler_params=pltpu.CompilerParams(vmem_limit_bytes=32 * 1024 * 1024),
    )(t, z)


def local(channels, inverse, arrivals, arrival_cell, cell_owner, slots, symbols):
    group_count, user_rows, antennas = channels.shape
    user_cols = inverse.shape[2]
    capacity = arrivals.shape[2]
    cell_count = cell_owner.shape[0]
    grp_index = lax.axis_index("grp")
    row_index = lax.axis_index("row")
    col_index = lax.axis_index("col")
    y_index, x_index = row_index // 4, row_index % 4
    x_groups = [[4 * y + x for x in range(4)] for y in range(4)]

    def along_x(value, step):
        pairs = [(4 * y + x, 4 * y + (x + step) % 4) for y in range(4) for x in range(4)]
        return lax.ppermute(value, "row", pairs)

    def along_y(value, step):
        pairs = [(4 * y + x, 4 * ((y + step) % 4) + x) for y in range(4) for x in range(4)]
        return lax.ppermute(value, "row", pairs)

    def along_z(value, step):
        return lax.ppermute(value, "col", [(z, (z + step) % 4) for z in range(4)])

    def to_planes(value):
        padded = jnp.concatenate([value, jnp.zeros_like(value[:1])], axis=0)
        return lax.all_to_all(padded, "col", 0, 0, tiled=True)

    first_group = grp_index * group_count
    other_first = (1 - grp_index) * group_count

    with jax.named_scope("newcomers"):
        mine = lax.dynamic_slice_in_dim(arrivals, first_group, group_count, 0)
        theirs = lax.dynamic_slice_in_dim(arrivals, other_first, group_count, 0)
        swapped = lax.ppermute(theirs, "grp", [(0, 1), (1, 0)])
        from_0 = jnp.where(grp_index == 0, mine, swapped)
        from_1 = jnp.where(grp_index == 0, swapped, mine)
        chunk = jnp.stack([from_0, from_1], axis=2)
        per_group = EPOCHS * 2 * capacity
        chunk = chunk.reshape(group_count * per_group, antennas)
        chunk = jnp.pad(chunk, ((0, 112 - group_count * per_group), (0, 0)))
        gathered = lax.all_gather(chunk, "row")

    with jax.named_scope("planes"):
        full_rows = to_planes(inverse.astype(bf16))
        by_x = full_rows.reshape(4, user_rows, 4, user_rows).transpose(2, 1, 0, 3)
        square = lax.all_to_all(by_x, "row", 0, 0, axis_index_groups=x_groups, tiled=True)
        square = jnp.roll(square, (-x_index, -y_index), axis=(0, 2))
        square = square.reshape(4 * user_rows, 4 * user_rows)
        symbol_part = jnp.einsum(
            "grc,gcs->grs", inverse, symbols.astype(f32), precision=highest
        )
        precoded = jnp.sum(to_planes(symbol_part), axis=0)

    plane_group = first_group + jnp.minimum(col_index, group_count - 1)
    slot_plane = lax.dynamic_slice_in_dim(slots, plane_group, 1, 0).reshape(TOTAL)
    row_ids = row_index * user_rows + jnp.arange(user_rows, dtype=jnp.int32)
    place_rows = (slot_plane[None, :] == row_ids[:, None]).astype(f32)

    cells_mine = lax.dynamic_slice_in_dim(arrival_cell, first_group, group_count, 0)[..., 0]
    slots_mine = lax.dynamic_slice_in_dim(slots, first_group, group_count, 0)
    cell_table = (cells_mine[..., None] == jnp.arange(cell_count, dtype=jnp.int32)).astype(
        jnp.int32
    )
    owners = jnp.sum(cell_table * cell_owner, axis=-1)
    arrival_order = jnp.arange(ARRIVE, dtype=jnp.int32)
    earlier = (cells_mine[..., :, None] == cells_mine[..., None, :]) & (
        arrival_order[:, None] < arrival_order[None, :]
    )
    ranking = jnp.sum(earlier.astype(jnp.int32), axis=-2)
    window = 40
    rows_of = jnp.arange(16, dtype=jnp.int32)[:, None]
    with jax.named_scope("pick"):
        picked = []
        for g in range(group_count):
            start = g * per_group // 8 * 8
            epoch = jnp.arange(EPOCHS, dtype=jnp.int32)[:, None]
            inside = g * per_group - start + epoch * 2 * capacity
            inside = inside + owners[g] // 16 * capacity + ranking[g]
            place = (owners[g] % 16 * window + inside).reshape(TOTAL)
            choose = (place[:, None] == jnp.arange(16 * window, dtype=jnp.int32)[None, :]).astype(
                bf16
            )
            source = gathered[:, start:start + window].reshape(16 * window, antennas)
            picked.append(jnp.dot(choose, source, preferred_element_type=f32).astype(bf16))
        newcomers = jnp.stack(picked, axis=0)

    with jax.named_scope("columns"):
        share = TOTAL // 16
        few = lax.dynamic_slice_in_dim(newcomers, row_index * share, share, 1)
        column_part = jnp.einsum(
            "gkm,gjm->gkj", channels, newcomers, preferred_element_type=f32
        )
        gram_part = jnp.einsum("gkm,gjm->gkj", few, newcomers, preferred_element_type=f32)
        both = jnp.concatenate([column_part, gram_part], axis=1).astype(bf16)
        summed = jnp.sum(to_planes(both).astype(f32), axis=0)
        columns = summed[:user_rows]
        gram = summed[user_rows:]
        own = columns.astype(bf16)
        by_row = jnp.concatenate([own] + [along_x(own, -d) for d in (1, 2, 3)], axis=0)
        by_col = jnp.concatenate([own] + [along_y(own, -d) for d in (1, 2, 3)], axis=0)

    with jax.named_scope("schur"):
        partial = jnp.dot(square, by_col, preferred_element_type=f32)
        partial_low = partial.astype(bf16)
        schur_part = lax.dot_general(
            by_row, partial_low, (((0,), (0,)), ((), ())), preferred_element_type=f32
        )
        target_part = lax.dot_general(
            columns - place_rows, precoded, (((0,), (0,)), ((), ())), precision=highest
        )
        pieces = [partial[:user_rows]]
        for d in (1, 2, 3):
            block = partial_low[d * user_rows:(d + 1) * user_rows]
            pieces.append(along_x(block, d).astype(f32))
        weighted = pieces[0] + pieces[1] + pieces[2] + pieces[3]
        packed = jnp.concatenate([schur_part, target_part], axis=1).astype(bf16)
        packed = packed.reshape(16, share, TOTAL + STREAMS)
        shared = lax.all_to_all(packed, "row", 0, 0, tiled=True).astype(f32)
        shared = jnp.sum(shared, axis=0)
        share_ids = row_index * share + jnp.arange(share, dtype=jnp.int32)
        identity = loading * (
            share_ids[:, None] == jnp.arange(TOTAL, dtype=jnp.int32)[None, :]
        ).astype(f32)
        schur_rows = gram + identity - shared[:, :TOTAL]
        ready = jnp.concatenate([schur_rows, shared[:, TOTAL:]], axis=1)
        ready = jnp.broadcast_to(ready[None], (16, share, TOTAL + STREAMS))
        whole = lax.all_to_all(ready, "row", 0, 0, tiled=True).reshape(TOTAL, TOTAL + STREAMS)

    with jax.named_scope("solve"):
        schur_inverse, effect = invert(whole[:, :TOTAL], whole[:, TOTAL:])

    with jax.named_scope("users"):
        weighted_all = lax.all_gather(weighted.astype(bf16), "row")
        border_rows = weighted - place_rows
        filled = jnp.sum(place_rows, axis=1)
        users = precoded * (1.0 - filled)[:, None] + jnp.dot(
            border_rows, effect, precision=highest
        )
        users = jnp.broadcast_to(users.astype(bf16)[None], (4, user_rows, STREAMS))
        users_side = lax.all_to_all(users, "col", 0, 0, tiled=True)[:group_count]

    with jax.named_scope("signal"):
        slot_all = slots_mine.reshape(group_count, TOTAL)
        placing = (slot_all[:, None, :] == row_ids[None, :, None]).astype(bf16)
        channel = channels + jnp.einsum(
            "gkj,gjm->gkm", placing, newcomers, preferred_element_type=f32
        ).astype(bf16)
        signal_part = jnp.einsum(
            "gks,gkm->gsm", users_side, channel, preferred_element_type=f32
        ).astype(bf16)
        each = STREAMS // 16
        signal_part = signal_part.reshape(group_count, 16, each, antennas)
        received = lax.all_to_all(signal_part, "row", 1, 1, tiled=True)
        signal = jnp.sum(received.astype(f32), axis=1)
        power = jnp.sum(signal * signal, axis=(1, 2))
        power = jnp.broadcast_to(power[None, None, :], (64, 1, group_count))
        power = lax.all_to_all(power, ("row", "col"), 0, 0, tiled=True)
        total_power = jnp.sum(power, axis=(0, 1)) / (STREAMS * ANTENNAS)
        transmit = signal * lax.rsqrt(total_power + epsilon)[:, None, None]
        transmit = jnp.swapaxes(transmit, 0, 1)

    with jax.named_scope("update"):
        all_ids = jnp.arange(16 * user_rows, dtype=jnp.int32)
        place_all = (slot_plane[None, :] == all_ids[:, None]).astype(bf16)
        border_all = weighted_all.reshape(16 * user_rows, TOTAL) - place_all
        half = jnp.dot(border_rows, schur_inverse, precision=highest).astype(bf16)
        change = lax.dot_general(
            half, border_all, (((1,), (1,)), ((), ())), preferred_element_type=f32
        ).astype(bf16)
        change = change.reshape(user_rows, 4, user_cols)
        stacked = []
        for d in range(4):
            block = lax.dynamic_index_in_dim(change, (col_index + d) % 4, 1, keepdims=False)
            stacked.append(block if d == 0 else along_z(block, d))
        stacked = jnp.stack(stacked, axis=0)
        col_ids = col_index * user_cols + jnp.arange(user_cols, dtype=jnp.int32)
        diagonal = row_ids[:, None] == col_ids[None, :]
        updated = []
        for g in range(group_count):
            add = lax.dynamic_index_in_dim(stacked, (col_index - g) % 4, 0, keepdims=False)
            full = jnp.any(slot_all[g][None, :] == row_ids[:, None], axis=1)
            gone = jnp.where(diagonal & full[:, None], 1.0 / loading, 0.0)
            updated.append(inverse[g] - gone + add.astype(f32))
        updated = jnp.stack(updated, axis=0)
    return (updated, transmit)


def solution(mesh):
    placed = (
        P("grp", "row", "col"),
        P("grp", "row", "col"),
        P(None, None, ("grp", "row"), "col"),
        P(),
        P(),
        P(),
        P("grp", "col", None),
    )
    return jax.shard_map(
        local,
        mesh=mesh,
        in_specs=placed,
        out_specs=(P("grp", "row", "col"), P("row", "grp", "col")),
        check_vma=False,
    )
```

```python
import jax
import jax.numpy as jnp
from jax import lax
from jax.experimental import pallas as pl
from jax.experimental.pallas import tpu as pltpu
from jax.sharding import PartitionSpec as P

ANTENNAS = 8192
ARRIVE = 128
EPOCHS = 3
STREAMS = 256
TOTAL = ARRIVE * EPOCHS
BLOCK = 128
PANEL = 8
WINDOW = 48
SHARE = TOTAL // 16
SHARE_PAD = 32

loading = 1.0
epsilon = 1e-06
highest = lax.Precision.HIGHEST
f32 = jnp.float32
bf16 = jnp.bfloat16
VMEM = pl.BlockSpec(memory_space=pltpu.VMEM)
SMEM = pl.BlockSpec(memory_space=pltpu.SMEM)
ANY = pl.BlockSpec(memory_space=pl.ANY)


def params():
    return pltpu.CompilerParams(vmem_limit_bytes=40 * 1024 * 1024)


def cost(flops, nbytes):
    return pl.CostEstimate(flops=flops, bytes_accessed=nbytes, transcendentals=0)


def dot(a, b):
    return jnp.dot(a, b, preferred_element_type=f32)


def dot_t(a, b):
    return lax.dot_general(a, b, (((1,), (1,)), ((), ())), preferred_element_type=f32)


def t_dot(a, b):
    return lax.dot_general(a, b, (((0,), (0,)), ((), ())), preferred_element_type=f32)


def halves(a):
    high = a.astype(bf16)
    return high, (a - high.astype(f32)).astype(bf16)


def split(product, a, b):
    a_high, a_low = halves(a)
    b_high, b_low = halves(b)
    return product(a_high, b_low) + product(a_low, b_high) + product(a_high, b_high)


def placing(slots_ref, first, rows):
    ids = first + lax.broadcasted_iota(jnp.int32, (rows, TOTAL), 0)
    return (ids == slots_ref[...].reshape(1, TOTAL)).astype(f32)


def choosing(place_ref, g):
    ids = lax.broadcasted_iota(jnp.int32, (16 * WINDOW, TOTAL), 0)
    return (ids == place_ref[g]).astype(f32).astype(bf16)


def start_windows(gathered_ref, window_ref, sems, groups, per_group):
    copies = []
    for g in range(groups):
        start = g * per_group // 16 * 16
        copy = pltpu.make_async_copy(
            gathered_ref.at[:, pl.ds(start, WINDOW), :], window_ref.at[g], sems.at[g]
        )
        copy.start()
        copies.append(copy)
    return copies


def columns_kernel(gathered_ref, channel_ref, place_ref, few_ref, out_ref, window_ref, sems):
    groups, user_rows, antennas = channel_ref.shape
    copies = start_windows(gathered_ref, window_ref, sems, groups, 2 * EPOCHS * 6)
    out_ref[groups] = jnp.zeros(out_ref.shape[1:], bf16)
    for g in range(groups):
        choose = choosing(place_ref, g)
        lanes = lax.broadcasted_iota(jnp.int32, (SHARE_PAD, 16 * WINDOW), 1)
        choose_few = (lanes == few_ref[g]).astype(f32).astype(bf16)
        copies[g].wait()
        window = window_ref[g].reshape(16 * WINDOW, antennas)
        few = dot(choose_few, window).astype(bf16)
        wide = dot_t(channel_ref[g], window).astype(bf16)
        wide_few = dot_t(few, window).astype(bf16)
        out_ref[g, :user_rows] = dot(wide, choose).astype(bf16)
        out_ref[g, user_rows:] = dot(wide_few, choose).astype(bf16)


def make_columns(gathered, channels, place, few):
    groups, user_rows, antennas = channels.shape
    return pl.pallas_call(
        columns_kernel,
        out_shape=jax.ShapeDtypeStruct((groups + 1, user_rows + SHARE_PAD, TOTAL), bf16),
        in_specs=[ANY, VMEM, VMEM, VMEM],
        out_specs=VMEM,
        scratch_shapes=[
            pltpu.VMEM((groups, 16, WINDOW, antennas), bf16),
            pltpu.SemaphoreType.DMA((groups,)),
        ],
        compiler_params=params(),
        cost_estimate=cost(4_000_000_000, 12_000_000),
        name="columns",
    )(gathered, channels, place, few)


def channel_kernel(first_ref, gathered_ref, channel_ref, place_ref, slots_ref, out_ref, window_ref, sems):
    groups, user_rows, antennas = channel_ref.shape
    copies = start_windows(gathered_ref, window_ref, sems, groups, 2 * EPOCHS * 6)
    for g in range(groups):
        here = placing(slots_ref.at[g], first_ref[0], user_rows).astype(bf16)
        route = dot_t(here, choosing(place_ref, g)).astype(bf16)
        copies[g].wait()
        window = window_ref[g].reshape(16 * WINDOW, antennas)
        out_ref[g] = channel_ref[g] + dot(route, window).astype(bf16)


def make_channel(first, gathered, channels, place, slots_mine):
    groups, user_rows, antennas = channels.shape
    return pl.pallas_call(
        channel_kernel,
        out_shape=jax.ShapeDtypeStruct(channels.shape, bf16),
        in_specs=[SMEM, ANY, VMEM, VMEM, VMEM],
        out_specs=VMEM,
        scratch_shapes=[
            pltpu.VMEM((groups, 16, WINDOW, antennas), bf16),
            pltpu.SemaphoreType.DMA((groups,)),
        ],
        compiler_params=params(),
        cost_estimate=cost(4_000_000_000, 14_000_000),
        name="channel",
    )(first, gathered, channels, place, slots_mine)


def middle_kernel(
    where_ref, square_ref, own_ref, row1_ref, row2_ref, row3_ref, col1_ref, col2_ref, col3_ref,
    columns_ref, precoded_ref, slots_ref, first_out, block1_out, block2_out, block3_out, packed_out,
):
    y, x, first = where_ref[0], where_ref[1], where_ref[2]
    user_rows = own_ref.shape[0]
    by_row = [own_ref, row1_ref, row2_ref, row3_ref]
    by_col = [own_ref, col1_ref, col2_ref, col3_ref]
    outs = [first_out, block1_out, block2_out, block3_out]
    schur = None
    for d in range(4):
        rows = pl.ds(pl.multiple_of((x + d) % 4 * user_rows, user_rows), user_rows)
        block = dot(square_ref[y, rows, :], own_ref[...])
        for e in range(1, 4):
            block += dot(square_ref[(y + e) % 4, rows, :], by_col[e][...])
        low = block.astype(bf16)
        outs[d][...] = block if d == 0 else low
        part = t_dot(by_row[d][...], low)
        schur = part if d == 0 else schur + part
    packed_out[:, :TOTAL] = schur.astype(bf16)
    border = columns_ref[...] - placing(slots_ref, first, user_rows)
    packed_out[:, TOTAL:] = split(t_dot, border, precoded_ref[...]).astype(bf16)


def make_middle(where, square, by_row, by_col, columns, precoded, slot_plane):
    shape = columns.shape
    return pl.pallas_call(
        middle_kernel,
        out_shape=(
            jax.ShapeDtypeStruct(shape, f32),
            jax.ShapeDtypeStruct(shape, bf16),
            jax.ShapeDtypeStruct(shape, bf16),
            jax.ShapeDtypeStruct(shape, bf16),
            jax.ShapeDtypeStruct((TOTAL, TOTAL + STREAMS), bf16),
        ),
        in_specs=[SMEM] + [VMEM] * 11,
        out_specs=(VMEM,) * 5,
        compiler_params=params(),
        cost_estimate=cost(2_000_000_000, 8_000_000),
        name="middle",
    )(where, square, *by_row, *by_col[1:], columns, precoded, slot_plane)


def invert_block(a):
    lane = lax.broadcasted_iota(jnp.int32, (1, BLOCK), 1)
    sub = lax.broadcasted_iota(jnp.int32, (PANEL, 1), 0)
    for k in range(0, BLOCK, PANEL):
        inside = (lane >= k) & (lane < k + PANEL)
        rows = a[k:k + PANEL, :]
        cols = [
            jnp.broadcast_to(rows[:, k + j:k + j + 1], (PANEL, BLOCK)) for j in range(PANEL)
        ]
        rows = jnp.where(inside, (lane - k == sub).astype(f32), rows)
        for i in range(PANEL):
            scale = 1.0 / cols[i][i:i + 1, :]
            factor = cols[i] - (sub == i).astype(f32)
            for j in range(i + 1, PANEL):
                cols[j] = cols[j] - factor * (cols[j][i:i + 1, :] * scale)
            rows = rows - factor * (rows[i:i + 1, :] * scale)
        rest = jnp.where(inside, 0.0, a)
        for i in range(PANEL):
            rest = rest - a[:, k + i:k + i + 1] * rows[i:i + 1, :]
        pieces = [rest[:k]] if k else []
        pieces.append(rows)
        if k + PANEL < BLOCK:
            pieces.append(rest[k + PANEL:])
        a = jnp.concatenate(pieces, axis=0)
    return a


def solve_kernel(first_ref, whole_ref, weighted_ref, precoded_ref, slots_ref, inv_ref, users_ref):
    inv_ref[...] = whole_ref[:, :TOTAL]

    @pl.loop(0, TOTAL // BLOCK)
    def _(b):
        start = pl.multiple_of(b * BLOCK, BLOCK)
        here = pl.ds(start, BLOCK)
        pivot_inv = invert_block(inv_ref[here, here])
        panel = inv_ref[:, here]
        row_id = lax.broadcasted_iota(jnp.int32, (TOTAL, BLOCK), 0)
        lane_id = lax.broadcasted_iota(jnp.int32, (TOTAL, BLOCK), 1)
        unit = (row_id == lane_id + start).astype(f32)
        inv_ref[:, here] = unit
        rows = inv_ref[here, :]
        scaled = split(dot, pivot_inv, rows)
        inside = (row_id >= start) & (row_id < start + BLOCK)
        rest = jnp.where(inside, 0.0, panel)
        inv_ref[here, :] = jnp.zeros((BLOCK, TOTAL), f32)
        inv_ref[...] = inv_ref[...] - split(dot, rest, scaled)
        inv_ref[here, :] = scaled

    effect = split(dot, inv_ref[...], whole_ref[:, TOTAL:])
    place = placing(slots_ref, first_ref[0], weighted_ref.shape[0])
    kept = 1.0 - jnp.sum(place, axis=1, keepdims=True)
    users = precoded_ref[...] * kept + split(dot, weighted_ref[...] - place, effect)
    for z in range(4):
        users_ref[z] = users.astype(bf16)


def make_solve(first, whole, weighted, precoded, slot_plane):
    return pl.pallas_call(
        solve_kernel,
        out_shape=(
            jax.ShapeDtypeStruct((TOTAL, TOTAL), f32),
            jax.ShapeDtypeStruct((4, weighted.shape[0], STREAMS), bf16),
        ),
        in_specs=[SMEM] + [VMEM] * 4,
        out_specs=(VMEM,) * 2,
        compiler_params=params(),
        cost_estimate=cost(10_000_000_000, 4_000_000),
        name="solve",
    )(first, whole, weighted, precoded, slot_plane)


def signal_kernel(users_ref, channel_ref, out_ref):
    part = t_dot(users_ref[0], channel_ref[0]).astype(bf16)
    out_ref[...] = part.reshape(out_ref.shape)


def make_signal(users_side, channel):
    groups, user_rows, antennas = channel.shape
    tile = 1024
    each = STREAMS // 16
    return pl.pallas_call(
        signal_kernel,
        out_shape=jax.ShapeDtypeStruct((16, groups, each, antennas), bf16),
        grid=(groups, antennas // tile),
        in_specs=[
            pl.BlockSpec((1, user_rows, STREAMS), lambda g, m: (g, 0, 0)),
            pl.BlockSpec((1, user_rows, tile), lambda g, m: (g, 0, m)),
        ],
        out_specs=pl.BlockSpec((16, 1, each, tile), lambda g, m: (0, g, 0, m)),
        compiler_params=params(),
        cost_estimate=cost(800_000_000, 7_000_000),
        name="signal",
    )(users_side, channel)


def update_kernel(first_ref, weighted_ref, inv_ref, all_ref, slots_ref, out_ref):
    user_rows = weighted_ref.shape[0]
    border = weighted_ref[...] - placing(slots_ref, first_ref[0], user_rows)
    half = split(dot, border, inv_ref[...]).astype(bf16)
    for z in range(4):
        there = all_ref[4 * z:4 * z + 4].reshape(4 * user_rows, TOTAL).astype(f32)
        there = there - placing(slots_ref, 4 * user_rows * z, 4 * user_rows)
        out_ref[z] = dot_t(half, there.astype(bf16)).astype(bf16)


def make_update(first, weighted, schur_inverse, weighted_all, slot_plane):
    user_rows = weighted.shape[0]
    return pl.pallas_call(
        update_kernel,
        out_shape=jax.ShapeDtypeStruct((4, user_rows, 4 * user_rows), bf16),
        in_specs=[SMEM] + [VMEM] * 4,
        out_specs=VMEM,
        compiler_params=params(),
        cost_estimate=cost(1_500_000_000, 8_000_000),
        name="update",
    )(first, weighted, schur_inverse, weighted_all, slot_plane)


def local(channels, inverse, arrivals, arrival_cell, cell_owner, slots, symbols):
    group_count, user_rows, antennas = channels.shape
    user_cols = inverse.shape[2]
    capacity = arrivals.shape[2]
    cell_count = cell_owner.shape[0]
    grp_index = lax.axis_index("grp")
    row_index = lax.axis_index("row")
    col_index = lax.axis_index("col")
    y_index, x_index = row_index // 4, row_index % 4
    x_groups = [[4 * y + x for x in range(4)] for y in range(4)]

    def along_x(value, step):
        pairs = [(4 * y + x, 4 * y + (x + step) % 4) for y in range(4) for x in range(4)]
        return lax.ppermute(value, "row", pairs)

    def along_y(value, step):
        pairs = [(4 * y + x, 4 * ((y + step) % 4) + x) for y in range(4) for x in range(4)]
        return lax.ppermute(value, "row", pairs)

    def to_planes(value):
        padded = jnp.concatenate([value, jnp.zeros_like(value[:1])], axis=0)
        return lax.all_to_all(padded, "col", 0, 0, tiled=True)

    first_group = grp_index * group_count
    other_first = (1 - grp_index) * group_count
    first_row = row_index * user_rows
    first_arg = first_row.reshape(1)

    with jax.named_scope("newcomers"):
        mine = lax.dynamic_slice_in_dim(arrivals, first_group, group_count, 0)
        theirs = lax.dynamic_slice_in_dim(arrivals, other_first, group_count, 0)
        swapped = lax.ppermute(theirs, "grp", [(0, 1), (1, 0)])
        from_0 = jnp.where(grp_index == 0, mine, swapped)
        from_1 = jnp.where(grp_index == 0, swapped, mine)
        chunk = jnp.stack([from_0, from_1], axis=2)
        per_group = EPOCHS * 2 * capacity
        chunk = chunk.reshape(group_count * per_group, antennas)
        chunk = jnp.pad(chunk, ((0, 112 - group_count * per_group), (0, 0)))
        gathered = lax.all_gather(chunk, "row")

    with jax.named_scope("planes"):
        low = inverse.astype(bf16).reshape(group_count, user_rows, 4, user_rows)
        by_x = low.transpose(2, 0, 1, 3)
        by_x = lax.all_to_all(by_x, "row", 0, 0, axis_index_groups=x_groups, tiled=True)
        by_group = by_x.transpose(1, 0, 2, 3).reshape(group_count, 4 * user_rows, user_rows)
        square = to_planes(by_group)
        symbol_part = jnp.einsum(
            "grc,gcs->grs", inverse, symbols.astype(f32), precision=highest
        )
        precoded = jnp.sum(to_planes(symbol_part), axis=0)

    plane_group = first_group + jnp.minimum(col_index, group_count - 1)
    slot_plane = lax.dynamic_slice_in_dim(slots, plane_group, 1, 0).reshape(1, TOTAL)
    row_ids = first_row + jnp.arange(user_rows, dtype=jnp.int32)

    cells_mine = lax.dynamic_slice_in_dim(arrival_cell, first_group, group_count, 0)[..., 0]
    slots_mine = lax.dynamic_slice_in_dim(slots, first_group, group_count, 0)
    slots_mine = slots_mine.reshape(group_count, 1, TOTAL)
    cell_table = (cells_mine[..., None] == jnp.arange(cell_count, dtype=jnp.int32)).astype(
        jnp.int32
    )
    owners = jnp.sum(cell_table * cell_owner, axis=-1)
    arrival_order = jnp.arange(ARRIVE, dtype=jnp.int32)
    earlier = (cells_mine[..., :, None] == cells_mine[..., None, :]) & (
        arrival_order[:, None] < arrival_order[None, :]
    )
    ranking = jnp.sum(earlier.astype(jnp.int32), axis=-2)
    with jax.named_scope("places"):
        offset = jnp.arange(group_count, dtype=jnp.int32) * per_group % 16
        epoch = jnp.arange(EPOCHS, dtype=jnp.int32)
        inside = offset[:, None] + epoch[None, :] * 2 * capacity
        inside = inside[:, :, None] + owners // 16 * capacity + ranking
        place = (owners % 16 * WINDOW + inside).reshape(group_count, 1, TOTAL)
        few = lax.dynamic_slice_in_dim(place, row_index * SHARE, SHARE, 2)
        few = jnp.pad(few, ((0, 0), (0, 0), (0, SHARE_PAD - SHARE)), constant_values=-1)
        few = few.reshape(group_count, SHARE_PAD, 1)

    with jax.named_scope("columns"):
        gathered, square, precoded = lax.optimization_barrier((gathered, square, precoded))
        both = make_columns(gathered, channels, place, few)
        both = lax.all_to_all(both, "col", 0, 0, tiled=True)
        summed = jnp.sum(both.astype(f32), axis=0)
        columns = summed[:user_rows]
        gram = summed[user_rows:user_rows + SHARE]
        own = columns.astype(bf16)
        by_row = [own] + [along_x(own, -d) for d in (1, 2, 3)]
        by_col = [own] + [along_y(own, -d) for d in (1, 2, 3)]

    with jax.named_scope("schur"):
        where = jnp.stack([y_index, x_index, first_row])
        block0, block1, block2, block3, packed = make_middle(
            where, square, by_row, by_col, columns, precoded, slot_plane
        )
        weighted = block0
        for d, block in ((1, block1), (2, block2), (3, block3)):
            weighted = weighted + along_x(block, d).astype(f32)
        packed = packed.reshape(16, SHARE, TOTAL + STREAMS)
        shared = lax.all_to_all(packed, "row", 0, 0, tiled=True).astype(f32)
        shared = jnp.sum(shared, axis=0)
        share_ids = row_index * SHARE + jnp.arange(SHARE, dtype=jnp.int32)
        identity = loading * (
            share_ids[:, None] == jnp.arange(TOTAL, dtype=jnp.int32)[None, :]
        ).astype(f32)
        schur_rows = gram + identity - shared[:, :TOTAL]
        ready = jnp.concatenate([schur_rows, shared[:, TOTAL:]], axis=1)
        ready = jnp.broadcast_to(ready[None], (16, SHARE, TOTAL + STREAMS))
        whole = lax.all_to_all(ready, "row", 0, 0, tiled=True).reshape(TOTAL, TOTAL + STREAMS)

    with jax.named_scope("users"):
        weighted_all = lax.all_gather(weighted.astype(bf16), "row")
        channel = make_channel(first_arg, gathered, channels, place, slots_mine)
        schur_inverse, users = make_solve(first_arg, whole, weighted, precoded, slot_plane)
        users_side = lax.all_to_all(users, "col", 0, 0, tiled=True)

    with jax.named_scope("update"):
        change = make_update(first_arg, weighted, schur_inverse, weighted_all, slot_plane)
        change = lax.all_to_all(change, "col", 0, 0, tiled=True)

    with jax.named_scope("signal"):
        signal_part = make_signal(users_side, channel)
        received = lax.all_to_all(signal_part, "row", 0, 0, tiled=True)
        received, change = lax.optimization_barrier((received, change))
        signal = jnp.sum(received.astype(f32), axis=0)
        power = jnp.sum(signal * signal, axis=(1, 2))
        power = jnp.broadcast_to(power[None, None, :], (64, 1, group_count))
        power = lax.all_to_all(power, ("row", "col"), 0, 0, tiled=True)
        total_power = jnp.sum(power, axis=(0, 1)) / (STREAMS * ANTENNAS)
        transmit = signal * lax.rsqrt(total_power + epsilon)[:, None, None]
        transmit = jnp.swapaxes(transmit, 0, 1)

    with jax.named_scope("final"):
        col_ids = col_index * user_cols + jnp.arange(user_cols, dtype=jnp.int32)
        diagonal = row_ids[:, None] == col_ids[None, :]
        full = jnp.any(slots_mine == row_ids[None, :, None], axis=2)
        gone = jnp.where(diagonal[None] & full[:, :, None], 1.0 / loading, 0.0)
        updated = inverse - gone + change[:group_count].astype(f32)
    return (updated, transmit)


def solution(mesh):
    placed = (
        P("grp", "row", "col"),
        P("grp", "row", "col"),
        P(None, None, ("grp", "row"), "col"),
        P(),
        P(),
        P(),
        P("grp", "col", None),
    )
    return jax.shard_map(
        local,
        mesh=mesh,
        in_specs=placed,
        out_specs=(P("grp", "row", "col"), P("row", "grp", "col")),
        check_vma=False,
    )
```

```python
import jax
import jax.numpy as jnp
from jax import lax
from jax.experimental import pallas as pl
from jax.experimental.pallas import tpu as pltpu
from jax.sharding import PartitionSpec as P

ANTENNAS = 8192
ARRIVE = 128
EPOCHS = 3
STREAMS = 256
TOTAL = ARRIVE * EPOCHS
BLOCK = 128
PANEL = 8
WINDOW = 48
SHARE = TOTAL // 16

loading = 1.0
epsilon = 1e-06
highest = lax.Precision.HIGHEST
f32 = jnp.float32
bf16 = jnp.bfloat16
VMEM = pl.BlockSpec(memory_space=pltpu.VMEM)
SMEM = pl.BlockSpec(memory_space=pltpu.SMEM)
HBM = pl.BlockSpec(memory_space=pltpu.HBM)


def params():
    return pltpu.CompilerParams(vmem_limit_bytes=40 * 1024 * 1024)


def cost(flops, nbytes):
    return pl.CostEstimate(flops=flops, bytes_accessed=nbytes, transcendentals=0)


def dot(a, b):
    return jnp.dot(a, b, preferred_element_type=f32)


def dot_t(a, b):
    return lax.dot_general(a, b, (((1,), (1,)), ((), ())), preferred_element_type=f32)


def t_dot(a, b):
    return lax.dot_general(a, b, (((0,), (0,)), ((), ())), preferred_element_type=f32)


def halves(a):
    high = a.astype(bf16)
    return high, (a - high.astype(f32)).astype(bf16)


def split(product, a, b):
    a_high, a_low = halves(a)
    b_high, b_low = halves(b)
    return product(a_high, b_low) + product(a_low, b_high) + product(a_high, b_high)


def placing(slots_ref, first, rows):
    ids = first + lax.broadcasted_iota(jnp.int32, (rows, TOTAL), 0)
    return (ids == slots_ref[...].reshape(1, TOTAL)).astype(f32)


def choosing(place_ref, g):
    ids = lax.broadcasted_iota(jnp.int32, (16 * WINDOW, TOTAL), 0)
    return (ids == place_ref[g]).astype(f32).astype(bf16)


def start_inputs(gathered_ref, channel_ref, window_ref, held_ref, sems, groups, per_group):
    copies = []
    for g in range(groups):
        start = g * per_group // 16 * 16
        window = pltpu.make_async_copy(
            gathered_ref.at[:, pl.ds(start, WINDOW), :], window_ref.at[g], sems.at[0, g]
        )
        channel = pltpu.make_async_copy(channel_ref.at[g], held_ref.at[g], sems.at[1, g])
        window.start()
        channel.start()
        copies.append((window, channel))
    return copies


def input_scratch(groups, user_rows, antennas):
    return [
        pltpu.VMEM((groups, 16, WINDOW, antennas), bf16),
        pltpu.VMEM((groups, user_rows, antennas), bf16),
        pltpu.SemaphoreType.DMA((2, groups)),
    ]


def columns_kernel(
    row_ref, gathered_ref, channel_ref, place_ref, out_ref, window_ref, held_ref, sems
):
    groups, user_rows, antennas = held_ref.shape
    copies = start_inputs(
        gathered_ref, channel_ref, window_ref, held_ref, sems, groups, 2 * EPOCHS * 6
    )
    out_ref[groups] = jnp.zeros(out_ref.shape[1:], bf16)
    for g in range(groups):
        choose = choosing(place_ref, g)
        for copy in copies[g]:
            copy.wait()
        window = window_ref[g].reshape(16 * WINDOW, antennas)
        wide = dot_t(held_ref[g], window).astype(bf16)
        out_ref[g, :user_rows] = dot(wide, choose).astype(bf16)
        wide = dot_t(window_ref[g, row_ref[0]], window).astype(bf16)
        out_ref[g, user_rows:] = dot(wide, choose).astype(bf16)


def make_columns(row, gathered, channels, place):
    groups, user_rows, antennas = channels.shape
    return pl.pallas_call(
        columns_kernel,
        out_shape=jax.ShapeDtypeStruct((groups + 1, user_rows + WINDOW, TOTAL), bf16),
        in_specs=[SMEM, HBM, HBM, VMEM],
        out_specs=VMEM,
        scratch_shapes=input_scratch(groups, user_rows, antennas),
        compiler_params=params(),
        cost_estimate=cost(4_000_000_000, 12_000_000),
        name="columns",
    )(row, gathered, channels, place)


def channel_kernel(
    first_ref, gathered_ref, channel_ref, place_ref, slots_ref, out_ref, window_ref, held_ref, sems
):
    groups, user_rows, antennas = held_ref.shape
    copies = start_inputs(
        gathered_ref, channel_ref, window_ref, held_ref, sems, groups, 2 * EPOCHS * 6
    )
    for g in range(groups):
        here = placing(slots_ref.at[g], first_ref[0], user_rows).astype(bf16)
        route = dot_t(here, choosing(place_ref, g)).astype(bf16)
        for copy in copies[g]:
            copy.wait()
        window = window_ref[g].reshape(16 * WINDOW, antennas)
        out_ref[g] = held_ref[g] + dot(route, window).astype(bf16)


def make_channel(first, gathered, channels, place, slots_mine):
    groups, user_rows, antennas = channels.shape
    return pl.pallas_call(
        channel_kernel,
        out_shape=jax.ShapeDtypeStruct(channels.shape, bf16),
        in_specs=[SMEM, HBM, HBM, VMEM, VMEM],
        out_specs=VMEM,
        scratch_shapes=input_scratch(groups, user_rows, antennas),
        compiler_params=params(),
        cost_estimate=cost(4_000_000_000, 14_000_000),
        name="channel",
    )(first, gathered, channels, place, slots_mine)


def middle_kernel(
    where_ref, square0_ref, square1_ref, square2_ref, square3_ref, own_ref, row1_ref, row2_ref,
    row3_ref, col1_ref, col2_ref, col3_ref, columns_ref, precoded_ref, slots_ref, gram_ref,
    place_ref, first_out, block1_out, block2_out, block3_out, packed_out,
):
    y, row, first = where_ref[0], where_ref[1], where_ref[2]
    user_rows = own_ref.shape[0]
    squares = [square0_ref, square1_ref, square2_ref, square3_ref]
    by_row = [own_ref, row1_ref, row2_ref, row3_ref]
    by_col = [own_ref, col1_ref, col2_ref, col3_ref]
    outs = [first_out, block1_out, block2_out, block3_out]
    ids = row * WINDOW + lax.broadcasted_iota(jnp.int32, (WINDOW, TOTAL), 0)
    choose = (ids == place_ref[...]).astype(f32).astype(bf16)
    schur = -t_dot(choose, gram_ref[...].astype(bf16))
    for d in range(4):
        block = dot(squares[d][y], own_ref[...])
        for e in range(1, 4):
            block += dot(squares[d][(y + e) % 4], by_col[e][...])
        low = block.astype(bf16)
        outs[d][...] = block if d == 0 else low
        schur += t_dot(by_row[d][...], low)
    packed_out[:, :TOTAL] = schur.astype(bf16)
    border = columns_ref[...] - placing(slots_ref, first, user_rows)
    packed_out[:, TOTAL:] = split(t_dot, border, precoded_ref[...]).astype(bf16)


def make_middle(where, squares, by_row, by_col, columns, precoded, slot_plane, gram, place_plane):
    shape = columns.shape
    return pl.pallas_call(
        middle_kernel,
        out_shape=(
            jax.ShapeDtypeStruct(shape, f32),
            jax.ShapeDtypeStruct(shape, bf16),
            jax.ShapeDtypeStruct(shape, bf16),
            jax.ShapeDtypeStruct(shape, bf16),
            jax.ShapeDtypeStruct((TOTAL, TOTAL + STREAMS), bf16),
        ),
        in_specs=[SMEM] + [VMEM] * 16,
        out_specs=(VMEM,) * 5,
        compiler_params=params(),
        cost_estimate=cost(2_000_000_000, 8_000_000),
        name="middle",
    )(where, *squares, *by_row, *by_col[1:], columns, precoded, slot_plane, gram, place_plane)


def invert_block(a):
    lane = lax.broadcasted_iota(jnp.int32, (1, BLOCK), 1)
    sub = lax.broadcasted_iota(jnp.int32, (PANEL, 1), 0)
    for k in range(0, BLOCK, PANEL):
        inside = (lane >= k) & (lane < k + PANEL)
        rows = a[k:k + PANEL, :]
        cols = [
            jnp.broadcast_to(rows[:, k + j:k + j + 1], (PANEL, BLOCK)) for j in range(PANEL)
        ]
        rows = jnp.where(inside, (lane - k == sub).astype(f32), rows)
        for i in range(PANEL):
            scale = 1.0 / cols[i][i:i + 1, :]
            factor = cols[i] - (sub == i).astype(f32)
            for j in range(i + 1, PANEL):
                cols[j] = cols[j] - factor * (cols[j][i:i + 1, :] * scale)
            rows = rows - factor * (rows[i:i + 1, :] * scale)
        rest = jnp.where(inside, 0.0, a)
        for i in range(PANEL):
            rest = rest - a[:, k + i:k + i + 1] * rows[i:i + 1, :]
        pieces = [rest[:k]] if k else []
        pieces.append(rows)
        if k + PANEL < BLOCK:
            pieces.append(rest[k + PANEL:])
        a = jnp.concatenate(pieces, axis=0)
    return a


def solve_kernel(first_ref, whole_ref, weighted_ref, precoded_ref, slots_ref, inv_ref, users_ref):
    inv_ref[...] = whole_ref[:, :TOTAL]

    @pl.loop(0, TOTAL // BLOCK)
    def _(b):
        start = pl.multiple_of(b * BLOCK, BLOCK)
        here = pl.ds(start, BLOCK)
        pivot_inv = invert_block(inv_ref[here, here])
        panel = inv_ref[:, here]
        row_id = lax.broadcasted_iota(jnp.int32, (TOTAL, BLOCK), 0)
        lane_id = lax.broadcasted_iota(jnp.int32, (TOTAL, BLOCK), 1)
        unit = (row_id == lane_id + start).astype(f32)
        inv_ref[:, here] = unit
        rows = inv_ref[here, :]
        scaled = split(dot, pivot_inv, rows)
        inside = (row_id >= start) & (row_id < start + BLOCK)
        rest = jnp.where(inside, 0.0, panel)
        inv_ref[here, :] = jnp.zeros((BLOCK, TOTAL), f32)
        inv_ref[...] = inv_ref[...] - split(dot, rest, scaled)
        inv_ref[here, :] = scaled

    effect = split(dot, inv_ref[...], whole_ref[:, TOTAL:])
    place = placing(slots_ref, first_ref[0], weighted_ref.shape[0])
    kept = 1.0 - jnp.sum(place, axis=1, keepdims=True)
    users = precoded_ref[...] * kept + split(dot, weighted_ref[...] - place, effect)
    for z in range(4):
        users_ref[z] = users.astype(bf16)


def make_solve(first, whole, weighted, precoded, slot_plane):
    return pl.pallas_call(
        solve_kernel,
        out_shape=(
            jax.ShapeDtypeStruct((TOTAL, TOTAL), f32),
            jax.ShapeDtypeStruct((4, weighted.shape[0], STREAMS), bf16),
        ),
        in_specs=[SMEM] + [VMEM] * 4,
        out_specs=(VMEM,) * 2,
        compiler_params=params(),
        cost_estimate=cost(10_000_000_000, 4_000_000),
        name="solve",
    )(first, whole, weighted, precoded, slot_plane)


def signal_kernel(users_ref, channel_ref, out_ref, held_ref, sems):
    groups, _, antennas = channel_ref.shape
    tile = antennas // 2
    copies = []
    for g in range(groups):
        for m in range(0, antennas, tile):
            part = t_dot(users_ref[g], channel_ref[g, :, m:m + tile]).astype(bf16)
            held_ref[g, :, :, m:m + tile] = part.reshape(16, STREAMS // 16, tile)
        copy = pltpu.make_async_copy(held_ref.at[g], out_ref.at[:, g], sems.at[g])
        copy.start()
        copies.append(copy)
    for copy in copies:
        copy.wait()


def make_signal(users_side, channel):
    groups, _, antennas = channel.shape
    each = STREAMS // 16
    return pl.pallas_call(
        signal_kernel,
        out_shape=jax.ShapeDtypeStruct((16, groups, each, antennas), bf16),
        in_specs=[VMEM, VMEM],
        out_specs=HBM,
        scratch_shapes=[
            pltpu.VMEM((groups, 16, each, antennas), bf16),
            pltpu.SemaphoreType.DMA((groups,)),
        ],
        compiler_params=params(),
        cost_estimate=cost(800_000_000, 7_000_000),
        name="signal",
    )(users_side, channel)


def update_kernel(
    where_ref, weighted_ref, inv_ref, all_ref, slots_ref, out0, out1, out2, out3, held_ref, sems
):
    first, plane = where_ref[0], where_ref[1]
    user_rows = weighted_ref.shape[0]
    border = weighted_ref[...] - placing(slots_ref, first, user_rows)
    half = split(dot, border, inv_ref[...]).astype(bf16)
    copies = []
    for d, out in enumerate([out0, out1, out2, out3]):
        z = (plane + d) % 4
        there = all_ref[pl.ds(4 * z, 4)].reshape(4 * user_rows, TOTAL).astype(f32)
        there = there - placing(slots_ref, 4 * user_rows * z, 4 * user_rows)
        held_ref[d] = dot_t(half, there.astype(bf16)).astype(bf16)
        copy = pltpu.make_async_copy(held_ref.at[d], out, sems.at[d])
        copy.start()
        copies.append(copy)
    for copy in copies:
        copy.wait()


def make_update(where, weighted, schur_inverse, weighted_all, slot_plane):
    user_rows = weighted.shape[0]
    return pl.pallas_call(
        update_kernel,
        out_shape=(jax.ShapeDtypeStruct((user_rows, 4 * user_rows), bf16),) * 4,
        in_specs=[SMEM] + [VMEM] * 4,
        out_specs=(HBM,) * 4,
        scratch_shapes=[
            pltpu.VMEM((4, user_rows, 4 * user_rows), bf16),
            pltpu.SemaphoreType.DMA((4,)),
        ],
        compiler_params=params(),
        cost_estimate=cost(1_500_000_000, 8_000_000),
        name="update",
    )(where, weighted, schur_inverse, weighted_all, slot_plane)


def local(channels, inverse, arrivals, arrival_cell, cell_owner, slots, symbols):
    group_count, user_rows, antennas = channels.shape
    user_cols = inverse.shape[2]
    capacity = arrivals.shape[2]
    cell_count = cell_owner.shape[0]
    grp_index = lax.axis_index("grp")
    row_index = lax.axis_index("row")
    col_index = lax.axis_index("col")
    y_index, x_index = row_index // 4, row_index % 4

    def along_x(value, step):
        pairs = [(4 * y + x, 4 * y + (x + step) % 4) for y in range(4) for x in range(4)]
        return lax.ppermute(value, "row", pairs)

    def along_y(value, step):
        pairs = [(4 * y + x, 4 * ((y + step) % 4) + x) for y in range(4) for x in range(4)]
        return lax.ppermute(value, "row", pairs)

    def along_z(value, step):
        return lax.ppermute(value, "col", [(z, (z + step) % 4) for z in range(4)])

    def to_planes(value):
        padded = jnp.concatenate([value, jnp.zeros_like(value[:1])], axis=0)
        return lax.all_to_all(padded, "col", 0, 0, tiled=True)

    first_group = grp_index * group_count
    other_first = (1 - grp_index) * group_count
    first_row = row_index * user_rows
    first_arg = first_row.reshape(1)

    with jax.named_scope("newcomers"):
        mine = lax.dynamic_slice_in_dim(arrivals, first_group, group_count, 0)
        theirs = lax.dynamic_slice_in_dim(arrivals, other_first, group_count, 0)
        swapped = lax.ppermute(theirs, "grp", [(0, 1), (1, 0)])
        from_0 = jnp.where(grp_index == 0, mine, swapped)
        from_1 = jnp.where(grp_index == 0, swapped, mine)
        chunk = jnp.stack([from_0, from_1], axis=2)
        per_group = EPOCHS * 2 * capacity
        chunk = chunk.reshape(group_count * per_group, antennas)
        chunk = jnp.pad(chunk, ((0, 112 - group_count * per_group), (0, 0)))
        gathered = lax.all_gather(chunk, "row")

    with jax.named_scope("planes"):
        low = inverse.astype(bf16).reshape(group_count, user_rows, 4, user_rows)
        full_rows = to_planes(low.transpose(0, 2, 1, 3))
        symbol_part = jnp.einsum(
            "grc,gcs->grs", inverse, symbols.astype(f32), precision=highest
        )
        precoded = jnp.sum(to_planes(symbol_part), axis=0)

    plane_group = first_group + jnp.minimum(col_index, group_count - 1)
    slot_plane = lax.dynamic_slice_in_dim(slots, plane_group, 1, 0).reshape(1, TOTAL)
    row_ids = first_row + jnp.arange(user_rows, dtype=jnp.int32)

    cells_mine = lax.dynamic_slice_in_dim(arrival_cell, first_group, group_count, 0)[..., 0]
    slots_mine = lax.dynamic_slice_in_dim(slots, first_group, group_count, 0)
    slots_mine = slots_mine.reshape(group_count, 1, TOTAL)
    cell_table = (cells_mine[..., None] == jnp.arange(cell_count, dtype=jnp.int32)).astype(
        jnp.int32
    )
    owners = jnp.sum(cell_table * cell_owner, axis=-1)
    arrival_order = jnp.arange(ARRIVE, dtype=jnp.int32)
    earlier = (cells_mine[..., :, None] == cells_mine[..., None, :]) & (
        arrival_order[:, None] < arrival_order[None, :]
    )
    ranking = jnp.sum(earlier.astype(jnp.int32), axis=-2)
    with jax.named_scope("places"):
        offset = jnp.arange(group_count, dtype=jnp.int32) * per_group % 16
        epoch = jnp.arange(EPOCHS, dtype=jnp.int32)
        inside = offset[:, None] + epoch[None, :] * 2 * capacity
        inside = inside[:, :, None] + owners // 16 * capacity + ranking
        place = (owners % 16 * WINDOW + inside).reshape(group_count, 1, TOTAL)
        plane_place = lax.dynamic_slice_in_dim(
            place, jnp.minimum(col_index, group_count - 1), 1, 0
        ).reshape(1, TOTAL)

    with jax.named_scope("columns"):
        gathered, full_rows, precoded = lax.optimization_barrier(
            (gathered, full_rows, precoded)
        )
        squares = []
        for d in range(4):
            piece = lax.dynamic_index_in_dim(full_rows, (x_index + d) % 4, 1, keepdims=False)
            squares.append(along_x(piece, d) if d else piece)
        both = make_columns(row_index.reshape(1), gathered, channels, place)
        both = lax.all_to_all(both, "col", 0, 0, tiled=True)
        summed = jnp.sum(both.astype(f32), axis=0)
        columns = summed[:user_rows]
        gram = summed[user_rows:]
        own = columns.astype(bf16)
        by_row = [own] + [along_x(own, d) for d in (1, 2, 3)]
        by_col = [own] + [along_y(own, -d) for d in (1, 2, 3)]

    with jax.named_scope("schur"):
        where = jnp.stack([y_index, row_index, first_row])
        block0, block1, block2, block3, packed = make_middle(
            where, squares, by_row, by_col, columns, precoded, slot_plane, gram, plane_place
        )
        packed = packed.reshape(16, SHARE, TOTAL + STREAMS)
        shared = lax.all_to_all(packed, "row", 0, 0, tiled=True)
        shared, block1, block2, block3 = lax.optimization_barrier(
            (shared, block1, block2, block3)
        )
        weighted = block0
        for d, block in ((1, block1), (2, block2), (3, block3)):
            weighted = weighted + along_x(block, -d).astype(f32)
        shared = jnp.sum(shared.astype(f32), axis=0)
        share_ids = row_index * SHARE + jnp.arange(SHARE, dtype=jnp.int32)
        identity = loading * (
            share_ids[:, None] == jnp.arange(TOTAL, dtype=jnp.int32)[None, :]
        ).astype(f32)
        schur_rows = identity - shared[:, :TOTAL]
        ready = jnp.concatenate([schur_rows, shared[:, TOTAL:]], axis=1)
        ready = jnp.broadcast_to(ready[None], (16, SHARE, TOTAL + STREAMS))
        whole = lax.all_to_all(ready, "row", 0, 0, tiled=True).reshape(TOTAL, TOTAL + STREAMS)

    with jax.named_scope("users"):
        weighted_all = lax.all_gather(weighted.astype(bf16), "row")
        channel = make_channel(first_arg, gathered, channels, place, slots_mine)
        whole, channel = lax.optimization_barrier((whole, channel))
        schur_inverse, users = make_solve(first_arg, whole, weighted, precoded, slot_plane)
        users_side = lax.all_to_all(users, "col", 0, 0, tiled=True)

    with jax.named_scope("update"):
        changes = make_update(
            jnp.stack([first_row, col_index]), weighted, schur_inverse, weighted_all, slot_plane
        )
        changes = [changes[0]] + [along_z(changes[d], d) for d in (1, 2, 3)]

    with jax.named_scope("signal"):
        signal_part = make_signal(users_side, channel)
        received = lax.all_to_all(signal_part, "row", 0, 0, tiled=True)
        received, changes = lax.optimization_barrier((received, changes))
        signal = jnp.sum(received.astype(f32), axis=0)
        power = jnp.sum(signal * signal, axis=(1, 2))
        power = jnp.broadcast_to(power[None, None, :], (64, 1, group_count))
        power = lax.all_to_all(power, ("row", "col"), 0, 0, tiled=True)
        total_power = jnp.sum(power, axis=(0, 1)) / (STREAMS * ANTENNAS)
        transmit = signal * lax.rsqrt(total_power + epsilon)[:, None, None]
        transmit = jnp.swapaxes(transmit, 0, 1)

    with jax.named_scope("final"):
        col_ids = col_index * user_cols + jnp.arange(user_cols, dtype=jnp.int32)
        diagonal = row_ids[:, None] == col_ids[None, :]
        full = jnp.any(slots_mine == row_ids[None, :, None], axis=2)
        gone = jnp.where(diagonal[None] & full[:, :, None], 1.0 / loading, 0.0)
        updated = []
        for g in range(group_count):
            step = (col_index - g) % 4
            add = changes[0]
            for d in (1, 2, 3):
                add = jnp.where(step == d, changes[d], add)
            updated.append(inverse[g] - gone[g] + add.astype(f32))
        updated = jnp.stack(updated, axis=0)
    return (updated, transmit)


def solution(mesh):
    placed = (
        P("grp", "row", "col"),
        P("grp", "row", "col"),
        P(None, None, ("grp", "row"), "col"),
        P(),
        P(),
        P(),
        P("grp", "col", None),
    )
    return jax.shard_map(
        local,
        mesh=mesh,
        in_specs=placed,
        out_specs=(P("grp", "row", "col"), P("row", "grp", "col")),
        check_vma=False,
    )
```

```python
import jax
import jax.numpy as jnp
from jax import lax
from jax.experimental import pallas as pl
from jax.experimental.pallas import tpu as pltpu
from jax.sharding import PartitionSpec as P

ANTENNAS = 8192
ARRIVE = 128
EPOCHS = 3
STREAMS = 256
TOTAL = ARRIVE * EPOCHS
BLOCK = 128
PANEL = 8
WINDOW = 48
SHARE = TOTAL // 16

loading = 1.0
epsilon = 1e-06
highest = lax.Precision.HIGHEST
f32 = jnp.float32
bf16 = jnp.bfloat16
VMEM = pl.BlockSpec(memory_space=pltpu.VMEM)
SMEM = pl.BlockSpec(memory_space=pltpu.SMEM)
HBM = pl.BlockSpec(memory_space=pltpu.HBM)


def params(mib=40):
    return pltpu.CompilerParams(vmem_limit_bytes=mib * 1024 * 1024)


def cost(flops, nbytes):
    return pl.CostEstimate(flops=flops, bytes_accessed=nbytes, transcendentals=0)


def dot(a, b):
    return jnp.dot(a, b, preferred_element_type=f32)


def dot_t(a, b):
    return lax.dot_general(a, b, (((1,), (1,)), ((), ())), preferred_element_type=f32)


def t_dot(a, b):
    return lax.dot_general(a, b, (((0,), (0,)), ((), ())), preferred_element_type=f32)


def halves(a):
    high = a.astype(bf16)
    return high, (a - high.astype(f32)).astype(bf16)


def split(product, a, b):
    a_high, a_low = halves(a)
    b_high, b_low = halves(b)
    return product(a_high, b_low) + product(a_low, b_high) + product(a_high, b_high)


def placing(slots_ref, first, rows):
    ids = first + lax.broadcasted_iota(jnp.int32, (rows, TOTAL), 0)
    return (ids == slots_ref[...].reshape(1, TOTAL)).astype(f32)


def choosing(place_ref, g):
    ids = lax.broadcasted_iota(jnp.int32, (16 * WINDOW, TOTAL), 0)
    return (ids == place_ref[g]).astype(f32).astype(bf16)


def start_inputs(gathered_ref, channel_ref, window_ref, held_ref, sems, row=None):
    groups, user_rows = channel_ref.shape[:2]
    copies = []
    for g in range(groups):
        start = g * 2 * EPOCHS * 6 // 16 * 16
        source = gathered_ref.at[:, pl.ds(start, WINDOW), :]
        parts = [
            pltpu.make_async_copy(channel_ref.at[g], held_ref.at[g, :user_rows], sems.at[0, g]),
            pltpu.make_async_copy(source, window_ref.at[g], sems.at[1, g]),
        ]
        if row is not None:
            source = gathered_ref.at[row, pl.ds(start, WINDOW), :]
            parts.append(
                pltpu.make_async_copy(source, held_ref.at[g, user_rows:], sems.at[2, g])
            )
        for part in parts:
            part.start()
        copies.append(parts)
    return copies


def input_scratch(groups, rows, antennas):
    return [
        pltpu.VMEM((groups, 16, WINDOW, antennas), bf16),
        pltpu.VMEM((groups, rows, antennas), bf16),
        pltpu.SemaphoreType.DMA((3, groups)),
    ]


def columns_kernel(
    row_ref, gathered_ref, channel_ref, place_ref, out_ref, window_ref, held_ref, sems
):
    groups, _, antennas = channel_ref.shape
    copies = start_inputs(gathered_ref, channel_ref, window_ref, held_ref, sems, row_ref[0])
    out_ref[groups] = jnp.zeros(out_ref.shape[1:], bf16)
    for g in range(groups):
        choose = choosing(place_ref, g)
        for copy in copies[g]:
            copy.wait()
        window = window_ref[g].reshape(16 * WINDOW, antennas)
        wide = dot_t(held_ref[g], window).astype(bf16)
        out_ref[g] = dot(wide, choose).astype(bf16)


def make_columns(row, gathered, channels, place):
    groups, user_rows, antennas = channels.shape
    return pl.pallas_call(
        columns_kernel,
        out_shape=jax.ShapeDtypeStruct((groups + 1, user_rows + WINDOW, TOTAL), bf16),
        in_specs=[SMEM, HBM, HBM, VMEM],
        out_specs=VMEM,
        scratch_shapes=input_scratch(groups, user_rows + WINDOW, antennas),
        compiler_params=params(60),
        cost_estimate=cost(4_000_000_000, 12_000_000),
        name="columns",
    )(row, gathered, channels, place)


def channel_kernel(
    first_ref, gathered_ref, channel_ref, place_ref, slots_ref, out_ref, window_ref, held_ref, sems
):
    groups, user_rows, antennas = channel_ref.shape
    copies = start_inputs(gathered_ref, channel_ref, window_ref, held_ref, sems)
    for g in range(groups):
        here = placing(slots_ref.at[g], first_ref[0], user_rows).astype(bf16)
        route = dot_t(here, choosing(place_ref, g)).astype(bf16)
        for copy in copies[g]:
            copy.wait()
        window = window_ref[g].reshape(16 * WINDOW, antennas)
        out_ref[g] = held_ref[g] + dot(route, window).astype(bf16)


def make_channel(first, gathered, channels, place, slots_mine):
    groups, user_rows, antennas = channels.shape
    return pl.pallas_call(
        channel_kernel,
        out_shape=jax.ShapeDtypeStruct(channels.shape, bf16),
        in_specs=[SMEM, HBM, HBM, VMEM, VMEM],
        out_specs=VMEM,
        scratch_shapes=input_scratch(groups, user_rows, antennas),
        compiler_params=params(60),
        cost_estimate=cost(4_000_000_000, 14_000_000),
        name="channel",
    )(first, gathered, channels, place, slots_mine)


def middle_kernel(
    where_ref, square0_ref, square1_ref, square2_ref, square3_ref, own_ref, row1_ref, row2_ref,
    row3_ref, col1_ref, col2_ref, col3_ref, columns_ref, precoded_ref, slots_ref, gram_ref,
    place_ref, first_out, block1_out, block2_out, block3_out, packed_out,
):
    y, row, first = where_ref[0], where_ref[1], where_ref[2]
    user_rows = own_ref.shape[0]
    squares = [square0_ref, square1_ref, square2_ref, square3_ref]
    by_row = [own_ref, row1_ref, row2_ref, row3_ref]
    by_col = [own_ref, col1_ref, col2_ref, col3_ref]
    outs = [first_out, block1_out, block2_out, block3_out]
    ids = row * WINDOW + lax.broadcasted_iota(jnp.int32, (WINDOW, TOTAL), 0)
    choose = (ids == place_ref[...]).astype(f32).astype(bf16)
    schur = -t_dot(choose, gram_ref[...].astype(bf16))
    for d in range(4):
        block = dot(squares[d][y], own_ref[...])
        for e in range(1, 4):
            block += dot(squares[d][(y + e) % 4], by_col[e][...])
        low = block.astype(bf16)
        outs[d][...] = block if d == 0 else low
        schur += t_dot(by_row[d][...], low)
    packed_out[:, :TOTAL] = schur.astype(bf16)
    border = columns_ref[...] - placing(slots_ref, first, user_rows)
    packed_out[:, TOTAL:] = split(t_dot, border, precoded_ref[...]).astype(bf16)


def make_middle(where, squares, by_row, by_col, columns, precoded, slot_plane, gram, place_plane):
    shape = columns.shape
    return pl.pallas_call(
        middle_kernel,
        out_shape=(
            jax.ShapeDtypeStruct(shape, f32),
            jax.ShapeDtypeStruct(shape, bf16),
            jax.ShapeDtypeStruct(shape, bf16),
            jax.ShapeDtypeStruct(shape, bf16),
            jax.ShapeDtypeStruct((TOTAL, TOTAL + STREAMS), bf16),
        ),
        in_specs=[SMEM] + [VMEM] * 16,
        out_specs=(VMEM,) * 5,
        compiler_params=params(),
        cost_estimate=cost(2_000_000_000, 8_000_000),
        name="middle",
    )(where, *squares, *by_row, *by_col[1:], columns, precoded, slot_plane, gram, place_plane)


def invert_block(a):
    lane = lax.broadcasted_iota(jnp.int32, (1, BLOCK), 1)
    sub = lax.broadcasted_iota(jnp.int32, (PANEL, 1), 0)
    for k in range(0, BLOCK, PANEL):
        inside = (lane >= k) & (lane < k + PANEL)
        rows = a[k:k + PANEL, :]
        cols = [
            jnp.broadcast_to(rows[:, k + j:k + j + 1], (PANEL, BLOCK)) for j in range(PANEL)
        ]
        rows = jnp.where(inside, (lane - k == sub).astype(f32), rows)
        for i in range(PANEL):
            scale = 1.0 / cols[i][i:i + 1, :]
            factor = cols[i] - (sub == i).astype(f32)
            for j in range(i + 1, PANEL):
                cols[j] = cols[j] - factor * (cols[j][i:i + 1, :] * scale)
            rows = rows - factor * (rows[i:i + 1, :] * scale)
        rest = jnp.where(inside, 0.0, a)
        for i in range(PANEL):
            rest = rest - a[:, k + i:k + i + 1] * rows[i:i + 1, :]
        pieces = [rest[:k]] if k else []
        pieces.append(rows)
        if k + PANEL < BLOCK:
            pieces.append(rest[k + PANEL:])
        a = jnp.concatenate(pieces, axis=0)
    return a


def solve_kernel(first_ref, whole_ref, weighted_ref, precoded_ref, slots_ref, inv_ref, users_ref):
    inv_ref[...] = whole_ref[:, :TOTAL]

    @pl.loop(0, TOTAL // BLOCK)
    def _(b):
        start = pl.multiple_of(b * BLOCK, BLOCK)
        here = pl.ds(start, BLOCK)
        pivot_inv = invert_block(inv_ref[here, here])
        panel = inv_ref[:, here]
        row_id = lax.broadcasted_iota(jnp.int32, (TOTAL, BLOCK), 0)
        lane_id = lax.broadcasted_iota(jnp.int32, (TOTAL, BLOCK), 1)
        unit = (row_id == lane_id + start).astype(f32)
        inv_ref[:, here] = unit
        rows = inv_ref[here, :]
        scaled = split(dot, pivot_inv, rows)
        inside = (row_id >= start) & (row_id < start + BLOCK)
        rest = jnp.where(inside, 0.0, panel)
        inv_ref[here, :] = jnp.zeros((BLOCK, TOTAL), f32)
        inv_ref[...] = inv_ref[...] - split(dot, rest, scaled)
        inv_ref[here, :] = scaled

    effect = split(dot, inv_ref[...], whole_ref[:, TOTAL:])
    place = placing(slots_ref, first_ref[0], weighted_ref.shape[0])
    kept = 1.0 - jnp.sum(place, axis=1, keepdims=True)
    users = precoded_ref[...] * kept + split(dot, weighted_ref[...] - place, effect)
    for z in range(4):
        users_ref[z] = users.astype(bf16)


def make_solve(first, whole, weighted, precoded, slot_plane):
    return pl.pallas_call(
        solve_kernel,
        out_shape=(
            jax.ShapeDtypeStruct((TOTAL, TOTAL), f32),
            jax.ShapeDtypeStruct((4, weighted.shape[0], STREAMS), bf16),
        ),
        in_specs=[SMEM] + [VMEM] * 4,
        out_specs=(VMEM,) * 2,
        compiler_params=params(),
        cost_estimate=cost(10_000_000_000, 4_000_000),
        name="solve",
    )(first, whole, weighted, precoded, slot_plane)


def signal_kernel(users_ref, channel_ref, out_ref, held_ref, sems):
    groups, _, antennas = channel_ref.shape
    tile = antennas // 2
    copies = []
    for g in range(groups):
        for m in range(0, antennas, tile):
            part = t_dot(users_ref[g], channel_ref[g, :, m:m + tile]).astype(bf16)
            held_ref[g, :, :, m:m + tile] = part.reshape(16, STREAMS // 16, tile)
        copy = pltpu.make_async_copy(held_ref.at[g], out_ref.at[:, g], sems.at[g])
        copy.start()
        copies.append(copy)
    for copy in copies:
        copy.wait()


def make_signal(users_side, channel):
    groups, _, antennas = channel.shape
    each = STREAMS // 16
    return pl.pallas_call(
        signal_kernel,
        out_shape=jax.ShapeDtypeStruct((16, groups, each, antennas), bf16),
        in_specs=[VMEM, VMEM],
        out_specs=HBM,
        scratch_shapes=[
            pltpu.VMEM((groups, 16, each, antennas), bf16),
            pltpu.SemaphoreType.DMA((groups,)),
        ],
        compiler_params=params(),
        cost_estimate=cost(800_000_000, 7_000_000),
        name="signal",
    )(users_side, channel)


def update_kernel(
    where_ref, weighted_ref, inv_ref, all_ref, slots_ref, out0, out1, out2, out3, held_ref, sems
):
    first, plane = where_ref[0], where_ref[1]
    user_rows = weighted_ref.shape[0]
    border = weighted_ref[...] - placing(slots_ref, first, user_rows)
    half = split(dot, border, inv_ref[...]).astype(bf16)
    copies = []
    for d, out in enumerate([out0, out1, out2, out3]):
        z = (plane + d) % 4
        there = all_ref[pl.ds(4 * z, 4)].reshape(4 * user_rows, TOTAL).astype(f32)
        there = there - placing(slots_ref, 4 * user_rows * z, 4 * user_rows)
        held_ref[d] = dot_t(half, there.astype(bf16)).astype(bf16)
        copy = pltpu.make_async_copy(held_ref.at[d], out, sems.at[d])
        copy.start()
        copies.append(copy)
    for copy in copies:
        copy.wait()


def make_update(where, weighted, schur_inverse, weighted_all, slot_plane):
    user_rows = weighted.shape[0]
    return pl.pallas_call(
        update_kernel,
        out_shape=(jax.ShapeDtypeStruct((user_rows, 4 * user_rows), bf16),) * 4,
        in_specs=[SMEM] + [VMEM] * 4,
        out_specs=(HBM,) * 4,
        scratch_shapes=[
            pltpu.VMEM((4, user_rows, 4 * user_rows), bf16),
            pltpu.SemaphoreType.DMA((4,)),
        ],
        compiler_params=params(),
        cost_estimate=cost(1_500_000_000, 8_000_000),
        name="update",
    )(where, weighted, schur_inverse, weighted_all, slot_plane)


def local(channels, inverse, arrivals, arrival_cell, cell_owner, slots, symbols):
    group_count, user_rows, antennas = channels.shape
    user_cols = inverse.shape[2]
    capacity = arrivals.shape[2]
    cell_count = cell_owner.shape[0]
    grp_index = lax.axis_index("grp")
    row_index = lax.axis_index("row")
    col_index = lax.axis_index("col")
    y_index, x_index = row_index // 4, row_index % 4

    def along_x(value, step):
        pairs = [(4 * y + x, 4 * y + (x + step) % 4) for y in range(4) for x in range(4)]
        return lax.ppermute(value, "row", pairs)

    def along_y(value, step):
        pairs = [(4 * y + x, 4 * ((y + step) % 4) + x) for y in range(4) for x in range(4)]
        return lax.ppermute(value, "row", pairs)

    def along_z(value, step):
        return lax.ppermute(value, "col", [(z, (z + step) % 4) for z in range(4)])

    def to_planes(value):
        padded = jnp.concatenate([value, jnp.zeros_like(value[:1])], axis=0)
        return lax.all_to_all(padded, "col", 0, 0, tiled=True)

    first_group = grp_index * group_count
    other_first = (1 - grp_index) * group_count
    first_row = row_index * user_rows
    first_arg = first_row.reshape(1)

    with jax.named_scope("newcomers"):
        mine = lax.dynamic_slice_in_dim(arrivals, first_group, group_count, 0)
        theirs = lax.dynamic_slice_in_dim(arrivals, other_first, group_count, 0)
        swapped = lax.ppermute(theirs, "grp", [(0, 1), (1, 0)])
        from_0 = jnp.where(grp_index == 0, mine, swapped)
        from_1 = jnp.where(grp_index == 0, swapped, mine)
        chunk = jnp.stack([from_0, from_1], axis=2)
        per_group = EPOCHS * 2 * capacity
        chunk = chunk.reshape(group_count * per_group, antennas)
        chunk = jnp.pad(chunk, ((0, 112 - group_count * per_group), (0, 0)))
        gathered = lax.all_gather(chunk, "row")

    with jax.named_scope("planes"):
        low = inverse.astype(bf16).reshape(group_count, user_rows, 4, user_rows)
        full_rows = to_planes(low.transpose(0, 2, 1, 3))
        symbol_part = jnp.einsum(
            "grc,gcs->grs", inverse, symbols.astype(f32), precision=highest
        )
        precoded = jnp.sum(to_planes(symbol_part), axis=0)

    plane_group = first_group + jnp.minimum(col_index, group_count - 1)
    slot_plane = lax.dynamic_slice_in_dim(slots, plane_group, 1, 0).reshape(1, TOTAL)
    row_ids = first_row + jnp.arange(user_rows, dtype=jnp.int32)

    cells_mine = lax.dynamic_slice_in_dim(arrival_cell, first_group, group_count, 0)[..., 0]
    slots_mine = lax.dynamic_slice_in_dim(slots, first_group, group_count, 0)
    slots_mine = slots_mine.reshape(group_count, 1, TOTAL)
    cell_table = (cells_mine[..., None] == jnp.arange(cell_count, dtype=jnp.int32)).astype(
        jnp.int32
    )
    owners = jnp.sum(cell_table * cell_owner, axis=-1)
    arrival_order = jnp.arange(ARRIVE, dtype=jnp.int32)
    earlier = (cells_mine[..., :, None] == cells_mine[..., None, :]) & (
        arrival_order[:, None] < arrival_order[None, :]
    )
    ranking = jnp.sum(earlier.astype(jnp.int32), axis=-2)
    with jax.named_scope("places"):
        offset = jnp.arange(group_count, dtype=jnp.int32) * per_group % 16
        epoch = jnp.arange(EPOCHS, dtype=jnp.int32)
        inside = offset[:, None] + epoch[None, :] * 2 * capacity
        inside = inside[:, :, None] + owners // 16 * capacity + ranking
        place = (owners % 16 * WINDOW + inside).reshape(group_count, 1, TOTAL)
        plane_place = lax.dynamic_slice_in_dim(
            place, jnp.minimum(col_index, group_count - 1), 1, 0
        ).reshape(1, TOTAL)

    with jax.named_scope("columns"):
        squares = []
        for d in range(4):
            piece = lax.dynamic_index_in_dim(full_rows, (x_index + d) % 4, 1, keepdims=False)
            squares.append(along_x(piece, d) if d in (1, 3) else piece)
        gathered, squares, precoded = lax.optimization_barrier((gathered, squares, precoded))
        squares[2] = along_x(squares[2], 2)
        both = make_columns(row_index.reshape(1), gathered, channels, place)
        both = lax.all_to_all(both, "col", 0, 0, tiled=True)
        both, squares = lax.optimization_barrier((both, squares))
        summed = jnp.sum(both.astype(f32), axis=0)
        columns = summed[:user_rows]
        gram = summed[user_rows:]
        own = columns.astype(bf16)
        by_row = [own] + [along_x(own, d) for d in (1, 2, 3)]
        by_col = [own] + [along_y(own, -d) for d in (1, 2, 3)]

    with jax.named_scope("schur"):
        where = jnp.stack([y_index, row_index, first_row])
        block0, block1, block2, block3, packed = make_middle(
            where, squares, by_row, by_col, columns, precoded, slot_plane, gram, plane_place
        )
        packed = packed.reshape(16, SHARE, TOTAL + STREAMS)
        shared = lax.all_to_all(packed, "row", 0, 0, tiled=True)
        shared = jnp.sum(shared.astype(f32), axis=0)
        share_ids = row_index * SHARE + jnp.arange(SHARE, dtype=jnp.int32)
        identity = loading * (
            share_ids[:, None] == jnp.arange(TOTAL, dtype=jnp.int32)[None, :]
        ).astype(f32)
        schur_rows = identity - shared[:, :TOTAL]
        ready = jnp.concatenate([schur_rows, shared[:, TOTAL:]], axis=1)
        ready = jnp.broadcast_to(ready[None], (16, SHARE, TOTAL + STREAMS))
        whole = lax.all_to_all(ready, "row", 0, 0, tiled=True).reshape(TOTAL, TOTAL + STREAMS)
        ready, block1, block2, block3 = lax.optimization_barrier((ready, block1, block2, block3))
        weighted = block0
        for d, block in ((1, block1), (2, block2), (3, block3)):
            weighted = weighted + along_x(block, -d).astype(f32)

    with jax.named_scope("users"):
        channel = make_channel(first_arg, gathered, channels, place, slots_mine)
        whole, channel, weighted = lax.optimization_barrier((whole, channel, weighted))
        weighted_all = lax.all_gather(weighted.astype(bf16), "row")
        schur_inverse, users = make_solve(first_arg, whole, weighted, precoded, slot_plane)
        users_side = lax.all_to_all(users, "col", 0, 0, tiled=True)

    with jax.named_scope("update"):
        changes = make_update(
            jnp.stack([first_row, col_index]), weighted, schur_inverse, weighted_all, slot_plane
        )
        changes = [changes[0]] + [along_z(changes[d], d) for d in (1, 2, 3)]

    with jax.named_scope("signal"):
        signal_part = make_signal(users_side, channel)
        received = lax.all_to_all(signal_part, "row", 0, 0, tiled=True)
        received, changes = lax.optimization_barrier((received, changes))
        signal = jnp.sum(received.astype(f32), axis=0)
        power = jnp.sum(signal * signal, axis=(1, 2))
        power = jnp.broadcast_to(power[None, None, :], (64, 1, group_count))
        power = lax.all_to_all(power, ("row", "col"), 0, 0, tiled=True)
        total_power = jnp.sum(power, axis=(0, 1)) / (STREAMS * ANTENNAS)
        transmit = signal * lax.rsqrt(total_power + epsilon)[:, None, None]
        transmit = jnp.swapaxes(transmit, 0, 1)

    with jax.named_scope("final"):
        col_ids = col_index * user_cols + jnp.arange(user_cols, dtype=jnp.int32)
        diagonal = row_ids[:, None] == col_ids[None, :]
        full = jnp.any(slots_mine == row_ids[None, :, None], axis=2)
        gone = jnp.where(diagonal[None] & full[:, :, None], 1.0 / loading, 0.0)
        updated = []
        for g in range(group_count):
            step = (col_index - g) % 4
            add = changes[0]
            for d in (1, 2, 3):
                add = jnp.where(step == d, changes[d], add)
            updated.append(inverse[g] - gone[g] + add.astype(f32))
        updated = jnp.stack(updated, axis=0)
    return (updated, transmit)


def solution(mesh):
    placed = (
        P("grp", "row", "col"),
        P("grp", "row", "col"),
        P(None, None, ("grp", "row"), "col"),
        P(),
        P(),
        P(),
        P("grp", "col", None),
    )
    return jax.shard_map(
        local,
        mesh=mesh,
        in_specs=placed,
        out_specs=(P("grp", "row", "col"), P("row", "grp", "col")),
        check_vma=False,
    )
```

```python
import jax
import jax.numpy as jnp
from jax import lax
from jax.experimental import pallas as pl
from jax.experimental.pallas import tpu as pltpu
from jax.sharding import PartitionSpec as P

ANTENNAS = 8192
ARRIVE = 128
EPOCHS = 3
STREAMS = 256
TOTAL = ARRIVE * EPOCHS
BLOCK = 128
PANEL = 8
WINDOW = 48
SHARE = TOTAL // 16

loading = 1.0
epsilon = 1e-06
highest = lax.Precision.HIGHEST
f32 = jnp.float32
bf16 = jnp.bfloat16
VMEM = pl.BlockSpec(memory_space=pltpu.VMEM)
SMEM = pl.BlockSpec(memory_space=pltpu.SMEM)
HBM = pl.BlockSpec(memory_space=pltpu.HBM)


def params(mib=40):
    return pltpu.CompilerParams(vmem_limit_bytes=mib * 1024 * 1024)


def cost(flops, nbytes):
    return pl.CostEstimate(flops=flops, bytes_accessed=nbytes, transcendentals=0)


def dot(a, b):
    return jnp.dot(a, b, preferred_element_type=f32)


def dot_t(a, b):
    return lax.dot_general(a, b, (((1,), (1,)), ((), ())), preferred_element_type=f32)


def t_dot(a, b):
    return lax.dot_general(a, b, (((0,), (0,)), ((), ())), preferred_element_type=f32)


def halves(a):
    high = a.astype(bf16)
    return high, (a - high.astype(f32)).astype(bf16)


def split(product, a, b):
    a_high, a_low = halves(a)
    b_high, b_low = halves(b)
    return product(a_high, b_low) + product(a_low, b_high) + product(a_high, b_high)


def placing(slots_ref, first, rows):
    ids = first + lax.broadcasted_iota(jnp.int32, (rows, TOTAL), 0)
    return (ids == slots_ref[...].reshape(1, TOTAL)).astype(f32)


def choosing(place_ref, g):
    ids = lax.broadcasted_iota(jnp.int32, (16 * WINDOW, TOTAL), 0)
    return (ids == place_ref[g]).astype(f32).astype(bf16)


def start_inputs(gathered_ref, channel_ref, window_ref, held_ref, sems, row=None):
    groups, user_rows = channel_ref.shape[:2]
    copies = []
    for g in range(groups):
        start = g * 2 * EPOCHS * 6 // 16 * 16
        source = gathered_ref.at[:, pl.ds(start, WINDOW), :]
        parts = [
            pltpu.make_async_copy(channel_ref.at[g], held_ref.at[g, :user_rows], sems.at[0, g]),
            pltpu.make_async_copy(source, window_ref.at[g], sems.at[1, g]),
        ]
        if row is not None:
            source = gathered_ref.at[row, pl.ds(start, WINDOW), :]
            parts.append(
                pltpu.make_async_copy(source, held_ref.at[g, user_rows:], sems.at[2, g])
            )
        for part in parts:
            part.start()
        copies.append(parts)
    return copies


def input_scratch(groups, rows, antennas):
    return [
        pltpu.VMEM((groups, 16, WINDOW, antennas), bf16),
        pltpu.VMEM((groups, rows, antennas), bf16),
        pltpu.SemaphoreType.DMA((3, groups)),
    ]


def columns_kernel(
    row_ref, gathered_ref, channel_ref, place_ref, out_ref, window_ref, held_ref, sems
):
    groups, _, antennas = channel_ref.shape
    copies = start_inputs(gathered_ref, channel_ref, window_ref, held_ref, sems, row_ref[0])
    out_ref[groups] = jnp.zeros(out_ref.shape[1:], bf16)
    for g in range(groups):
        choose = choosing(place_ref, g)
        for copy in copies[g]:
            copy.wait()
        window = window_ref[g].reshape(16 * WINDOW, antennas)
        wide = dot_t(held_ref[g], window).astype(bf16)
        out_ref[g] = dot(wide, choose).astype(bf16)


def make_columns(row, gathered, channels, place):
    groups, user_rows, antennas = channels.shape
    return pl.pallas_call(
        columns_kernel,
        out_shape=jax.ShapeDtypeStruct((groups + 1, user_rows + WINDOW, TOTAL), bf16),
        in_specs=[SMEM, HBM, HBM, VMEM],
        out_specs=VMEM,
        scratch_shapes=input_scratch(groups, user_rows + WINDOW, antennas),
        compiler_params=params(60),
        cost_estimate=cost(4_000_000_000, 12_000_000),
        name="columns",
    )(row, gathered, channels, place)


def channel_kernel(
    first_ref, gathered_ref, channel_ref, place_ref, slots_ref, out_ref, window_ref, held_ref, sems
):
    groups, user_rows, antennas = channel_ref.shape
    copies = start_inputs(gathered_ref, channel_ref, window_ref, held_ref, sems)
    for g in range(groups):
        here = placing(slots_ref.at[g], first_ref[0], user_rows).astype(bf16)
        route = dot_t(here, choosing(place_ref, g)).astype(bf16)
        for copy in copies[g]:
            copy.wait()
        window = window_ref[g].reshape(16 * WINDOW, antennas)
        out_ref[g] = held_ref[g] + dot(route, window).astype(bf16)


def make_channel(first, gathered, channels, place, slots_mine):
    groups, user_rows, antennas = channels.shape
    return pl.pallas_call(
        channel_kernel,
        out_shape=jax.ShapeDtypeStruct(channels.shape, bf16),
        in_specs=[SMEM, HBM, HBM, VMEM, VMEM],
        out_specs=VMEM,
        scratch_shapes=input_scratch(groups, user_rows, antennas),
        compiler_params=params(60),
        cost_estimate=cost(4_000_000_000, 14_000_000),
        name="channel",
    )(first, gathered, channels, place, slots_mine)


def middle_kernel(
    where_ref, square_ref, own_ref, row1_ref, row2_ref, row3_ref, col1_ref, col2_ref, col3_ref, columns_ref, precoded_ref, slots_ref, gram_ref,
    place_ref, first_out, block1_out, block2_out, block3_out, packed_out,
):
    y, row, first = where_ref[0], where_ref[1], where_ref[2]
    user_rows = own_ref.shape[0]
    by_row = [own_ref, row1_ref, row2_ref, row3_ref]
    by_col = [own_ref, col1_ref, col2_ref, col3_ref]
    outs = [first_out, block1_out, block2_out, block3_out]
    ids = row * WINDOW + lax.broadcasted_iota(jnp.int32, (WINDOW, TOTAL), 0)
    choose = (ids == place_ref[...]).astype(f32).astype(bf16)
    schur = -t_dot(choose, gram_ref[...].astype(bf16))
    for d in range(4):
        block = dot(square_ref[y, d], own_ref[...])
        for e in range(1, 4):
            block += dot(square_ref[(y + e) % 4, d], by_col[e][...])
        low = block.astype(bf16)
        outs[d][...] = block if d == 0 else low
        schur += t_dot(by_row[d][...], low)
    packed_out[:, :TOTAL] = schur.astype(bf16)
    border = columns_ref[...] - placing(slots_ref, first, user_rows)
    packed_out[:, TOTAL:] = split(t_dot, border, precoded_ref[...]).astype(bf16)


def make_middle(where, square, by_row, by_col, columns, precoded, slot_plane, gram, place_plane):
    shape = columns.shape
    return pl.pallas_call(
        middle_kernel,
        out_shape=(
            jax.ShapeDtypeStruct(shape, f32),
            jax.ShapeDtypeStruct(shape, bf16),
            jax.ShapeDtypeStruct(shape, bf16),
            jax.ShapeDtypeStruct(shape, bf16),
            jax.ShapeDtypeStruct((TOTAL, TOTAL + STREAMS), bf16),
        ),
        in_specs=[SMEM] + [VMEM] * 13,
        out_specs=(VMEM,) * 5,
        compiler_params=params(),
        cost_estimate=cost(2_000_000_000, 8_000_000),
        name="middle",
    )(where, square, *by_row, *by_col[1:], columns, precoded, slot_plane, gram, place_plane)


def invert_block(a):
    lane = lax.broadcasted_iota(jnp.int32, (1, BLOCK), 1)
    sub = lax.broadcasted_iota(jnp.int32, (PANEL, 1), 0)
    for k in range(0, BLOCK, PANEL):
        inside = (lane >= k) & (lane < k + PANEL)
        rows = a[k:k + PANEL, :]
        cols = [
            jnp.broadcast_to(rows[:, k + j:k + j + 1], (PANEL, BLOCK)) for j in range(PANEL)
        ]
        rows = jnp.where(inside, (lane - k == sub).astype(f32), rows)
        for i in range(PANEL):
            scale = 1.0 / cols[i][i:i + 1, :]
            factor = cols[i] - (sub == i).astype(f32)
            for j in range(i + 1, PANEL):
                cols[j] = cols[j] - factor * (cols[j][i:i + 1, :] * scale)
            rows = rows - factor * (rows[i:i + 1, :] * scale)
        rest = jnp.where(inside, 0.0, a)
        for i in range(PANEL):
            rest = rest - a[:, k + i:k + i + 1] * rows[i:i + 1, :]
        pieces = [rest[:k]] if k else []
        pieces.append(rows)
        if k + PANEL < BLOCK:
            pieces.append(rest[k + PANEL:])
        a = jnp.concatenate(pieces, axis=0)
    return a


def solve_kernel(first_ref, whole_ref, weighted_ref, precoded_ref, slots_ref, inv_ref, users_ref):
    inv_ref[...] = whole_ref[:, :TOTAL]

    @pl.loop(0, TOTAL // BLOCK)
    def _(b):
        start = pl.multiple_of(b * BLOCK, BLOCK)
        here = pl.ds(start, BLOCK)
        pivot_inv = invert_block(inv_ref[here, here])
        panel = inv_ref[:, here]
        row_id = lax.broadcasted_iota(jnp.int32, (TOTAL, BLOCK), 0)
        lane_id = lax.broadcasted_iota(jnp.int32, (TOTAL, BLOCK), 1)
        unit = (row_id == lane_id + start).astype(f32)
        inv_ref[:, here] = unit
        rows = inv_ref[here, :]
        scaled = split(dot, pivot_inv, rows)
        inside = (row_id >= start) & (row_id < start + BLOCK)
        rest = jnp.where(inside, 0.0, panel)
        inv_ref[here, :] = jnp.zeros((BLOCK, TOTAL), f32)
        inv_ref[...] = inv_ref[...] - split(dot, rest, scaled)
        inv_ref[here, :] = scaled

    effect = split(dot, inv_ref[...], whole_ref[:, TOTAL:])
    place = placing(slots_ref, first_ref[0], weighted_ref.shape[0])
    kept = 1.0 - jnp.sum(place, axis=1, keepdims=True)
    users = precoded_ref[...] * kept + split(dot, weighted_ref[...] - place, effect)
    for z in range(4):
        users_ref[z] = users.astype(bf16)


def make_solve(first, whole, weighted, precoded, slot_plane):
    return pl.pallas_call(
        solve_kernel,
        out_shape=(
            jax.ShapeDtypeStruct((TOTAL, TOTAL), f32),
            jax.ShapeDtypeStruct((4, weighted.shape[0], STREAMS), bf16),
        ),
        in_specs=[SMEM] + [VMEM] * 4,
        out_specs=(VMEM,) * 2,
        compiler_params=params(),
        cost_estimate=cost(10_000_000_000, 4_000_000),
        name="solve",
    )(first, whole, weighted, precoded, slot_plane)


def signal_kernel(users_ref, channel_ref, out_ref, held_ref, sems):
    groups, _, antennas = channel_ref.shape
    tile = antennas // 2
    copies = []
    for g in range(groups):
        for m in range(0, antennas, tile):
            part = t_dot(users_ref[g], channel_ref[g, :, m:m + tile]).astype(bf16)
            held_ref[g, :, :, m:m + tile] = part.reshape(16, STREAMS // 16, tile)
        copy = pltpu.make_async_copy(held_ref.at[g], out_ref.at[:, g], sems.at[g])
        copy.start()
        copies.append(copy)
    for copy in copies:
        copy.wait()


def make_signal(users_side, channel):
    groups, _, antennas = channel.shape
    each = STREAMS // 16
    return pl.pallas_call(
        signal_kernel,
        out_shape=jax.ShapeDtypeStruct((16, groups, each, antennas), bf16),
        in_specs=[VMEM, VMEM],
        out_specs=HBM,
        scratch_shapes=[
            pltpu.VMEM((groups, 16, each, antennas), bf16),
            pltpu.SemaphoreType.DMA((groups,)),
        ],
        compiler_params=params(),
        cost_estimate=cost(800_000_000, 7_000_000),
        name="signal",
    )(users_side, channel)


def update_kernel(
    where_ref, weighted_ref, inv_ref, all_ref, slots_ref, out0, out1, out2, out3, held_ref, sems
):
    first, plane = where_ref[0], where_ref[1]
    user_rows = weighted_ref.shape[0]
    border = weighted_ref[...] - placing(slots_ref, first, user_rows)
    half = split(dot, border, inv_ref[...]).astype(bf16)
    copies = []
    for d, out in enumerate([out0, out1, out2, out3]):
        z = (plane + d) % 4
        there = all_ref[pl.ds(4 * z, 4)].reshape(4 * user_rows, TOTAL).astype(f32)
        there = there - placing(slots_ref, 4 * user_rows * z, 4 * user_rows)
        held_ref[d] = dot_t(half, there.astype(bf16)).astype(bf16)
        copy = pltpu.make_async_copy(held_ref.at[d], out, sems.at[d])
        copy.start()
        copies.append(copy)
    for copy in copies:
        copy.wait()


def make_update(where, weighted, schur_inverse, weighted_all, slot_plane):
    user_rows = weighted.shape[0]
    return pl.pallas_call(
        update_kernel,
        out_shape=(jax.ShapeDtypeStruct((user_rows, 4 * user_rows), bf16),) * 4,
        in_specs=[SMEM] + [VMEM] * 4,
        out_specs=(HBM,) * 4,
        scratch_shapes=[
            pltpu.VMEM((4, user_rows, 4 * user_rows), bf16),
            pltpu.SemaphoreType.DMA((4,)),
        ],
        compiler_params=params(),
        cost_estimate=cost(1_500_000_000, 8_000_000),
        name="update",
    )(where, weighted, schur_inverse, weighted_all, slot_plane)


def local(channels, inverse, arrivals, arrival_cell, cell_owner, slots, symbols):
    group_count, user_rows, antennas = channels.shape
    user_cols = inverse.shape[2]
    capacity = arrivals.shape[2]
    cell_count = cell_owner.shape[0]
    grp_index = lax.axis_index("grp")
    row_index = lax.axis_index("row")
    col_index = lax.axis_index("col")
    y_index, x_index = row_index // 4, row_index % 4

    def along_x(value, step):
        pairs = [(4 * y + x, 4 * y + (x + step) % 4) for y in range(4) for x in range(4)]
        return lax.ppermute(value, "row", pairs)

    def along_y(value, step):
        pairs = [(4 * y + x, 4 * ((y + step) % 4) + x) for y in range(4) for x in range(4)]
        return lax.ppermute(value, "row", pairs)

    def along_z(value, step):
        return lax.ppermute(value, "col", [(z, (z + step) % 4) for z in range(4)])

    def to_planes(value):
        padded = jnp.concatenate([value, jnp.zeros_like(value[:1])], axis=0)
        return lax.all_to_all(padded, "col", 0, 0, tiled=True)

    first_group = grp_index * group_count
    other_first = (1 - grp_index) * group_count
    first_row = row_index * user_rows
    first_arg = first_row.reshape(1)

    with jax.named_scope("newcomers"):
        mine = lax.dynamic_slice_in_dim(arrivals, first_group, group_count, 0)
        theirs = lax.dynamic_slice_in_dim(arrivals, other_first, group_count, 0)
        swapped = lax.ppermute(theirs, "grp", [(0, 1), (1, 0)])
        from_0 = jnp.where(grp_index == 0, mine, swapped)
        from_1 = jnp.where(grp_index == 0, swapped, mine)
        chunk = jnp.stack([from_0, from_1], axis=2)
        per_group = EPOCHS * 2 * capacity
        chunk = chunk.reshape(group_count * per_group, antennas)
        chunk = jnp.pad(chunk, ((0, 112 - group_count * per_group), (0, 0)))
        gathered = lax.all_gather(chunk, "row")

    with jax.named_scope("planes"):
        low = inverse.astype(bf16).reshape(group_count, user_rows, 4, user_rows)
        low = low.transpose(2, 0, 1, 3)
        pieces = []
        for d in range(4):
            piece = lax.dynamic_index_in_dim(low, (x_index + d) % 4, 0, keepdims=False)
            pieces.append(along_x(piece, d) if d else piece)
        square = to_planes(jnp.stack(pieces, axis=1))
        symbol_part = jnp.einsum(
            "grc,gcs->grs", inverse, symbols.astype(f32), precision=highest
        )
        precoded = jnp.sum(to_planes(symbol_part), axis=0)

    plane_group = first_group + jnp.minimum(col_index, group_count - 1)
    slot_plane = lax.dynamic_slice_in_dim(slots, plane_group, 1, 0).reshape(1, TOTAL)
    row_ids = first_row + jnp.arange(user_rows, dtype=jnp.int32)

    cells_mine = lax.dynamic_slice_in_dim(arrival_cell, first_group, group_count, 0)[..., 0]
    slots_mine = lax.dynamic_slice_in_dim(slots, first_group, group_count, 0)
    slots_mine = slots_mine.reshape(group_count, 1, TOTAL)
    cell_table = (cells_mine[..., None] == jnp.arange(cell_count, dtype=jnp.int32)).astype(
        jnp.int32
    )
    owners = jnp.sum(cell_table * cell_owner, axis=-1)
    arrival_order = jnp.arange(ARRIVE, dtype=jnp.int32)
    earlier = (cells_mine[..., :, None] == cells_mine[..., None, :]) & (
        arrival_order[:, None] < arrival_order[None, :]
    )
    ranking = jnp.sum(earlier.astype(jnp.int32), axis=-2)
    with jax.named_scope("places"):
        offset = jnp.arange(group_count, dtype=jnp.int32) * per_group % 16
        epoch = jnp.arange(EPOCHS, dtype=jnp.int32)
        inside = offset[:, None] + epoch[None, :] * 2 * capacity
        inside = inside[:, :, None] + owners // 16 * capacity + ranking
        place = (owners % 16 * WINDOW + inside).reshape(group_count, 1, TOTAL)
        plane_place = lax.dynamic_slice_in_dim(
            place, jnp.minimum(col_index, group_count - 1), 1, 0
        ).reshape(1, TOTAL)

    with jax.named_scope("columns"):
        gathered, square, precoded = lax.optimization_barrier((gathered, square, precoded))
        both = make_columns(row_index.reshape(1), gathered, channels, place)
        both = lax.all_to_all(both, "col", 0, 0, tiled=True)
        summed = jnp.sum(both.astype(f32), axis=0)
        columns = summed[:user_rows]
        gram = summed[user_rows:]
        own = columns.astype(bf16)
        by_row = [own] + [along_x(own, d) for d in (1, 2, 3)]
        by_col = [own] + [along_y(own, -d) for d in (1, 2, 3)]

    with jax.named_scope("schur"):
        where = jnp.stack([y_index, row_index, first_row])
        block0, block1, block2, block3, packed = make_middle(
            where, square, by_row, by_col, columns, precoded, slot_plane, gram, plane_place
        )
        weighted = block0
        for d, block in ((1, block1), (2, block2), (3, block3)):
            weighted = weighted + along_x(block, -d).astype(f32)
        weighted_all = lax.all_gather(weighted.astype(bf16), "row")
        packed = packed.reshape(16, SHARE, TOTAL + STREAMS)
        shared = lax.all_to_all(packed, "row", 0, 0, tiled=True)
        shared = jnp.sum(shared.astype(f32), axis=0)
        share_ids = row_index * SHARE + jnp.arange(SHARE, dtype=jnp.int32)
        identity = loading * (
            share_ids[:, None] == jnp.arange(TOTAL, dtype=jnp.int32)[None, :]
        ).astype(f32)
        schur_rows = identity - shared[:, :TOTAL]
        ready = jnp.concatenate([schur_rows, shared[:, TOTAL:]], axis=1)
        ready = jnp.broadcast_to(ready[None], (16, SHARE, TOTAL + STREAMS))
        whole = lax.all_to_all(ready, "row", 0, 0, tiled=True).reshape(TOTAL, TOTAL + STREAMS)

    with jax.named_scope("users"):
        channel = make_channel(first_arg, gathered, channels, place, slots_mine)
        whole, channel = lax.optimization_barrier((whole, channel))
        schur_inverse, users = make_solve(first_arg, whole, weighted, precoded, slot_plane)
        users_side = lax.all_to_all(users, "col", 0, 0, tiled=True)

    with jax.named_scope("update"):
        changes = make_update(
            jnp.stack([first_row, col_index]), weighted, schur_inverse, weighted_all, slot_plane
        )
        changes = [changes[0]] + [along_z(changes[d], d) for d in (1, 2, 3)]

    with jax.named_scope("signal"):
        signal_part = make_signal(users_side, channel)
        received = lax.all_to_all(signal_part, "row", 0, 0, tiled=True)
        received, changes = lax.optimization_barrier((received, changes))
        signal = jnp.sum(received.astype(f32), axis=0)
        power = jnp.sum(signal * signal, axis=(1, 2))
        power = jnp.broadcast_to(power[None, None, :], (64, 1, group_count))
        power = lax.all_to_all(power, ("row", "col"), 0, 0, tiled=True)
        total_power = jnp.sum(power, axis=(0, 1)) / (STREAMS * ANTENNAS)
        transmit = signal * lax.rsqrt(total_power + epsilon)[:, None, None]
        transmit = jnp.swapaxes(transmit, 0, 1)

    with jax.named_scope("final"):
        col_ids = col_index * user_cols + jnp.arange(user_cols, dtype=jnp.int32)
        diagonal = row_ids[:, None] == col_ids[None, :]
        full = jnp.any(slots_mine == row_ids[None, :, None], axis=2)
        gone = jnp.where(diagonal[None] & full[:, :, None], 1.0 / loading, 0.0)
        updated = []
        for g in range(group_count):
            step = (col_index - g) % 4
            add = changes[0]
            for d in (1, 2, 3):
                add = jnp.where(step == d, changes[d], add)
            updated.append(inverse[g] - gone[g] + add.astype(f32))
        updated = jnp.stack(updated, axis=0)
    return (updated, transmit)


def solution(mesh):
    placed = (
        P("grp", "row", "col"),
        P("grp", "row", "col"),
        P(None, None, ("grp", "row"), "col"),
        P(),
        P(),
        P(),
        P("grp", "col", None),
    )
    return jax.shard_map(
        local,
        mesh=mesh,
        in_specs=placed,
        out_specs=(P("grp", "row", "col"), P("row", "grp", "col")),
        check_vma=False,
    )
```

```python
import jax
import jax.numpy as jnp
from jax import lax
from jax.experimental import pallas as pl
from jax.experimental.pallas import tpu as pltpu
from jax.sharding import PartitionSpec as P

ANTENNAS = 8192
ARRIVE = 128
EPOCHS = 3
STREAMS = 256
TOTAL = ARRIVE * EPOCHS
BLOCK = 128
PANEL = 8
WINDOW = 48
SHARE = TOTAL // 16

loading = 1.0
epsilon = 1e-06
highest = lax.Precision.HIGHEST
f32 = jnp.float32
bf16 = jnp.bfloat16
VMEM = pl.BlockSpec(memory_space=pltpu.VMEM)
SMEM = pl.BlockSpec(memory_space=pltpu.SMEM)
HBM = pl.BlockSpec(memory_space=pltpu.HBM)


def params(mib=40):
    return pltpu.CompilerParams(vmem_limit_bytes=mib * 1024 * 1024)


def cost(flops, nbytes):
    return pl.CostEstimate(flops=flops, bytes_accessed=nbytes, transcendentals=0)


def dot(a, b):
    return jnp.dot(a, b, preferred_element_type=f32)


def dot_t(a, b):
    return lax.dot_general(a, b, (((1,), (1,)), ((), ())), preferred_element_type=f32)


def t_dot(a, b):
    return lax.dot_general(a, b, (((0,), (0,)), ((), ())), preferred_element_type=f32)


def halves(a):
    high = a.astype(bf16)
    return high, (a - high.astype(f32)).astype(bf16)


def split(product, a, b):
    a_high, a_low = halves(a)
    b_high, b_low = halves(b)
    return product(a_high, b_low) + product(a_low, b_high) + product(a_high, b_high)


def placing(slots_ref, first, rows):
    ids = first + lax.broadcasted_iota(jnp.int32, (rows, TOTAL), 0)
    return (ids == slots_ref[...].reshape(1, TOTAL)).astype(f32)


def choosing(place_ref, g):
    ids = lax.broadcasted_iota(jnp.int32, (16 * WINDOW, TOTAL), 0)
    return (ids == place_ref[g]).astype(f32).astype(bf16)


def start_inputs(gathered_ref, channel_ref, window_ref, held_ref, sems):
    groups, user_rows = channel_ref.shape[:2]
    copies = []
    for g in range(groups):
        start = g * 2 * EPOCHS * 6 // 16 * 16
        source = gathered_ref.at[:, pl.ds(start, WINDOW), :]
        parts = [
            pltpu.make_async_copy(channel_ref.at[g], held_ref.at[g, :user_rows], sems.at[0, g]),
            pltpu.make_async_copy(source, window_ref.at[g], sems.at[1, g]),
        ]
        for part in parts:
            part.start()
        copies.append(parts)
    return copies


def input_scratch(groups, rows, antennas):
    return [
        pltpu.VMEM((groups, 16, WINDOW, antennas), bf16),
        pltpu.VMEM((groups, rows, antennas), bf16),
        pltpu.SemaphoreType.DMA((2, groups)),
    ]


def columns_kernel(
    row_ref, gathered_ref, channel_ref, place_ref, out_ref, whole_ref, held_ref, sems
):
    groups, user_rows, antennas = channel_ref.shape
    starts = [g * 2 * EPOCHS * 6 // 16 * 16 for g in range(groups)]
    copies = []
    begin = 0
    for g in range(groups):
        rows = pl.ds(begin, starts[g] + WINDOW - begin)
        copy = pltpu.make_async_copy(
            gathered_ref.at[:, rows, :], whole_ref.at[:, rows, :], sems.at[g]
        )
        copy.start()
        copies.append(copy)
        begin = starts[g] + WINDOW
    out_ref[groups] = jnp.zeros(out_ref.shape[1:], bf16)
    held_ref[:, :user_rows] = channel_ref[...]
    for g in range(groups):
        choose = choosing(place_ref, g)
        copies[g].wait()
        rows = pl.ds(starts[g], WINDOW)
        held_ref[g, user_rows:] = whole_ref[row_ref[0], rows, :]
        window = whole_ref[:, rows, :].reshape(16 * WINDOW, antennas)
        wide = dot_t(held_ref[g], window).astype(bf16)
        out_ref[g] = dot(wide, choose).astype(bf16)


def make_columns(row, gathered, channels, place):
    groups, user_rows, antennas = channels.shape
    return pl.pallas_call(
        columns_kernel,
        out_shape=jax.ShapeDtypeStruct((groups + 1, user_rows + WINDOW, TOTAL), bf16),
        in_specs=[SMEM, HBM, VMEM, VMEM],
        out_specs=VMEM,
        scratch_shapes=[
            pltpu.VMEM(gathered.shape, bf16),
            pltpu.VMEM((groups, user_rows + WINDOW, antennas), bf16),
            pltpu.SemaphoreType.DMA((groups,)),
        ],
        compiler_params=params(54),
        cost_estimate=cost(8_000_000_000, 12_000_000),
        name="columns",
    )(row, gathered, channels, place)


def channel_kernel(
    first_ref, gathered_ref, channel_ref, place_ref, slots_ref, out_ref, window_ref, held_ref, sems
):
    groups, user_rows, antennas = channel_ref.shape
    copies = start_inputs(gathered_ref, channel_ref, window_ref, held_ref, sems)
    for g in range(groups):
        here = placing(slots_ref.at[g], first_ref[0], user_rows).astype(bf16)
        route = dot_t(here, choosing(place_ref, g)).astype(bf16)
        for copy in copies[g]:
            copy.wait()
        window = window_ref[g].reshape(16 * WINDOW, antennas)
        out_ref[g] = held_ref[g] + dot(route, window).astype(bf16)


def make_channel(first, gathered, channels, place, slots_mine):
    groups, user_rows, antennas = channels.shape
    return pl.pallas_call(
        channel_kernel,
        out_shape=jax.ShapeDtypeStruct(channels.shape, bf16),
        in_specs=[SMEM, HBM, HBM, VMEM, VMEM],
        out_specs=VMEM,
        scratch_shapes=input_scratch(groups, user_rows, antennas),
        compiler_params=params(60),
        cost_estimate=cost(4_000_000_000, 14_000_000),
        name="channel",
    )(first, gathered, channels, place, slots_mine)


def middle_kernel(
    where_ref, square_ref, own_ref, row1_ref, row2_ref, row3_ref, col1_ref, col2_ref, col3_ref, columns_ref, precoded_ref, slots_ref, gram_ref,
    place_ref, first_out, block1_out, block2_out, block3_out, packed_out,
):
    y, row, first = where_ref[0], where_ref[1], where_ref[2]
    user_rows = own_ref.shape[0]
    by_row = [own_ref, row1_ref, row2_ref, row3_ref]
    by_col = [own_ref, col1_ref, col2_ref, col3_ref]
    outs = [first_out, block1_out, block2_out, block3_out]
    ids = row * WINDOW + lax.broadcasted_iota(jnp.int32, (WINDOW, TOTAL), 0)
    choose = (ids == place_ref[...]).astype(f32).astype(bf16)
    schur = -t_dot(choose, gram_ref[...].astype(bf16))
    for d in range(4):
        block = dot(square_ref[y, d], own_ref[...])
        for e in range(1, 4):
            block += dot(square_ref[(y + e) % 4, d], by_col[e][...])
        low = block.astype(bf16)
        outs[d][...] = block if d == 0 else low
        schur += t_dot(by_row[d][...], low)
    packed_out[:, :TOTAL] = schur.astype(bf16)
    border = columns_ref[...] - placing(slots_ref, first, user_rows)
    packed_out[:, TOTAL:] = split(t_dot, border, precoded_ref[...]).astype(bf16)


def make_middle(where, square, by_row, by_col, columns, precoded, slot_plane, gram, place_plane):
    shape = columns.shape
    return pl.pallas_call(
        middle_kernel,
        out_shape=(
            jax.ShapeDtypeStruct(shape, f32),
            jax.ShapeDtypeStruct(shape, bf16),
            jax.ShapeDtypeStruct(shape, bf16),
            jax.ShapeDtypeStruct(shape, bf16),
            jax.ShapeDtypeStruct((TOTAL, TOTAL + STREAMS), bf16),
        ),
        in_specs=[SMEM] + [VMEM] * 13,
        out_specs=(VMEM,) * 5,
        compiler_params=params(),
        cost_estimate=cost(2_000_000_000, 8_000_000),
        name="middle",
    )(where, square, *by_row, *by_col[1:], columns, precoded, slot_plane, gram, place_plane)


def invert_block(a):
    lane = lax.broadcasted_iota(jnp.int32, (1, BLOCK), 1)
    sub = lax.broadcasted_iota(jnp.int32, (PANEL, 1), 0)
    for k in range(0, BLOCK, PANEL):
        inside = (lane >= k) & (lane < k + PANEL)
        rows = a[k:k + PANEL, :]
        cols = [
            jnp.broadcast_to(rows[:, k + j:k + j + 1], (PANEL, BLOCK)) for j in range(PANEL)
        ]
        rows = jnp.where(inside, (lane - k == sub).astype(f32), rows)
        for i in range(PANEL):
            scale = 1.0 / cols[i][i:i + 1, :]
            factor = cols[i] - (sub == i).astype(f32)
            for j in range(i + 1, PANEL):
                cols[j] = cols[j] - factor * (cols[j][i:i + 1, :] * scale)
            rows = rows - factor * (rows[i:i + 1, :] * scale)
        rest = jnp.where(inside, 0.0, a)
        for i in range(PANEL):
            rest = rest - a[:, k + i:k + i + 1] * rows[i:i + 1, :]
        pieces = [rest[:k]] if k else []
        pieces.append(rows)
        if k + PANEL < BLOCK:
            pieces.append(rest[k + PANEL:])
        a = jnp.concatenate(pieces, axis=0)
    return a


def solve_kernel(
    first_ref, whole_ref, weighted_ref, precoded_ref, slots_ref, pivots_ref, users_ref, work_ref
):
    work_ref[...] = whole_ref[...]
    for b in range(EPOCHS):
        here = slice(b * BLOCK, (b + 1) * BLOCK)
        pivot = invert_block(work_ref[here, here])
        pivots_ref[b] = pivot
        scaled = split(dot, pivot, work_ref[here, here.stop:])
        work_ref[here, here.stop:] = scaled
        if b + 1 < EPOCHS:
            below = work_ref[here.stop:, here]
            work_ref[here.stop:, here.stop:] -= split(dot, below, scaled)
    effect = work_ref[TOTAL - BLOCK:, TOTAL:]
    for b in range(EPOCHS - 2, -1, -1):
        here = slice(b * BLOCK, (b + 1) * BLOCK)
        part = work_ref[here, TOTAL:] - split(dot, work_ref[here, here.stop:TOTAL], effect)
        effect = jnp.concatenate([part, effect], axis=0)
    place = placing(slots_ref, first_ref[0], weighted_ref.shape[0])
    kept = 1.0 - jnp.sum(place, axis=1, keepdims=True)
    users = precoded_ref[...] * kept + split(dot, weighted_ref[...] - place, effect)
    for z in range(4):
        users_ref[z] = users.astype(bf16)


def make_solve(first, whole, weighted, precoded, slot_plane):
    return pl.pallas_call(
        solve_kernel,
        out_shape=(
            jax.ShapeDtypeStruct((EPOCHS, BLOCK, BLOCK), f32),
            jax.ShapeDtypeStruct((4, weighted.shape[0], STREAMS), bf16),
        ),
        in_specs=[SMEM] + [VMEM] * 4,
        out_specs=(VMEM,) * 2,
        scratch_shapes=[pltpu.VMEM(whole.shape, f32)],
        compiler_params=params(),
        cost_estimate=cost(14_000_000_000, 4_000_000),
        name="solve",
    )(first, whole, weighted, precoded, slot_plane)


def inverse_of(whole_ref, pivots_ref, inv_ref):
    inv_ref[...] = whole_ref[:, :TOTAL]
    row_id = lax.broadcasted_iota(jnp.int32, (TOTAL, BLOCK), 0)
    lane_id = lax.broadcasted_iota(jnp.int32, (TOTAL, BLOCK), 1)
    for b in range(EPOCHS):
        here = slice(b * BLOCK, (b + 1) * BLOCK)
        inside = (row_id >= here.start) & (row_id < here.stop)
        rest = jnp.where(inside, 0.0, inv_ref[:, here])
        inv_ref[:, here] = (row_id == lane_id + here.start).astype(f32)
        scaled = split(dot, pivots_ref[b], inv_ref[here, :])
        inv_ref[here, :] = jnp.zeros((BLOCK, TOTAL), f32)
        inv_ref[...] = inv_ref[...] - split(dot, rest, scaled)
        inv_ref[here, :] = scaled


def signal_kernel(users_ref, channel_ref, out_ref, held_ref, sems):
    groups, _, antennas = channel_ref.shape
    tile = antennas // 2
    copies = []
    for g in range(groups):
        for m in range(0, antennas, tile):
            part = t_dot(users_ref[g], channel_ref[g, :, m:m + tile]).astype(bf16)
            held_ref[g, :, :, m:m + tile] = part.reshape(16, STREAMS // 16, tile)
        copy = pltpu.make_async_copy(held_ref.at[g], out_ref.at[:, g], sems.at[g])
        copy.start()
        copies.append(copy)
    for copy in copies:
        copy.wait()


def make_signal(users_side, channel):
    groups, _, antennas = channel.shape
    each = STREAMS // 16
    return pl.pallas_call(
        signal_kernel,
        out_shape=jax.ShapeDtypeStruct((16, groups, each, antennas), bf16),
        in_specs=[VMEM, VMEM],
        out_specs=HBM,
        scratch_shapes=[
            pltpu.VMEM((groups, 16, each, antennas), bf16),
            pltpu.SemaphoreType.DMA((groups,)),
        ],
        compiler_params=params(),
        cost_estimate=cost(800_000_000, 7_000_000),
        name="signal",
    )(users_side, channel)


def total_kernel(received_ref, signal_ref, power_ref, sums_ref):
    g = pl.program_id(0)
    signal = jnp.sum(received_ref[:, 0].astype(f32), axis=0)
    signal_ref[0] = signal
    power = jnp.sum(signal * signal)
    lane = lax.broadcasted_iota(jnp.int32, sums_ref.shape, 1)

    @pl.when(g == 0)
    def _():
        sums_ref[...] = jnp.zeros(sums_ref.shape, f32)

    sums_ref[...] = jnp.where(lane == g, power, sums_ref[...])

    @pl.when(g == pl.num_programs(0) - 1)
    def _():
        power_ref[...] = jnp.broadcast_to(sums_ref[...][None], power_ref.shape)


def make_total(received):
    sources, groups, each, antennas = received.shape
    return pl.pallas_call(
        total_kernel,
        out_shape=(
            jax.ShapeDtypeStruct((groups, each, antennas), f32),
            jax.ShapeDtypeStruct((64, 1, 128), f32),
        ),
        grid=(groups,),
        in_specs=[pl.BlockSpec((sources, 1, each, antennas), lambda g: (0, g, 0, 0))],
        out_specs=(
            pl.BlockSpec((1, each, antennas), lambda g: (g, 0, 0)),
            pl.BlockSpec((64, 1, 128), lambda g: (0, 0, 0)),
        ),
        scratch_shapes=[pltpu.VMEM((1, 128), f32)],
        compiler_params=params(),
        cost_estimate=cost(2_000_000_000, 4_000_000),
        name="total",
    )(received)


def update_kernel(
    where_ref, weighted_ref, whole_ref, pivots_ref, all_ref, slots_ref,
    out0, out1, out2, out3, inv_ref, held_ref, sems,
):
    first, plane = where_ref[0], where_ref[1]
    user_rows = weighted_ref.shape[0]
    inverse_of(whole_ref, pivots_ref, inv_ref)
    border = weighted_ref[...] - placing(slots_ref, first, user_rows)
    half = split(dot, border, inv_ref[...]).astype(bf16)
    copies = []
    for d, out in enumerate([out0, out1, out2, out3]):
        z = (plane + d) % 4
        there = all_ref[pl.ds(4 * z, 4)].reshape(4 * user_rows, TOTAL).astype(f32)
        there = there - placing(slots_ref, 4 * user_rows * z, 4 * user_rows)
        held_ref[d] = dot_t(half, there.astype(bf16)).astype(bf16)
        copy = pltpu.make_async_copy(held_ref.at[d], out, sems.at[d])
        copy.start()
        copies.append(copy)
    for copy in copies:
        copy.wait()


def make_update(where, weighted, whole, pivots, weighted_all, slot_plane):
    user_rows = weighted.shape[0]
    return pl.pallas_call(
        update_kernel,
        out_shape=(jax.ShapeDtypeStruct((user_rows, 4 * user_rows), bf16),) * 4,
        in_specs=[SMEM] + [VMEM] * 5,
        out_specs=(HBM,) * 4,
        scratch_shapes=[
            pltpu.VMEM((TOTAL, TOTAL), f32),
            pltpu.VMEM((4, user_rows, 4 * user_rows), bf16),
            pltpu.SemaphoreType.DMA((4,)),
        ],
        compiler_params=params(),
        cost_estimate=cost(1_500_000_000, 8_000_000),
        name="update",
    )(where, weighted, whole, pivots, weighted_all, slot_plane)


def local(channels, inverse, arrivals, arrival_cell, cell_owner, slots, symbols):
    group_count, user_rows, antennas = channels.shape
    user_cols = inverse.shape[2]
    capacity = arrivals.shape[2]
    cell_count = cell_owner.shape[0]
    grp_index = lax.axis_index("grp")
    row_index = lax.axis_index("row")
    col_index = lax.axis_index("col")
    y_index, x_index = row_index // 4, row_index % 4

    def along_x(value, step):
        pairs = [(4 * y + x, 4 * y + (x + step) % 4) for y in range(4) for x in range(4)]
        return lax.ppermute(value, "row", pairs)

    def along_y(value, step):
        pairs = [(4 * y + x, 4 * ((y + step) % 4) + x) for y in range(4) for x in range(4)]
        return lax.ppermute(value, "row", pairs)

    def along_z(value, step):
        return lax.ppermute(value, "col", [(z, (z + step) % 4) for z in range(4)])

    def to_planes(value):
        padded = jnp.concatenate([value, jnp.zeros_like(value[:1])], axis=0)
        return lax.all_to_all(padded, "col", 0, 0, tiled=True)

    first_group = grp_index * group_count
    other_first = (1 - grp_index) * group_count
    first_row = row_index * user_rows
    first_arg = first_row.reshape(1)

    with jax.named_scope("newcomers"):
        mine = lax.dynamic_slice_in_dim(arrivals, first_group, group_count, 0)
        theirs = lax.dynamic_slice_in_dim(arrivals, other_first, group_count, 0)
        swapped = lax.ppermute(theirs, "grp", [(0, 1), (1, 0)])
        from_0 = jnp.where(grp_index == 0, mine, swapped)
        from_1 = jnp.where(grp_index == 0, swapped, mine)
        chunk = jnp.stack([from_0, from_1], axis=2)
        per_group = EPOCHS * 2 * capacity
        chunk = chunk.reshape(group_count * per_group, antennas)
        chunk = jnp.pad(chunk, ((0, 112 - group_count * per_group), (0, 0)))
        gathered = lax.all_gather(chunk, "row")

    with jax.named_scope("planes"):
        low = inverse.astype(bf16).reshape(group_count, user_rows, 4, user_rows)
        low = low.transpose(2, 0, 1, 3)
        pieces = []
        for d in range(4):
            piece = lax.dynamic_index_in_dim(low, (x_index + d) % 4, 0, keepdims=False)
            pieces.append(along_x(piece, d) if d else piece)
        square = to_planes(jnp.stack(pieces, axis=1))
        symbol_part = jnp.einsum(
            "grc,gcs->grs", inverse, symbols.astype(f32), precision=highest
        )
        precoded = jnp.sum(to_planes(symbol_part), axis=0)

    plane_group = first_group + jnp.minimum(col_index, group_count - 1)
    slot_plane = lax.dynamic_slice_in_dim(slots, plane_group, 1, 0).reshape(1, TOTAL)
    row_ids = first_row + jnp.arange(user_rows, dtype=jnp.int32)

    cells_mine = lax.dynamic_slice_in_dim(arrival_cell, first_group, group_count, 0)[..., 0]
    slots_mine = lax.dynamic_slice_in_dim(slots, first_group, group_count, 0)
    slots_mine = slots_mine.reshape(group_count, 1, TOTAL)
    cell_table = (cells_mine[..., None] == jnp.arange(cell_count, dtype=jnp.int32)).astype(
        jnp.int32
    )
    owners = jnp.sum(cell_table * cell_owner, axis=-1)
    arrival_order = jnp.arange(ARRIVE, dtype=jnp.int32)
    earlier = (cells_mine[..., :, None] == cells_mine[..., None, :]) & (
        arrival_order[:, None] < arrival_order[None, :]
    )
    ranking = jnp.sum(earlier.astype(jnp.int32), axis=-2)
    with jax.named_scope("places"):
        offset = jnp.arange(group_count, dtype=jnp.int32) * per_group % 16
        epoch = jnp.arange(EPOCHS, dtype=jnp.int32)
        inside = offset[:, None] + epoch[None, :] * 2 * capacity
        inside = inside[:, :, None] + owners // 16 * capacity + ranking
        place = (owners % 16 * WINDOW + inside).reshape(group_count, 1, TOTAL)
        plane_place = lax.dynamic_slice_in_dim(
            place, jnp.minimum(col_index, group_count - 1), 1, 0
        ).reshape(1, TOTAL)

    with jax.named_scope("columns"):
        gathered, square, precoded = lax.optimization_barrier((gathered, square, precoded))
        both = make_columns(row_index.reshape(1), gathered, channels, place)
        both = lax.all_to_all(both, "col", 0, 0, tiled=True)
        summed = jnp.sum(both.astype(f32), axis=0)
        columns = summed[:user_rows]
        gram = summed[user_rows:]
        own = columns.astype(bf16)
        by_row = [own] + [along_x(own, d) for d in (1, 2, 3)]
        by_col = [own] + [along_y(own, -d) for d in (1, 2, 3)]

    with jax.named_scope("schur"):
        where = jnp.stack([y_index, row_index, first_row])
        block0, block1, block2, block3, packed = make_middle(
            where, square, by_row, by_col, columns, precoded, slot_plane, gram, plane_place
        )
        packed = packed.reshape(16, SHARE, TOTAL + STREAMS)
        shared = lax.all_to_all(packed, "row", 0, 0, tiled=True)
        blocks = [along_x(block1, -1), along_x(block2, -2), along_x(block3, -3)]
        shared, blocks = lax.optimization_barrier((shared, blocks))
        weighted = block0
        for block in blocks:
            weighted = weighted + block.astype(f32)
        weighted_all = lax.all_gather(weighted.astype(bf16), "row")
        shared = jnp.sum(shared.astype(f32), axis=0)
        share_ids = row_index * SHARE + jnp.arange(SHARE, dtype=jnp.int32)
        identity = loading * (
            share_ids[:, None] == jnp.arange(TOTAL, dtype=jnp.int32)[None, :]
        ).astype(f32)
        schur_rows = identity - shared[:, :TOTAL]
        ready = jnp.concatenate([schur_rows, shared[:, TOTAL:]], axis=1)
        ready = jnp.broadcast_to(ready[None], (16, SHARE, TOTAL + STREAMS))
        whole = lax.all_to_all(ready, "row", 0, 0, tiled=True).reshape(TOTAL, TOTAL + STREAMS)

    with jax.named_scope("users"):
        channel = make_channel(first_arg, gathered, channels, place, slots_mine)
        whole, channel = lax.optimization_barrier((whole, channel))
        pivots, users = make_solve(first_arg, whole, weighted, precoded, slot_plane)
        users_side = lax.all_to_all(users, "col", 0, 0, tiled=True)

    with jax.named_scope("update"):
        changes = make_update(
            jnp.stack([first_row, col_index]), weighted, whole, pivots, weighted_all, slot_plane
        )
        changes = [changes[0]] + [along_z(changes[d], d) for d in (1, 2, 3)]

    with jax.named_scope("signal"):
        signal_part = make_signal(users_side, channel)
        received = lax.all_to_all(signal_part, "row", 0, 0, tiled=True)
        received, changes = lax.optimization_barrier((received, changes))
        signal, power = make_total(received)
        power = lax.all_to_all(power, ("row", "col"), 0, 0, tiled=True)
        total_power = jnp.sum(power, axis=(0, 1))[:group_count] / (STREAMS * ANTENNAS)
        transmit = signal * lax.rsqrt(total_power + epsilon)[:, None, None]
        transmit = jnp.swapaxes(transmit, 0, 1)

    with jax.named_scope("final"):
        col_ids = col_index * user_cols + jnp.arange(user_cols, dtype=jnp.int32)
        diagonal = row_ids[:, None] == col_ids[None, :]
        full = jnp.any(slots_mine == row_ids[None, :, None], axis=2)
        gone = jnp.where(diagonal[None] & full[:, :, None], 1.0 / loading, 0.0)
        updated = []
        for g in range(group_count):
            step = (col_index - g) % 4
            add = changes[0]
            for d in (1, 2, 3):
                add = jnp.where(step == d, changes[d], add)
            updated.append(inverse[g] - gone[g] + add.astype(f32))
        updated = jnp.stack(updated, axis=0)
    return (updated, transmit)


def solution(mesh):
    placed = (
        P("grp", "row", "col"),
        P("grp", "row", "col"),
        P(None, None, ("grp", "row"), "col"),
        P(),
        P(),
        P(),
        P("grp", "col", None),
    )
    return jax.shard_map(
        local,
        mesh=mesh,
        in_specs=placed,
        out_specs=(P("grp", "row", "col"), P("row", "grp", "col")),
        check_vma=False,
    )
```

```python
import jax
import jax.numpy as jnp
from jax import lax
from jax.experimental import pallas as pl
from jax.experimental.pallas import tpu as pltpu
from jax.sharding import PartitionSpec as P

ANTENNAS = 8192
ARRIVE = 128
EPOCHS = 3
STREAMS = 256
TOTAL = ARRIVE * EPOCHS
BLOCK = 128
PANEL = 8
WINDOW = 48
SHARE = TOTAL // 16

loading = 1.0
epsilon = 1e-06
highest = lax.Precision.HIGHEST
f32 = jnp.float32
bf16 = jnp.bfloat16
VMEM = pl.BlockSpec(memory_space=pltpu.VMEM)
SMEM = pl.BlockSpec(memory_space=pltpu.SMEM)
HBM = pl.BlockSpec(memory_space=pltpu.HBM)


def params(mib=40):
    return pltpu.CompilerParams(vmem_limit_bytes=mib * 1024 * 1024)


def cost(flops, nbytes):
    return pl.CostEstimate(flops=flops, bytes_accessed=nbytes, transcendentals=0)


def dot(a, b):
    return jnp.dot(a, b, preferred_element_type=f32)


def dot_t(a, b):
    return lax.dot_general(a, b, (((1,), (1,)), ((), ())), preferred_element_type=f32)


def t_dot(a, b):
    return lax.dot_general(a, b, (((0,), (0,)), ((), ())), preferred_element_type=f32)


def halves(a):
    high = a.astype(bf16)
    return high, (a - high.astype(f32)).astype(bf16)


def split(product, a, b):
    a_high, a_low = halves(a)
    b_high, b_low = halves(b)
    return product(a_high, b_low) + product(a_low, b_high) + product(a_high, b_high)


def placing(slots_ref, first, rows):
    ids = first + lax.broadcasted_iota(jnp.int32, (rows, TOTAL), 0)
    return (ids == slots_ref[...].reshape(1, TOTAL)).astype(f32)


def choosing(place_ref, g):
    ids = lax.broadcasted_iota(jnp.int32, (16 * WINDOW, TOTAL), 0)
    return (ids == place_ref[g]).astype(f32).astype(bf16)


def start_inputs(gathered_ref, channel_ref, window_ref, held_ref, sems, row=None):
    groups, user_rows = channel_ref.shape[:2]
    copies = []
    for g in range(groups):
        start = g * 2 * EPOCHS * 6 // 16 * 16
        source = gathered_ref.at[:, pl.ds(start, WINDOW), :]
        parts = [
            pltpu.make_async_copy(channel_ref.at[g], held_ref.at[g, :user_rows], sems.at[0, g]),
            pltpu.make_async_copy(source, window_ref.at[g], sems.at[1, g]),
        ]
        if row is not None:
            source = gathered_ref.at[row, pl.ds(start, WINDOW), :]
            parts.append(
                pltpu.make_async_copy(source, held_ref.at[g, user_rows:], sems.at[2, g])
            )
        for part in parts:
            part.start()
        copies.append(parts)
    return copies


def input_scratch(groups, rows, antennas):
    return [
        pltpu.VMEM((groups, 16, WINDOW, antennas), bf16),
        pltpu.VMEM((groups, rows, antennas), bf16),
        pltpu.SemaphoreType.DMA((3, groups)),
    ]


def columns_kernel(
    row_ref, gathered_ref, channel_ref, place_ref, out_ref, window_ref, held_ref, sems
):
    groups, _, antennas = channel_ref.shape
    copies = start_inputs(gathered_ref, channel_ref, window_ref, held_ref, sems, row_ref[0])
    out_ref[groups] = jnp.zeros(out_ref.shape[1:], bf16)
    for g in range(groups):
        choose = choosing(place_ref, g)
        for copy in copies[g]:
            copy.wait()
        window = window_ref[g].reshape(16 * WINDOW, antennas)
        wide = dot_t(held_ref[g], window).astype(bf16)
        out_ref[g] = dot(wide, choose).astype(bf16)


def make_columns(row, gathered, channels, place):
    groups, user_rows, antennas = channels.shape
    return pl.pallas_call(
        columns_kernel,
        out_shape=jax.ShapeDtypeStruct((groups + 1, user_rows + WINDOW, TOTAL), bf16),
        in_specs=[SMEM, HBM, HBM, VMEM],
        out_specs=VMEM,
        scratch_shapes=input_scratch(groups, user_rows + WINDOW, antennas),
        compiler_params=params(60),
        cost_estimate=cost(4_000_000_000, 12_000_000),
        name="columns",
    )(row, gathered, channels, place)


def channel_kernel(
    first_ref, gathered_ref, channel_ref, place_ref, slots_ref, out_ref, window_ref, held_ref, sems
):
    groups, user_rows, antennas = channel_ref.shape
    copies = start_inputs(gathered_ref, channel_ref, window_ref, held_ref, sems)
    for g in range(groups):
        here = placing(slots_ref.at[g], first_ref[0], user_rows).astype(bf16)
        route = dot_t(here, choosing(place_ref, g)).astype(bf16)
        for copy in copies[g]:
            copy.wait()
        window = window_ref[g].reshape(16 * WINDOW, antennas)
        out_ref[g] = held_ref[g] + dot(route, window).astype(bf16)


def make_channel(first, gathered, channels, place, slots_mine):
    groups, user_rows, antennas = channels.shape
    return pl.pallas_call(
        channel_kernel,
        out_shape=jax.ShapeDtypeStruct(channels.shape, bf16),
        in_specs=[SMEM, HBM, HBM, VMEM, VMEM],
        out_specs=VMEM,
        scratch_shapes=input_scratch(groups, user_rows, antennas),
        compiler_params=params(60),
        cost_estimate=cost(4_000_000_000, 14_000_000),
        name="channel",
    )(first, gathered, channels, place, slots_mine)


def pieces_kernel(x_ref, inverse_ref, out0, out1, out2, out3):
    size = out0.shape[-1]
    for d, out in enumerate([out0, out1, out2, out3]):
        start = pl.multiple_of((x_ref[0] + d) % 4 * size, size)
        out[...] = inverse_ref[:, :, pl.ds(start, size)].astype(bf16)


def make_pieces(x, inverse):
    groups, user_rows = inverse.shape[:2]
    shape = jax.ShapeDtypeStruct((groups, user_rows, user_rows), bf16)
    return pl.pallas_call(
        pieces_kernel,
        out_shape=(shape,) * 4,
        in_specs=[SMEM, VMEM],
        out_specs=(VMEM,) * 4,
        compiler_params=params(16),
        cost_estimate=cost(100_000_000, 5_000_000),
        name="pieces",
    )(x, inverse)


def middle_kernel(
    where_ref, square_ref, own_ref, row1_ref, row2_ref, row3_ref, col1_ref, col2_ref, col3_ref, columns_ref, precoded_ref, slots_ref, gram_ref,
    place_ref, first_out, block1_out, block2_out, block3_out, packed_out,
):
    y, row, first = where_ref[0], where_ref[1], where_ref[2]
    user_rows = own_ref.shape[0]
    by_row = [own_ref, row1_ref, row2_ref, row3_ref]
    by_col = [own_ref, col1_ref, col2_ref, col3_ref]
    outs = [first_out, block1_out, block2_out, block3_out]
    ids = row * WINDOW + lax.broadcasted_iota(jnp.int32, (WINDOW, TOTAL), 0)
    choose = (ids == place_ref[...]).astype(f32).astype(bf16)
    schur = -t_dot(choose, gram_ref[...].astype(bf16))
    for d in range(4):
        block = dot(square_ref[y, d], own_ref[...])
        for e in range(1, 4):
            block += dot(square_ref[(y + e) % 4, d], by_col[e][...])
        low = block.astype(bf16)
        outs[d][...] = block if d == 0 else low
        schur += t_dot(by_row[d][...], low)
    packed_out[:, :TOTAL] = schur.astype(bf16)
    border = columns_ref[...] - placing(slots_ref, first, user_rows)
    packed_out[:, TOTAL:] = split(t_dot, border, precoded_ref[...]).astype(bf16)


def make_middle(where, square, by_row, by_col, columns, precoded, slot_plane, gram, place_plane):
    shape = columns.shape
    return pl.pallas_call(
        middle_kernel,
        out_shape=(
            jax.ShapeDtypeStruct(shape, f32),
            jax.ShapeDtypeStruct(shape, bf16),
            jax.ShapeDtypeStruct(shape, bf16),
            jax.ShapeDtypeStruct(shape, bf16),
            jax.ShapeDtypeStruct((TOTAL, TOTAL + STREAMS), bf16),
        ),
        in_specs=[SMEM] + [VMEM] * 13,
        out_specs=(VMEM,) * 5,
        compiler_params=params(),
        cost_estimate=cost(2_000_000_000, 8_000_000),
        name="middle",
    )(where, square, *by_row, *by_col[1:], columns, precoded, slot_plane, gram, place_plane)


def invert_block(a):
    lane = lax.broadcasted_iota(jnp.int32, (1, BLOCK), 1)
    sub = lax.broadcasted_iota(jnp.int32, (PANEL, 1), 0)
    for k in range(0, BLOCK, PANEL):
        inside = (lane >= k) & (lane < k + PANEL)
        rows = a[k:k + PANEL, :]
        cols = [
            jnp.broadcast_to(rows[:, k + j:k + j + 1], (PANEL, BLOCK)) for j in range(PANEL)
        ]
        rows = jnp.where(inside, (lane - k == sub).astype(f32), rows)
        for i in range(PANEL):
            scale = 1.0 / cols[i][i:i + 1, :]
            factor = cols[i] - (sub == i).astype(f32)
            for j in range(i + 1, PANEL):
                cols[j] = cols[j] - factor * (cols[j][i:i + 1, :] * scale)
            rows = rows - factor * (rows[i:i + 1, :] * scale)
        rest = jnp.where(inside, 0.0, a)
        for i in range(PANEL):
            rest = rest - a[:, k + i:k + i + 1] * rows[i:i + 1, :]
        pieces = [rest[:k]] if k else []
        pieces.append(rows)
        if k + PANEL < BLOCK:
            pieces.append(rest[k + PANEL:])
        a = jnp.concatenate(pieces, axis=0)
    return a


def solve_kernel(
    first_ref, whole_ref, weighted_ref, precoded_ref, slots_ref, pivots_ref, users_ref, work_ref
):
    work_ref[...] = whole_ref[...]
    for b in range(EPOCHS):
        here = slice(b * BLOCK, (b + 1) * BLOCK)
        pivot = invert_block(work_ref[here, here])
        pivots_ref[b] = pivot
        scaled = split(dot, pivot, work_ref[here, here.stop:])
        work_ref[here, here.stop:] = scaled
        if b + 1 < EPOCHS:
            below = work_ref[here.stop:, here]
            work_ref[here.stop:, here.stop:] -= split(dot, below, scaled)
    effect = work_ref[TOTAL - BLOCK:, TOTAL:]
    for b in range(EPOCHS - 2, -1, -1):
        here = slice(b * BLOCK, (b + 1) * BLOCK)
        part = work_ref[here, TOTAL:] - split(dot, work_ref[here, here.stop:TOTAL], effect)
        effect = jnp.concatenate([part, effect], axis=0)
    place = placing(slots_ref, first_ref[0], weighted_ref.shape[0])
    kept = 1.0 - jnp.sum(place, axis=1, keepdims=True)
    users = precoded_ref[...] * kept + split(dot, weighted_ref[...] - place, effect)
    for z in range(4):
        users_ref[z] = users.astype(bf16)


def make_solve(first, whole, weighted, precoded, slot_plane):
    return pl.pallas_call(
        solve_kernel,
        out_shape=(
            jax.ShapeDtypeStruct((EPOCHS, BLOCK, BLOCK), f32),
            jax.ShapeDtypeStruct((4, weighted.shape[0], STREAMS), bf16),
        ),
        in_specs=[SMEM] + [VMEM] * 4,
        out_specs=(VMEM,) * 2,
        scratch_shapes=[pltpu.VMEM(whole.shape, f32)],
        compiler_params=params(),
        cost_estimate=cost(14_000_000_000, 4_000_000),
        name="solve",
    )(first, whole, weighted, precoded, slot_plane)


def inverse_of(whole_ref, pivots_ref, inv_ref):
    inv_ref[...] = whole_ref[:, :TOTAL]
    row_id = lax.broadcasted_iota(jnp.int32, (TOTAL, BLOCK), 0)
    lane_id = lax.broadcasted_iota(jnp.int32, (TOTAL, BLOCK), 1)
    for b in range(EPOCHS):
        here = slice(b * BLOCK, (b + 1) * BLOCK)
        inside = (row_id >= here.start) & (row_id < here.stop)
        rest = jnp.where(inside, 0.0, inv_ref[:, here])
        inv_ref[:, here] = (row_id == lane_id + here.start).astype(f32)
        scaled = split(dot, pivots_ref[b], inv_ref[here, :])
        inv_ref[here, :] = jnp.zeros((BLOCK, TOTAL), f32)
        inv_ref[...] = inv_ref[...] - split(dot, rest, scaled)
        inv_ref[here, :] = scaled


def signal_kernel(users_ref, channel_ref, out_ref, held_ref, sems):
    groups, _, antennas = channel_ref.shape
    tile = antennas // 2
    copies = []
    for g in range(groups):
        for m in range(0, antennas, tile):
            part = t_dot(users_ref[g], channel_ref[g, :, m:m + tile]).astype(bf16)
            held_ref[g, :, :, m:m + tile] = part.reshape(16, STREAMS // 16, tile)
        copy = pltpu.make_async_copy(held_ref.at[g], out_ref.at[:, g], sems.at[g])
        copy.start()
        copies.append(copy)
    for copy in copies:
        copy.wait()


def make_signal(users_side, channel):
    groups, _, antennas = channel.shape
    each = STREAMS // 16
    return pl.pallas_call(
        signal_kernel,
        out_shape=jax.ShapeDtypeStruct((16, groups, each, antennas), bf16),
        in_specs=[VMEM, VMEM],
        out_specs=HBM,
        scratch_shapes=[
            pltpu.VMEM((groups, 16, each, antennas), bf16),
            pltpu.SemaphoreType.DMA((groups,)),
        ],
        compiler_params=params(),
        cost_estimate=cost(800_000_000, 7_000_000),
        name="signal",
    )(users_side, channel)


def total_kernel(received_ref, signal_ref, power_ref, sums_ref):
    g = pl.program_id(0)
    signal = jnp.sum(received_ref[:, 0].astype(f32), axis=0)
    signal_ref[0] = signal
    power = jnp.sum(signal * signal)
    lane = lax.broadcasted_iota(jnp.int32, sums_ref.shape, 1)

    @pl.when(g == 0)
    def _():
        sums_ref[...] = jnp.zeros(sums_ref.shape, f32)

    sums_ref[...] = jnp.where(lane == g, power, sums_ref[...])

    @pl.when(g == pl.num_programs(0) - 1)
    def _():
        power_ref[...] = jnp.broadcast_to(sums_ref[...][None], power_ref.shape)


def make_total(received):
    sources, groups, each, antennas = received.shape
    return pl.pallas_call(
        total_kernel,
        out_shape=(
            jax.ShapeDtypeStruct((groups, each, antennas), f32),
            jax.ShapeDtypeStruct((64, 1, 128), f32),
        ),
        grid=(groups,),
        in_specs=[pl.BlockSpec((sources, 1, each, antennas), lambda g: (0, g, 0, 0))],
        out_specs=(
            pl.BlockSpec((1, each, antennas), lambda g: (g, 0, 0)),
            pl.BlockSpec((64, 1, 128), lambda g: (0, 0, 0)),
        ),
        scratch_shapes=[pltpu.VMEM((1, 128), f32)],
        compiler_params=params(),
        cost_estimate=cost(2_000_000_000, 4_000_000),
        name="total",
    )(received)


def update_kernel(
    where_ref, weighted_ref, whole_ref, pivots_ref, all_ref, slots_ref,
    out0, out1, out2, out3, inv_ref, held_ref, sems,
):
    first, plane = where_ref[0], where_ref[1]
    user_rows = weighted_ref.shape[0]
    inverse_of(whole_ref, pivots_ref, inv_ref)
    border = weighted_ref[...] - placing(slots_ref, first, user_rows)
    half = split(dot, border, inv_ref[...]).astype(bf16)
    copies = []
    for d, out in enumerate([out0, out1, out2, out3]):
        z = (plane + d) % 4
        there = all_ref[pl.ds(4 * z, 4)].reshape(4 * user_rows, TOTAL).astype(f32)
        there = there - placing(slots_ref, 4 * user_rows * z, 4 * user_rows)
        held_ref[d] = dot_t(half, there.astype(bf16)).astype(bf16)
        copy = pltpu.make_async_copy(held_ref.at[d], out, sems.at[d])
        copy.start()
        copies.append(copy)
    for copy in copies:
        copy.wait()


def make_update(where, weighted, whole, pivots, weighted_all, slot_plane):
    user_rows = weighted.shape[0]
    return pl.pallas_call(
        update_kernel,
        out_shape=(jax.ShapeDtypeStruct((user_rows, 4 * user_rows), bf16),) * 4,
        in_specs=[SMEM] + [VMEM] * 5,
        out_specs=(HBM,) * 4,
        scratch_shapes=[
            pltpu.VMEM((TOTAL, TOTAL), f32),
            pltpu.VMEM((4, user_rows, 4 * user_rows), bf16),
            pltpu.SemaphoreType.DMA((4,)),
        ],
        compiler_params=params(),
        cost_estimate=cost(1_500_000_000, 8_000_000),
        name="update",
    )(where, weighted, whole, pivots, weighted_all, slot_plane)


def local(channels, inverse, arrivals, arrival_cell, cell_owner, slots, symbols):
    group_count, user_rows, antennas = channels.shape
    user_cols = inverse.shape[2]
    capacity = arrivals.shape[2]
    cell_count = cell_owner.shape[0]
    grp_index = lax.axis_index("grp")
    row_index = lax.axis_index("row")
    col_index = lax.axis_index("col")
    y_index, x_index = row_index // 4, row_index % 4

    def along_x(value, step):
        pairs = [(4 * y + x, 4 * y + (x + step) % 4) for y in range(4) for x in range(4)]
        return lax.ppermute(value, "row", pairs)

    def along_y(value, step):
        pairs = [(4 * y + x, 4 * ((y + step) % 4) + x) for y in range(4) for x in range(4)]
        return lax.ppermute(value, "row", pairs)

    def along_z(value, step):
        return lax.ppermute(value, "col", [(z, (z + step) % 4) for z in range(4)])

    def to_planes(value):
        padded = jnp.concatenate([value, jnp.zeros_like(value[:1])], axis=0)
        return lax.all_to_all(padded, "col", 0, 0, tiled=True)

    first_group = grp_index * group_count
    other_first = (1 - grp_index) * group_count
    first_row = row_index * user_rows
    first_arg = first_row.reshape(1)

    with jax.named_scope("newcomers"):
        mine = lax.dynamic_slice_in_dim(arrivals, first_group, group_count, 0)
        theirs = lax.dynamic_slice_in_dim(arrivals, other_first, group_count, 0)
        swapped = lax.ppermute(theirs, "grp", [(0, 1), (1, 0)])
        from_0 = jnp.where(grp_index == 0, mine, swapped)
        from_1 = jnp.where(grp_index == 0, swapped, mine)
        chunk = jnp.stack([from_0, from_1], axis=2)
        per_group = EPOCHS * 2 * capacity
        chunk = chunk.reshape(group_count * per_group, antennas)
        chunk = jnp.pad(chunk, ((0, 112 - group_count * per_group), (0, 0)))
        gathered = lax.all_gather(chunk, "row")

    with jax.named_scope("planes"):
        pieces = list(make_pieces(x_index.reshape(1), inverse))
        for d in (1, 2, 3):
            pieces[d] = along_x(pieces[d], d)
        square = to_planes(jnp.stack(pieces, axis=1))
        symbol_part = jnp.einsum(
            "grc,gcs->grs", inverse, symbols.astype(f32), precision=highest
        )
        precoded = jnp.sum(to_planes(symbol_part), axis=0)

    plane_group = first_group + jnp.minimum(col_index, group_count - 1)
    slot_plane = lax.dynamic_slice_in_dim(slots, plane_group, 1, 0).reshape(1, TOTAL)
    row_ids = first_row + jnp.arange(user_rows, dtype=jnp.int32)

    cells_mine = lax.dynamic_slice_in_dim(arrival_cell, first_group, group_count, 0)[..., 0]
    slots_mine = lax.dynamic_slice_in_dim(slots, first_group, group_count, 0)
    slots_mine = slots_mine.reshape(group_count, 1, TOTAL)
    cell_table = (cells_mine[..., None] == jnp.arange(cell_count, dtype=jnp.int32)).astype(
        jnp.int32
    )
    owners = jnp.sum(cell_table * cell_owner, axis=-1)
    arrival_order = jnp.arange(ARRIVE, dtype=jnp.int32)
    earlier = (cells_mine[..., :, None] == cells_mine[..., None, :]) & (
        arrival_order[:, None] < arrival_order[None, :]
    )
    ranking = jnp.sum(earlier.astype(jnp.int32), axis=-2)
    with jax.named_scope("places"):
        offset = jnp.arange(group_count, dtype=jnp.int32) * per_group % 16
        epoch = jnp.arange(EPOCHS, dtype=jnp.int32)
        inside = offset[:, None] + epoch[None, :] * 2 * capacity
        inside = inside[:, :, None] + owners // 16 * capacity + ranking
        place = (owners % 16 * WINDOW + inside).reshape(group_count, 1, TOTAL)
        plane_place = lax.dynamic_slice_in_dim(
            place, jnp.minimum(col_index, group_count - 1), 1, 0
        ).reshape(1, TOTAL)

    with jax.named_scope("columns"):
        gathered, square, precoded = lax.optimization_barrier((gathered, square, precoded))
        both = make_columns(row_index.reshape(1), gathered, channels, place)
        both = lax.all_to_all(both, "col", 0, 0, tiled=True)
        summed = jnp.sum(both.astype(f32), axis=0)
        columns = summed[:user_rows]
        gram = summed[user_rows:]
        own = columns.astype(bf16)
        by_row = [own] + [along_x(own, d) for d in (1, 2, 3)]
        by_col = [own] + [along_y(own, -d) for d in (1, 2, 3)]

    with jax.named_scope("schur"):
        where = jnp.stack([y_index, row_index, first_row])
        block0, block1, block2, block3, packed = make_middle(
            where, square, by_row, by_col, columns, precoded, slot_plane, gram, plane_place
        )
        weighted = block0
        for d, block in ((1, block1), (2, block2), (3, block3)):
            weighted = weighted + along_x(block, -d).astype(f32)
        weighted_all = lax.all_gather(weighted.astype(bf16), "row")
        packed = packed.reshape(16, SHARE, TOTAL + STREAMS)
        shared = lax.all_to_all(packed, "row", 0, 0, tiled=True)
        shared = jnp.sum(shared.astype(f32), axis=0)
        share_ids = row_index * SHARE + jnp.arange(SHARE, dtype=jnp.int32)
        identity = loading * (
            share_ids[:, None] == jnp.arange(TOTAL, dtype=jnp.int32)[None, :]
        ).astype(f32)
        schur_rows = identity - shared[:, :TOTAL]
        ready = jnp.concatenate([schur_rows, shared[:, TOTAL:]], axis=1)
        ready = jnp.broadcast_to(ready[None], (16, SHARE, TOTAL + STREAMS))
        whole = lax.all_to_all(ready, "row", 0, 0, tiled=True).reshape(TOTAL, TOTAL + STREAMS)

    with jax.named_scope("users"):
        channel = make_channel(first_arg, gathered, channels, place, slots_mine)
        whole, channel = lax.optimization_barrier((whole, channel))
        pivots, users = make_solve(first_arg, whole, weighted, precoded, slot_plane)
        users_side = lax.all_to_all(users, "col", 0, 0, tiled=True)

    with jax.named_scope("update"):
        changes = make_update(
            jnp.stack([first_row, col_index]), weighted, whole, pivots, weighted_all, slot_plane
        )
        changes = [changes[0]] + [along_z(changes[d], d) for d in (1, 2, 3)]

    with jax.named_scope("signal"):
        signal_part = make_signal(users_side, channel)
        received = lax.all_to_all(signal_part, "row", 0, 0, tiled=True)
        received, changes = lax.optimization_barrier((received, changes))
        signal, power = make_total(received)
        power = lax.all_to_all(power, ("row", "col"), 0, 0, tiled=True)
        total_power = jnp.sum(power, axis=(0, 1))[:group_count] / (STREAMS * ANTENNAS)
        transmit = signal * lax.rsqrt(total_power + epsilon)[:, None, None]
        transmit = jnp.swapaxes(transmit, 0, 1)

    with jax.named_scope("final"):
        col_ids = col_index * user_cols + jnp.arange(user_cols, dtype=jnp.int32)
        diagonal = row_ids[:, None] == col_ids[None, :]
        full = jnp.any(slots_mine == row_ids[None, :, None], axis=2)
        gone = jnp.where(diagonal[None] & full[:, :, None], 1.0 / loading, 0.0)
        updated = []
        for g in range(group_count):
            step = (col_index - g) % 4
            add = changes[0]
            for d in (1, 2, 3):
                add = jnp.where(step == d, changes[d], add)
            updated.append(inverse[g] - gone[g] + add.astype(f32))
        updated = jnp.stack(updated, axis=0)
    return (updated, transmit)


def solution(mesh):
    placed = (
        P("grp", "row", "col"),
        P("grp", "row", "col"),
        P(None, None, ("grp", "row"), "col"),
        P(),
        P(),
        P(),
        P("grp", "col", None),
    )
    return jax.shard_map(
        local,
        mesh=mesh,
        in_specs=placed,
        out_specs=(P("grp", "row", "col"), P("row", "grp", "col")),
        check_vma=False,
    )
```

```python
import jax
import jax.numpy as jnp
from jax import lax
from jax.experimental import pallas as pl
from jax.experimental.pallas import tpu as pltpu
from jax.sharding import PartitionSpec as P

ANTENNAS = 8192
ARRIVE = 128
EPOCHS = 3
STREAMS = 256
TOTAL = ARRIVE * EPOCHS
BLOCK = 128
PANEL = 8
WINDOW = 48
SHARE = TOTAL // 16

loading = 1.0
epsilon = 1e-06
highest = lax.Precision.HIGHEST
f32 = jnp.float32
bf16 = jnp.bfloat16
VMEM = pl.BlockSpec(memory_space=pltpu.VMEM)
SMEM = pl.BlockSpec(memory_space=pltpu.SMEM)
HBM = pl.BlockSpec(memory_space=pltpu.HBM)


def params(mib=40):
    return pltpu.CompilerParams(vmem_limit_bytes=mib * 1024 * 1024)


def cost(flops, nbytes):
    return pl.CostEstimate(flops=flops, bytes_accessed=nbytes, transcendentals=0)


def dot(a, b):
    return jnp.dot(a, b, preferred_element_type=f32)


def dot_t(a, b):
    return lax.dot_general(a, b, (((1,), (1,)), ((), ())), preferred_element_type=f32)


def t_dot(a, b):
    return lax.dot_general(a, b, (((0,), (0,)), ((), ())), preferred_element_type=f32)


def halves(a):
    high = a.astype(bf16)
    return high, (a - high.astype(f32)).astype(bf16)


def split(product, a, b):
    a_high, a_low = halves(a)
    b_high, b_low = halves(b)
    return product(a_high, b_low) + product(a_low, b_high) + product(a_high, b_high)


def placing(slots_ref, first, rows):
    ids = first + lax.broadcasted_iota(jnp.int32, (rows, TOTAL), 0)
    return (ids == slots_ref[...].reshape(1, TOTAL)).astype(f32)


def choosing(place_ref, g):
    ids = lax.broadcasted_iota(jnp.int32, (16 * WINDOW, TOTAL), 0)
    return (ids == place_ref[g]).astype(f32).astype(bf16)


def start_inputs(gathered_ref, channel_ref, window_ref, held_ref, sems, row=None):
    groups, user_rows = channel_ref.shape[:2]
    copies = []
    for g in range(groups):
        start = g * 2 * EPOCHS * 6 // 16 * 16
        source = gathered_ref.at[:, pl.ds(start, WINDOW), :]
        parts = [
            pltpu.make_async_copy(channel_ref.at[g], held_ref.at[g, :user_rows], sems.at[0, g]),
            pltpu.make_async_copy(source, window_ref.at[g], sems.at[1, g]),
        ]
        if row is not None:
            source = gathered_ref.at[row, pl.ds(start, WINDOW), :]
            parts.append(
                pltpu.make_async_copy(source, held_ref.at[g, user_rows:], sems.at[2, g])
            )
        for part in parts:
            part.start()
        copies.append(parts)
    return copies


def input_scratch(groups, rows, antennas):
    return [
        pltpu.VMEM((groups, 16, WINDOW, antennas), bf16),
        pltpu.VMEM((groups, rows, antennas), bf16),
        pltpu.SemaphoreType.DMA((3, groups)),
    ]


def columns_kernel(
    row_ref, gathered_ref, channel_ref, place_ref, out_ref, window_ref, held_ref, sems
):
    groups, _, antennas = channel_ref.shape
    copies = start_inputs(gathered_ref, channel_ref, window_ref, held_ref, sems, row_ref[0])
    out_ref[groups] = jnp.zeros(out_ref.shape[1:], bf16)
    for g in range(groups):
        choose = choosing(place_ref, g)
        for copy in copies[g]:
            copy.wait()
        window = window_ref[g].reshape(16 * WINDOW, antennas)
        wide = dot_t(held_ref[g], window).astype(bf16)
        out_ref[g] = dot(wide, choose).astype(bf16)


def make_columns(row, gathered, channels, place):
    groups, user_rows, antennas = channels.shape
    return pl.pallas_call(
        columns_kernel,
        out_shape=jax.ShapeDtypeStruct((groups + 1, user_rows + WINDOW, TOTAL), bf16),
        in_specs=[SMEM, HBM, HBM, VMEM],
        out_specs=VMEM,
        scratch_shapes=input_scratch(groups, user_rows + WINDOW, antennas),
        compiler_params=params(60),
        cost_estimate=cost(4_000_000_000, 12_000_000),
        name="columns",
    )(row, gathered, channels, place)


def channel_kernel(
    first_ref, gathered_ref, channel_ref, place_ref, slots_ref, out_ref, window_ref, held_ref, sems
):
    groups, user_rows, antennas = channel_ref.shape
    copies = start_inputs(gathered_ref, channel_ref, window_ref, held_ref, sems)
    for g in range(groups):
        here = placing(slots_ref.at[g], first_ref[0], user_rows).astype(bf16)
        route = dot_t(here, choosing(place_ref, g)).astype(bf16)
        for copy in copies[g]:
            copy.wait()
        window = window_ref[g].reshape(16 * WINDOW, antennas)
        out_ref[g] = held_ref[g] + dot(route, window).astype(bf16)


def make_channel(first, gathered, channels, place, slots_mine):
    groups, user_rows, antennas = channels.shape
    return pl.pallas_call(
        channel_kernel,
        out_shape=jax.ShapeDtypeStruct(channels.shape, bf16),
        in_specs=[SMEM, HBM, HBM, VMEM, VMEM],
        out_specs=VMEM,
        scratch_shapes=input_scratch(groups, user_rows, antennas),
        compiler_params=params(60),
        cost_estimate=cost(4_000_000_000, 14_000_000),
        name="channel",
    )(first, gathered, channels, place, slots_mine)


def pieces_kernel(x_ref, inverse_ref, out0, out1, out2, out3):
    size = out0.shape[-1]
    for d, out in enumerate([out0, out1, out2, out3]):
        start = pl.multiple_of((x_ref[0] + d) % 4 * size, size)
        out[...] = inverse_ref[:, :, pl.ds(start, size)].astype(bf16)


def make_pieces(x, inverse):
    groups, user_rows = inverse.shape[:2]
    shape = jax.ShapeDtypeStruct((groups, user_rows, user_rows), bf16)
    return pl.pallas_call(
        pieces_kernel,
        out_shape=(shape,) * 4,
        in_specs=[SMEM, VMEM],
        out_specs=(VMEM,) * 4,
        compiler_params=params(16),
        cost_estimate=cost(100_000_000, 5_000_000),
        name="pieces",
    )(x, inverse)


def target_kernel(where_ref, summed_ref, precoded_ref, slots_ref, place_ref, base_out):
    row, first = where_ref[1], where_ref[2]
    user_rows = precoded_ref.shape[0]
    ids = row * WINDOW + lax.broadcasted_iota(jnp.int32, (WINDOW, TOTAL), 0)
    choose = (ids == place_ref[...]).astype(f32).astype(bf16)
    base_out[:, :TOTAL] = -t_dot(choose, summed_ref[user_rows:].astype(bf16))
    border = summed_ref[:user_rows] - placing(slots_ref, first, user_rows)
    base_out[:, TOTAL:] = split(t_dot, border, precoded_ref[...])


def make_target(where, summed, precoded, slot_plane, place_plane):
    return pl.pallas_call(
        target_kernel,
        out_shape=jax.ShapeDtypeStruct((TOTAL, TOTAL + STREAMS), f32),
        in_specs=[SMEM] + [VMEM] * 4,
        out_specs=VMEM,
        compiler_params=params(16),
        cost_estimate=cost(1_000_000_000, 2_000_000),
        name="target",
    )(where, summed, precoded, slot_plane, place_plane)


def middle_kernel(
    where_ref, square_ref, own_ref, row1_ref, row2_ref, row3_ref, col1_ref, col2_ref, col3_ref,
    base_ref, first_out, block1_out, block2_out, block3_out, packed_out,
):
    y = where_ref[0]
    by_row = [own_ref, row1_ref, row2_ref, row3_ref]
    by_col = [own_ref, col1_ref, col2_ref, col3_ref]
    outs = [first_out, block1_out, block2_out, block3_out]
    schur = base_ref[:, :TOTAL]
    for d in range(4):
        block = dot(square_ref[y, d], own_ref[...])
        for e in range(1, 4):
            block += dot(square_ref[(y + e) % 4, d], by_col[e][...])
        low = block.astype(bf16)
        outs[d][...] = block if d == 0 else low
        schur += t_dot(by_row[d][...], low)
    packed_out[:, :TOTAL] = schur.astype(bf16)
    packed_out[:, TOTAL:] = base_ref[:, TOTAL:].astype(bf16)


def make_middle(where, square, by_row, by_col, base):
    shape = by_row[0].shape
    return pl.pallas_call(
        middle_kernel,
        out_shape=(
            jax.ShapeDtypeStruct(shape, f32),
            jax.ShapeDtypeStruct(shape, bf16),
            jax.ShapeDtypeStruct(shape, bf16),
            jax.ShapeDtypeStruct(shape, bf16),
            jax.ShapeDtypeStruct((TOTAL, TOTAL + STREAMS), bf16),
        ),
        in_specs=[SMEM] + [VMEM] * 9,
        out_specs=(VMEM,) * 5,
        compiler_params=params(),
        cost_estimate=cost(2_000_000_000, 8_000_000),
        name="middle",
    )(where, square, *by_row, *by_col[1:], base)


def invert_block(a):
    lane = lax.broadcasted_iota(jnp.int32, (1, BLOCK), 1)
    sub = lax.broadcasted_iota(jnp.int32, (PANEL, 1), 0)
    for k in range(0, BLOCK, PANEL):
        inside = (lane >= k) & (lane < k + PANEL)
        rows = a[k:k + PANEL, :]
        cols = [
            jnp.broadcast_to(rows[:, k + j:k + j + 1], (PANEL, BLOCK)) for j in range(PANEL)
        ]
        rows = jnp.where(inside, (lane - k == sub).astype(f32), rows)
        for i in range(PANEL):
            scale = 1.0 / cols[i][i:i + 1, :]
            factor = cols[i] - (sub == i).astype(f32)
            for j in range(i + 1, PANEL):
                cols[j] = cols[j] - factor * (cols[j][i:i + 1, :] * scale)
            rows = rows - factor * (rows[i:i + 1, :] * scale)
        rest = jnp.where(inside, 0.0, a)
        for i in range(PANEL):
            rest = rest - a[:, k + i:k + i + 1] * rows[i:i + 1, :]
        pieces = [rest[:k]] if k else []
        pieces.append(rows)
        if k + PANEL < BLOCK:
            pieces.append(rest[k + PANEL:])
        a = jnp.concatenate(pieces, axis=0)
    return a


def solve_kernel(
    first_ref, whole_ref, weighted_ref, precoded_ref, slots_ref, pivots_ref, users_ref, work_ref
):
    work_ref[...] = whole_ref[...]

    @pl.loop(0, EPOCHS)
    def _(b):
        start = pl.ds(pl.multiple_of(b * BLOCK, BLOCK), BLOCK)
        pivots_ref[b] = invert_block(work_ref[start, start])
        for k in range(EPOCHS):
            here = slice(k * BLOCK, (k + 1) * BLOCK)

            @pl.when(b == k)
            def _():
                scaled = split(dot, pivots_ref[k], work_ref[here, here.stop:])
                work_ref[here, here.stop:] = scaled
                if k + 1 < EPOCHS:
                    below = work_ref[here.stop:, here]
                    work_ref[here.stop:, here.stop:] -= split(dot, below, scaled)

    effect = work_ref[TOTAL - BLOCK:, TOTAL:]
    for b in range(EPOCHS - 2, -1, -1):
        here = slice(b * BLOCK, (b + 1) * BLOCK)
        part = work_ref[here, TOTAL:] - split(dot, work_ref[here, here.stop:TOTAL], effect)
        effect = jnp.concatenate([part, effect], axis=0)
    place = placing(slots_ref, first_ref[0], weighted_ref.shape[0])
    kept = 1.0 - jnp.sum(place, axis=1, keepdims=True)
    users = precoded_ref[...] * kept + split(dot, weighted_ref[...] - place, effect)
    for z in range(4):
        users_ref[z] = users.astype(bf16)


def make_solve(first, whole, weighted, precoded, slot_plane):
    return pl.pallas_call(
        solve_kernel,
        out_shape=(
            jax.ShapeDtypeStruct((EPOCHS, BLOCK, BLOCK), f32),
            jax.ShapeDtypeStruct((4, weighted.shape[0], STREAMS), bf16),
        ),
        in_specs=[SMEM] + [VMEM] * 4,
        out_specs=(VMEM,) * 2,
        scratch_shapes=[pltpu.VMEM(whole.shape, f32)],
        compiler_params=params(),
        cost_estimate=cost(14_000_000_000, 4_000_000),
        name="solve",
    )(first, whole, weighted, precoded, slot_plane)


def inverse_of(whole_ref, pivots_ref, inv_ref):
    inv_ref[...] = whole_ref[:, :TOTAL]
    row_id = lax.broadcasted_iota(jnp.int32, (TOTAL, BLOCK), 0)
    lane_id = lax.broadcasted_iota(jnp.int32, (TOTAL, BLOCK), 1)
    for b in range(EPOCHS):
        here = slice(b * BLOCK, (b + 1) * BLOCK)
        inside = (row_id >= here.start) & (row_id < here.stop)
        rest = jnp.where(inside, 0.0, inv_ref[:, here])
        inv_ref[:, here] = (row_id == lane_id + here.start).astype(f32)
        scaled = split(dot, pivots_ref[b], inv_ref[here, :])
        inv_ref[here, :] = jnp.zeros((BLOCK, TOTAL), f32)
        inv_ref[...] = inv_ref[...] - split(dot, rest, scaled)
        inv_ref[here, :] = scaled


def signal_kernel(users_ref, channel_ref, out_ref, held_ref, sems):
    groups, _, antennas = channel_ref.shape
    tile = antennas // 2
    copies = []
    for g in range(groups):
        for m in range(0, antennas, tile):
            part = t_dot(users_ref[g], channel_ref[g, :, m:m + tile]).astype(bf16)
            held_ref[g, :, :, m:m + tile] = part.reshape(16, STREAMS // 16, tile)
        copy = pltpu.make_async_copy(held_ref.at[g], out_ref.at[:, g], sems.at[g])
        copy.start()
        copies.append(copy)
    for copy in copies:
        copy.wait()


def make_signal(users_side, channel):
    groups, _, antennas = channel.shape
    each = STREAMS // 16
    return pl.pallas_call(
        signal_kernel,
        out_shape=jax.ShapeDtypeStruct((16, groups, each, antennas), bf16),
        in_specs=[VMEM, VMEM],
        out_specs=HBM,
        scratch_shapes=[
            pltpu.VMEM((groups, 16, each, antennas), bf16),
            pltpu.SemaphoreType.DMA((groups,)),
        ],
        compiler_params=params(),
        cost_estimate=cost(800_000_000, 7_000_000),
        name="signal",
    )(users_side, channel)


def total_kernel(received_ref, signal_ref, power_ref, sums_ref):
    g = pl.program_id(0)
    signal = jnp.sum(received_ref[:, 0].astype(f32), axis=0)
    signal_ref[0] = signal
    power = jnp.sum(signal * signal)
    lane = lax.broadcasted_iota(jnp.int32, sums_ref.shape, 1)

    @pl.when(g == 0)
    def _():
        sums_ref[...] = jnp.zeros(sums_ref.shape, f32)

    sums_ref[...] = jnp.where(lane == g, power, sums_ref[...])

    @pl.when(g == pl.num_programs(0) - 1)
    def _():
        power_ref[...] = jnp.broadcast_to(sums_ref[...][None], power_ref.shape)


def make_total(received):
    sources, groups, each, antennas = received.shape
    return pl.pallas_call(
        total_kernel,
        out_shape=(
            jax.ShapeDtypeStruct((groups, each, antennas), f32),
            jax.ShapeDtypeStruct((64, 1, 128), f32),
        ),
        grid=(groups,),
        in_specs=[pl.BlockSpec((sources, 1, each, antennas), lambda g: (0, g, 0, 0))],
        out_specs=(
            pl.BlockSpec((1, each, antennas), lambda g: (g, 0, 0)),
            pl.BlockSpec((64, 1, 128), lambda g: (0, 0, 0)),
        ),
        scratch_shapes=[pltpu.VMEM((1, 128), f32)],
        compiler_params=params(),
        cost_estimate=cost(2_000_000_000, 4_000_000),
        name="total",
    )(received)


def update_kernel(
    where_ref, weighted_ref, whole_ref, pivots_ref, all_ref, slots_ref,
    out0, out1, out2, out3, inv_ref, held_ref, sems,
):
    first, plane = where_ref[0], where_ref[1]
    user_rows = weighted_ref.shape[0]
    inverse_of(whole_ref, pivots_ref, inv_ref)
    border = weighted_ref[...] - placing(slots_ref, first, user_rows)
    half = split(dot, border, inv_ref[...]).astype(bf16)
    copies = []
    for d, out in enumerate([out0, out1, out2, out3]):
        z = (plane + d) % 4
        there = all_ref[pl.ds(4 * z, 4)].reshape(4 * user_rows, TOTAL).astype(f32)
        there = there - placing(slots_ref, 4 * user_rows * z, 4 * user_rows)
        held_ref[d] = dot_t(half, there.astype(bf16)).astype(bf16)
        copy = pltpu.make_async_copy(held_ref.at[d], out, sems.at[d])
        copy.start()
        copies.append(copy)
    for copy in copies:
        copy.wait()


def make_update(where, weighted, whole, pivots, weighted_all, slot_plane):
    user_rows = weighted.shape[0]
    return pl.pallas_call(
        update_kernel,
        out_shape=(jax.ShapeDtypeStruct((user_rows, 4 * user_rows), bf16),) * 4,
        in_specs=[SMEM] + [VMEM] * 5,
        out_specs=(HBM,) * 4,
        scratch_shapes=[
            pltpu.VMEM((TOTAL, TOTAL), f32),
            pltpu.VMEM((4, user_rows, 4 * user_rows), bf16),
            pltpu.SemaphoreType.DMA((4,)),
        ],
        compiler_params=params(),
        cost_estimate=cost(1_500_000_000, 8_000_000),
        name="update",
    )(where, weighted, whole, pivots, weighted_all, slot_plane)


def local(channels, inverse, arrivals, arrival_cell, cell_owner, slots, symbols):
    group_count, user_rows, antennas = channels.shape
    user_cols = inverse.shape[2]
    capacity = arrivals.shape[2]
    cell_count = cell_owner.shape[0]
    grp_index = lax.axis_index("grp")
    row_index = lax.axis_index("row")
    col_index = lax.axis_index("col")
    y_index, x_index = row_index // 4, row_index % 4

    def along_x(value, step):
        pairs = [(4 * y + x, 4 * y + (x + step) % 4) for y in range(4) for x in range(4)]
        return lax.ppermute(value, "row", pairs)

    def along_y(value, step):
        pairs = [(4 * y + x, 4 * ((y + step) % 4) + x) for y in range(4) for x in range(4)]
        return lax.ppermute(value, "row", pairs)

    def along_z(value, step):
        return lax.ppermute(value, "col", [(z, (z + step) % 4) for z in range(4)])

    def to_planes(value):
        padded = jnp.concatenate([value, jnp.zeros_like(value[:1])], axis=0)
        return lax.all_to_all(padded, "col", 0, 0, tiled=True)

    first_group = grp_index * group_count
    other_first = (1 - grp_index) * group_count
    first_row = row_index * user_rows
    first_arg = first_row.reshape(1)

    with jax.named_scope("newcomers"):
        mine = lax.dynamic_slice_in_dim(arrivals, first_group, group_count, 0)
        theirs = lax.dynamic_slice_in_dim(arrivals, other_first, group_count, 0)
        swapped = lax.ppermute(theirs, "grp", [(0, 1), (1, 0)])
        from_0 = jnp.where(grp_index == 0, mine, swapped)
        from_1 = jnp.where(grp_index == 0, swapped, mine)
        chunk = jnp.stack([from_0, from_1], axis=2)
        per_group = EPOCHS * 2 * capacity
        chunk = chunk.reshape(group_count * per_group, antennas)
        chunk = jnp.pad(chunk, ((0, 112 - group_count * per_group), (0, 0)))
        gathered = lax.all_gather(chunk, "row")

    with jax.named_scope("planes"):
        pieces = list(make_pieces(x_index.reshape(1), inverse))
        for d in (1, 2, 3):
            pieces[d] = along_x(pieces[d], d)
        square = to_planes(jnp.stack(pieces, axis=1))
        symbol_part = jnp.einsum(
            "grc,gcs->grs", inverse, symbols.astype(f32), precision=highest
        )
        precoded = jnp.sum(to_planes(symbol_part), axis=0)

    plane_group = first_group + jnp.minimum(col_index, group_count - 1)
    slot_plane = lax.dynamic_slice_in_dim(slots, plane_group, 1, 0).reshape(1, TOTAL)
    row_ids = first_row + jnp.arange(user_rows, dtype=jnp.int32)

    cells_mine = lax.dynamic_slice_in_dim(arrival_cell, first_group, group_count, 0)[..., 0]
    slots_mine = lax.dynamic_slice_in_dim(slots, first_group, group_count, 0)
    slots_mine = slots_mine.reshape(group_count, 1, TOTAL)
    cell_table = (cells_mine[..., None] == jnp.arange(cell_count, dtype=jnp.int32)).astype(
        jnp.int32
    )
    owners = jnp.sum(cell_table * cell_owner, axis=-1)
    arrival_order = jnp.arange(ARRIVE, dtype=jnp.int32)
    earlier = (cells_mine[..., :, None] == cells_mine[..., None, :]) & (
        arrival_order[:, None] < arrival_order[None, :]
    )
    ranking = jnp.sum(earlier.astype(jnp.int32), axis=-2)
    with jax.named_scope("places"):
        offset = jnp.arange(group_count, dtype=jnp.int32) * per_group % 16
        epoch = jnp.arange(EPOCHS, dtype=jnp.int32)
        inside = offset[:, None] + epoch[None, :] * 2 * capacity
        inside = inside[:, :, None] + owners // 16 * capacity + ranking
        place = (owners % 16 * WINDOW + inside).reshape(group_count, 1, TOTAL)
        plane_place = lax.dynamic_slice_in_dim(
            place, jnp.minimum(col_index, group_count - 1), 1, 0
        ).reshape(1, TOTAL)

    with jax.named_scope("columns"):
        gathered, square, precoded = lax.optimization_barrier((gathered, square, precoded))
        both = make_columns(row_index.reshape(1), gathered, channels, place)
        both = lax.all_to_all(both, "col", 0, 0, tiled=True)
        summed = jnp.sum(both.astype(f32), axis=0)
        own = summed[:user_rows].astype(bf16)
        by_row = [own] + [along_x(own, d) for d in (1, 2, 3)]
        by_col = [own] + [along_y(own, -d) for d in (1, 2, 3)]

    with jax.named_scope("schur"):
        where = jnp.stack([y_index, row_index, first_row])
        base = make_target(where, summed, precoded, slot_plane, plane_place)
        block0, block1, block2, block3, packed = make_middle(where, square, by_row, by_col, base)
        weighted = block0
        for d, block in ((1, block1), (2, block2), (3, block3)):
            weighted = weighted + along_x(block, -d).astype(f32)
        weighted_all = lax.all_gather(weighted.astype(bf16), "row")
        packed = packed.reshape(16, SHARE, TOTAL + STREAMS)
        shared = lax.all_to_all(packed, "row", 0, 0, tiled=True)
        shared = jnp.sum(shared.astype(f32), axis=0)
        share_ids = row_index * SHARE + jnp.arange(SHARE, dtype=jnp.int32)
        identity = loading * (
            share_ids[:, None] == jnp.arange(TOTAL, dtype=jnp.int32)[None, :]
        ).astype(f32)
        schur_rows = identity - shared[:, :TOTAL]
        ready = jnp.concatenate([schur_rows, shared[:, TOTAL:]], axis=1)
        ready = jnp.broadcast_to(ready[None], (16, SHARE, TOTAL + STREAMS))
        whole = lax.all_to_all(ready, "row", 0, 0, tiled=True).reshape(TOTAL, TOTAL + STREAMS)

    with jax.named_scope("users"):
        channel = make_channel(first_arg, gathered, channels, place, slots_mine)
        whole, channel = lax.optimization_barrier((whole, channel))
        pivots, users = make_solve(first_arg, whole, weighted, precoded, slot_plane)
        users_side = lax.all_to_all(users, "col", 0, 0, tiled=True)

    with jax.named_scope("update"):
        changes = make_update(
            jnp.stack([first_row, col_index]), weighted, whole, pivots, weighted_all, slot_plane
        )
        changes = [changes[0]] + [along_z(changes[d], d) for d in (1, 2, 3)]

    with jax.named_scope("signal"):
        signal_part = make_signal(users_side, channel)
        received = lax.all_to_all(signal_part, "row", 0, 0, tiled=True)
        received, changes = lax.optimization_barrier((received, changes))
        signal, power = make_total(received)
        power = lax.all_to_all(power, ("row", "col"), 0, 0, tiled=True)
        total_power = jnp.sum(power, axis=(0, 1))[:group_count] / (STREAMS * ANTENNAS)
        transmit = signal * lax.rsqrt(total_power + epsilon)[:, None, None]
        transmit = jnp.swapaxes(transmit, 0, 1)

    with jax.named_scope("final"):
        col_ids = col_index * user_cols + jnp.arange(user_cols, dtype=jnp.int32)
        diagonal = row_ids[:, None] == col_ids[None, :]
        full = jnp.any(slots_mine == row_ids[None, :, None], axis=2)
        gone = jnp.where(diagonal[None] & full[:, :, None], 1.0 / loading, 0.0)
        updated = []
        for g in range(group_count):
            step = (col_index - g) % 4
            add = changes[0]
            for d in (1, 2, 3):
                add = jnp.where(step == d, changes[d], add)
            updated.append(inverse[g] - gone[g] + add.astype(f32))
        updated = jnp.stack(updated, axis=0)
    return (updated, transmit)


def solution(mesh):
    placed = (
        P("grp", "row", "col"),
        P("grp", "row", "col"),
        P(None, None, ("grp", "row"), "col"),
        P(),
        P(),
        P(),
        P("grp", "col", None),
    )
    return jax.shard_map(
        local,
        mesh=mesh,
        in_specs=placed,
        out_specs=(P("grp", "row", "col"), P("row", "grp", "col")),
        check_vma=False,
    )
```

```python
import jax
import jax.numpy as jnp
from jax import lax
from jax.experimental import pallas as pl
from jax.experimental.pallas import tpu as pltpu
from jax.sharding import PartitionSpec as P

ANTENNAS = 8192
ARRIVE = 128
EPOCHS = 3
STREAMS = 256
TOTAL = ARRIVE * EPOCHS
BLOCK = 128
PANEL = 8
WINDOW = 48
SHARE = TOTAL // 16

loading = 1.0
epsilon = 1e-06
highest = lax.Precision.HIGHEST
f32 = jnp.float32
bf16 = jnp.bfloat16
VMEM = pl.BlockSpec(memory_space=pltpu.VMEM)
SMEM = pl.BlockSpec(memory_space=pltpu.SMEM)
HBM = pl.BlockSpec(memory_space=pltpu.HBM)


def params(mib=40):
    return pltpu.CompilerParams(vmem_limit_bytes=mib * 1024 * 1024)


def cost(flops, nbytes):
    return pl.CostEstimate(flops=flops, bytes_accessed=nbytes, transcendentals=0)


def dot(a, b):
    return jnp.dot(a, b, preferred_element_type=f32)


def dot_t(a, b):
    return lax.dot_general(a, b, (((1,), (1,)), ((), ())), preferred_element_type=f32)


def t_dot(a, b):
    return lax.dot_general(a, b, (((0,), (0,)), ((), ())), preferred_element_type=f32)


def halves(a):
    high = a.astype(bf16)
    return high, (a - high.astype(f32)).astype(bf16)


def split(product, a, b):
    a_high, a_low = halves(a)
    b_high, b_low = halves(b)
    return product(a_high, b_low) + product(a_low, b_high) + product(a_high, b_high)


def placing(slots_ref, first, rows):
    ids = first + lax.broadcasted_iota(jnp.int32, (rows, TOTAL), 0)
    return (ids == slots_ref[...].reshape(1, TOTAL)).astype(f32)


def choosing(place_ref, g):
    ids = lax.broadcasted_iota(jnp.int32, (16 * WINDOW, TOTAL), 0)
    return (ids == place_ref[g]).astype(f32).astype(bf16)


def start_inputs(gathered_ref, channel_ref, window_ref, held_ref, sems):
    groups, user_rows = channel_ref.shape[:2]
    copies = []
    for g in range(groups):
        start = g * 2 * EPOCHS * 6 // 16 * 16
        source = gathered_ref.at[:, pl.ds(start, WINDOW), :]
        parts = [
            pltpu.make_async_copy(channel_ref.at[g], held_ref.at[g, :user_rows], sems.at[0, g]),
            pltpu.make_async_copy(source, window_ref.at[g], sems.at[1, g]),
        ]
        for part in parts:
            part.start()
        copies.append(parts)
    return copies


def input_scratch(groups, rows, antennas):
    return [
        pltpu.VMEM((groups, 16, WINDOW, antennas), bf16),
        pltpu.VMEM((groups, rows, antennas), bf16),
        pltpu.SemaphoreType.DMA((2, groups)),
    ]


def columns_kernel(
    row_ref, gathered_ref, channel_ref, place_ref, out_ref, window_ref, held_ref, sems
):
    groups, user_rows, antennas = channel_ref.shape
    copies = []
    for g in range(groups):
        start = g * 2 * EPOCHS * 6 // 16 * 16
        copy = pltpu.make_async_copy(
            gathered_ref.at[:, pl.ds(start, WINDOW), :], window_ref.at[g], sems.at[g]
        )
        copy.start()
        copies.append(copy)
    out_ref[groups] = jnp.zeros(out_ref.shape[1:], bf16)
    for g in range(groups):
        held_ref[g, :user_rows] = channel_ref[g]
        choose = choosing(place_ref, g)
        copies[g].wait()
        held_ref[g, user_rows:] = window_ref[g, row_ref[0]]
        window = window_ref[g].reshape(16 * WINDOW, antennas)
        wide = dot_t(held_ref[g], window).astype(bf16)
        out_ref[g] = dot(wide, choose).astype(bf16)


def make_columns(row, gathered, channels, place):
    groups, user_rows, antennas = channels.shape
    return pl.pallas_call(
        columns_kernel,
        out_shape=jax.ShapeDtypeStruct((groups + 1, user_rows + WINDOW, TOTAL), bf16),
        in_specs=[SMEM, HBM, VMEM, VMEM],
        out_specs=VMEM,
        scratch_shapes=[
            pltpu.VMEM((groups, 16, WINDOW, antennas), bf16),
            pltpu.VMEM((groups, user_rows + WINDOW, antennas), bf16),
            pltpu.SemaphoreType.DMA((groups,)),
        ],
        compiler_params=params(54),
        cost_estimate=cost(8_000_000_000, 12_000_000),
        name="columns",
    )(row, gathered, channels, place)


def channel_kernel(
    first_ref, gathered_ref, channel_ref, place_ref, slots_ref, out_ref, window_ref, held_ref, sems
):
    groups, user_rows, antennas = channel_ref.shape
    copies = start_inputs(gathered_ref, channel_ref, window_ref, held_ref, sems)
    for g in range(groups):
        here = placing(slots_ref.at[g], first_ref[0], user_rows).astype(bf16)
        route = dot_t(here, choosing(place_ref, g)).astype(bf16)
        for copy in copies[g]:
            copy.wait()
        window = window_ref[g].reshape(16 * WINDOW, antennas)
        out_ref[g] = held_ref[g] + dot(route, window).astype(bf16)


def make_channel(first, gathered, channels, place, slots_mine):
    groups, user_rows, antennas = channels.shape
    return pl.pallas_call(
        channel_kernel,
        out_shape=jax.ShapeDtypeStruct(channels.shape, bf16),
        in_specs=[SMEM, HBM, HBM, VMEM, VMEM],
        out_specs=VMEM,
        scratch_shapes=input_scratch(groups, user_rows, antennas),
        compiler_params=params(60),
        cost_estimate=cost(4_000_000_000, 14_000_000),
        name="channel",
    )(first, gathered, channels, place, slots_mine)


def pieces_kernel(x_ref, inverse_ref, out0, out1, out2, out3):
    size = out0.shape[-1]
    for d, out in enumerate([out0, out1, out2, out3]):
        start = pl.multiple_of((x_ref[0] + d) % 4 * size, size)
        out[...] = inverse_ref[:, :, pl.ds(start, size)].astype(bf16)


def make_pieces(x, inverse):
    groups, user_rows = inverse.shape[:2]
    shape = jax.ShapeDtypeStruct((groups, user_rows, user_rows), bf16)
    return pl.pallas_call(
        pieces_kernel,
        out_shape=(shape,) * 4,
        in_specs=[SMEM, VMEM],
        out_specs=(VMEM,) * 4,
        compiler_params=params(16),
        cost_estimate=cost(100_000_000, 5_000_000),
        name="pieces",
    )(x, inverse)


def target_kernel(where_ref, summed_ref, precoded_ref, slots_ref, place_ref, base_out):
    row, first = where_ref[1], where_ref[2]
    user_rows = precoded_ref.shape[0]
    ids = row * WINDOW + lax.broadcasted_iota(jnp.int32, (WINDOW, TOTAL), 0)
    choose = (ids == place_ref[...]).astype(f32).astype(bf16)
    base_out[:, :TOTAL] = -t_dot(choose, summed_ref[user_rows:].astype(bf16))
    border = summed_ref[:user_rows] - placing(slots_ref, first, user_rows)
    base_out[:, TOTAL:] = split(t_dot, border, precoded_ref[...])


def make_target(where, summed, precoded, slot_plane, place_plane):
    return pl.pallas_call(
        target_kernel,
        out_shape=jax.ShapeDtypeStruct((TOTAL, TOTAL + STREAMS), f32),
        in_specs=[SMEM] + [VMEM] * 4,
        out_specs=VMEM,
        compiler_params=params(16),
        cost_estimate=cost(1_000_000_000, 2_000_000),
        name="target",
    )(where, summed, precoded, slot_plane, place_plane)


def middle_kernel(
    where_ref, square_ref, own_ref, row1_ref, row2_ref, row3_ref, col1_ref, col2_ref, col3_ref,
    base_ref, first_out, block1_out, block2_out, block3_out, packed_out,
):
    y = where_ref[0]
    by_row = [own_ref, row1_ref, row2_ref, row3_ref]
    by_col = [own_ref, col1_ref, col2_ref, col3_ref]
    outs = [first_out, block1_out, block2_out, block3_out]
    schur = base_ref[:, :TOTAL]
    for d in range(4):
        block = dot(square_ref[y, d], own_ref[...])
        for e in range(1, 4):
            block += dot(square_ref[(y + e) % 4, d], by_col[e][...])
        low = block.astype(bf16)
        outs[d][...] = block if d == 0 else low
        schur += t_dot(by_row[d][...], low)
    packed_out[:, :TOTAL] = schur.astype(bf16)
    packed_out[:, TOTAL:] = base_ref[:, TOTAL:].astype(bf16)


def make_middle(where, square, by_row, by_col, base):
    shape = by_row[0].shape
    return pl.pallas_call(
        middle_kernel,
        out_shape=(
            jax.ShapeDtypeStruct(shape, f32),
            jax.ShapeDtypeStruct(shape, bf16),
            jax.ShapeDtypeStruct(shape, bf16),
            jax.ShapeDtypeStruct(shape, bf16),
            jax.ShapeDtypeStruct((TOTAL, TOTAL + STREAMS), bf16),
        ),
        in_specs=[SMEM] + [VMEM] * 9,
        out_specs=(VMEM,) * 5,
        compiler_params=params(),
        cost_estimate=cost(2_000_000_000, 8_000_000),
        name="middle",
    )(where, square, *by_row, *by_col[1:], base)


def invert_block(a):
    lane = lax.broadcasted_iota(jnp.int32, (1, BLOCK), 1)
    sub = lax.broadcasted_iota(jnp.int32, (PANEL, 1), 0)
    for k in range(0, BLOCK, PANEL):
        inside = (lane >= k) & (lane < k + PANEL)
        rows = a[k:k + PANEL, :]
        cols = [
            jnp.broadcast_to(rows[:, k + j:k + j + 1], (PANEL, BLOCK)) for j in range(PANEL)
        ]
        rows = jnp.where(inside, (lane - k == sub).astype(f32), rows)
        for i in range(PANEL):
            scale = 1.0 / cols[i][i:i + 1, :]
            factor = cols[i] - (sub == i).astype(f32)
            for j in range(i + 1, PANEL):
                cols[j] = cols[j] - factor * (cols[j][i:i + 1, :] * scale)
            rows = rows - factor * (rows[i:i + 1, :] * scale)
        rest = jnp.where(inside, 0.0, a)
        for i in range(PANEL):
            rest = rest - a[:, k + i:k + i + 1] * rows[i:i + 1, :]
        pieces = [rest[:k]] if k else []
        pieces.append(rows)
        if k + PANEL < BLOCK:
            pieces.append(rest[k + PANEL:])
        a = jnp.concatenate(pieces, axis=0)
    return a


def solve_kernel(
    first_ref, whole_ref, weighted_ref, precoded_ref, slots_ref, pivots_ref, users_ref, work_ref
):
    work_ref[...] = whole_ref[...]

    @pl.loop(0, EPOCHS)
    def _(b):
        start = pl.ds(pl.multiple_of(b * BLOCK, BLOCK), BLOCK)
        pivots_ref[b] = invert_block(work_ref[start, start])
        for k in range(EPOCHS):
            here = slice(k * BLOCK, (k + 1) * BLOCK)

            @pl.when(b == k)
            def _():
                scaled = split(dot, pivots_ref[k], work_ref[here, here.stop:])
                work_ref[here, here.stop:] = scaled
                if k + 1 < EPOCHS:
                    below = work_ref[here.stop:, here]
                    work_ref[here.stop:, here.stop:] -= split(dot, below, scaled)

    effect = work_ref[TOTAL - BLOCK:, TOTAL:]
    for b in range(EPOCHS - 2, -1, -1):
        here = slice(b * BLOCK, (b + 1) * BLOCK)
        part = work_ref[here, TOTAL:] - split(dot, work_ref[here, here.stop:TOTAL], effect)
        effect = jnp.concatenate([part, effect], axis=0)
    place = placing(slots_ref, first_ref[0], weighted_ref.shape[0])
    kept = 1.0 - jnp.sum(place, axis=1, keepdims=True)
    users = precoded_ref[...] * kept + split(dot, weighted_ref[...] - place, effect)
    for z in range(4):
        users_ref[z] = users.astype(bf16)


def make_solve(first, whole, weighted, precoded, slot_plane):
    return pl.pallas_call(
        solve_kernel,
        out_shape=(
            jax.ShapeDtypeStruct((EPOCHS, BLOCK, BLOCK), f32),
            jax.ShapeDtypeStruct((4, weighted.shape[0], STREAMS), bf16),
        ),
        in_specs=[SMEM] + [VMEM] * 4,
        out_specs=(VMEM,) * 2,
        scratch_shapes=[pltpu.VMEM(whole.shape, f32)],
        compiler_params=params(),
        cost_estimate=cost(14_000_000_000, 4_000_000),
        name="solve",
    )(first, whole, weighted, precoded, slot_plane)


def inverse_of(whole_ref, pivots_ref, inv_ref):
    inv_ref[...] = whole_ref[:, :TOTAL]
    row_id = lax.broadcasted_iota(jnp.int32, (TOTAL, BLOCK), 0)
    lane_id = lax.broadcasted_iota(jnp.int32, (TOTAL, BLOCK), 1)
    for b in range(EPOCHS):
        here = slice(b * BLOCK, (b + 1) * BLOCK)
        inside = (row_id >= here.start) & (row_id < here.stop)
        rest = jnp.where(inside, 0.0, inv_ref[:, here])
        inv_ref[:, here] = (row_id == lane_id + here.start).astype(f32)
        scaled = split(dot, pivots_ref[b], inv_ref[here, :])
        inv_ref[here, :] = jnp.zeros((BLOCK, TOTAL), f32)
        inv_ref[...] = inv_ref[...] - split(dot, rest, scaled)
        inv_ref[here, :] = scaled


def signal_kernel(users_ref, channel_ref, out_ref, held_ref, sems):
    groups, _, antennas = channel_ref.shape
    tile = antennas // 2
    copies = []
    for g in range(groups):
        for m in range(0, antennas, tile):
            part = t_dot(users_ref[g], channel_ref[g, :, m:m + tile]).astype(bf16)
            held_ref[g, :, :, m:m + tile] = part.reshape(16, STREAMS // 16, tile)
        copy = pltpu.make_async_copy(held_ref.at[g], out_ref.at[:, g], sems.at[g])
        copy.start()
        copies.append(copy)
    for copy in copies:
        copy.wait()


def make_signal(users_side, channel):
    groups, _, antennas = channel.shape
    each = STREAMS // 16
    return pl.pallas_call(
        signal_kernel,
        out_shape=jax.ShapeDtypeStruct((16, groups, each, antennas), bf16),
        in_specs=[VMEM, VMEM],
        out_specs=HBM,
        scratch_shapes=[
            pltpu.VMEM((groups, 16, each, antennas), bf16),
            pltpu.SemaphoreType.DMA((groups,)),
        ],
        compiler_params=params(),
        cost_estimate=cost(800_000_000, 7_000_000),
        name="signal",
    )(users_side, channel)


def total_kernel(received_ref, signal_ref, power_ref, sums_ref):
    g = pl.program_id(0)
    signal = jnp.sum(received_ref[:, 0].astype(f32), axis=0)
    signal_ref[0] = signal
    power = jnp.sum(signal * signal)
    lane = lax.broadcasted_iota(jnp.int32, sums_ref.shape, 1)

    @pl.when(g == 0)
    def _():
        sums_ref[...] = jnp.zeros(sums_ref.shape, f32)

    sums_ref[...] = jnp.where(lane == g, power, sums_ref[...])

    @pl.when(g == pl.num_programs(0) - 1)
    def _():
        power_ref[...] = jnp.broadcast_to(sums_ref[...], power_ref.shape)


def make_total(received):
    sources, groups, each, antennas = received.shape
    return pl.pallas_call(
        total_kernel,
        out_shape=(
            jax.ShapeDtypeStruct((groups, each, antennas), f32),
            jax.ShapeDtypeStruct((64 * 8, 128), f32),
        ),
        grid=(groups,),
        in_specs=[pl.BlockSpec((sources, 1, each, antennas), lambda g: (0, g, 0, 0))],
        out_specs=(
            pl.BlockSpec((1, each, antennas), lambda g: (g, 0, 0)),
            pl.BlockSpec((64 * 8, 128), lambda g: (0, 0)),
        ),
        scratch_shapes=[pltpu.VMEM((1, 128), f32)],
        compiler_params=params(),
        cost_estimate=cost(2_000_000_000, 4_000_000),
        name="total",
    )(received)


def update_kernel(
    where_ref, weighted_ref, whole_ref, pivots_ref, all_ref, slots_ref,
    out0, out1, out2, out3, inv_ref, held_ref, sems,
):
    first, plane = where_ref[0], where_ref[1]
    user_rows = weighted_ref.shape[0]
    inverse_of(whole_ref, pivots_ref, inv_ref)
    border = weighted_ref[...] - placing(slots_ref, first, user_rows)
    half = split(dot, border, inv_ref[...]).astype(bf16)
    copies = []
    for d, out in enumerate([out0, out1, out2, out3]):
        z = (plane + d) % 4
        there = all_ref[pl.ds(4 * z, 4)].reshape(4 * user_rows, TOTAL).astype(f32)
        there = there - placing(slots_ref, 4 * user_rows * z, 4 * user_rows)
        held_ref[d] = dot_t(half, there.astype(bf16)).astype(bf16)
        copy = pltpu.make_async_copy(held_ref.at[d], out, sems.at[d])
        copy.start()
        copies.append(copy)
    for copy in copies:
        copy.wait()


def make_update(where, weighted, whole, pivots, weighted_all, slot_plane):
    user_rows = weighted.shape[0]
    return pl.pallas_call(
        update_kernel,
        out_shape=(jax.ShapeDtypeStruct((user_rows, 4 * user_rows), bf16),) * 4,
        in_specs=[SMEM] + [VMEM] * 5,
        out_specs=(HBM,) * 4,
        scratch_shapes=[
            pltpu.VMEM((TOTAL, TOTAL), f32),
            pltpu.VMEM((4, user_rows, 4 * user_rows), bf16),
            pltpu.SemaphoreType.DMA((4,)),
        ],
        compiler_params=params(),
        cost_estimate=cost(1_500_000_000, 8_000_000),
        name="update",
    )(where, weighted, whole, pivots, weighted_all, slot_plane)


def local(channels, inverse, arrivals, arrival_cell, cell_owner, slots, symbols):
    group_count, user_rows, antennas = channels.shape
    user_cols = inverse.shape[2]
    capacity = arrivals.shape[2]
    cell_count = cell_owner.shape[0]
    grp_index = lax.axis_index("grp")
    row_index = lax.axis_index("row")
    col_index = lax.axis_index("col")
    y_index, x_index = row_index // 4, row_index % 4

    def along_x(value, step):
        pairs = [(4 * y + x, 4 * y + (x + step) % 4) for y in range(4) for x in range(4)]
        return lax.ppermute(value, "row", pairs)

    def along_y(value, step):
        pairs = [(4 * y + x, 4 * ((y + step) % 4) + x) for y in range(4) for x in range(4)]
        return lax.ppermute(value, "row", pairs)

    def along_z(value, step):
        return lax.ppermute(value, "col", [(z, (z + step) % 4) for z in range(4)])

    def to_planes(value):
        padded = jnp.concatenate([value, jnp.zeros_like(value[:1])], axis=0)
        return lax.all_to_all(padded, "col", 0, 0, tiled=True)

    first_group = grp_index * group_count
    other_first = (1 - grp_index) * group_count
    first_row = row_index * user_rows
    first_arg = first_row.reshape(1)

    with jax.named_scope("newcomers"):
        mine = lax.dynamic_slice_in_dim(arrivals, first_group, group_count, 0)
        theirs = lax.dynamic_slice_in_dim(arrivals, other_first, group_count, 0)
        swapped = lax.ppermute(theirs, "grp", [(0, 1), (1, 0)])
        from_0 = jnp.where(grp_index == 0, mine, swapped)
        from_1 = jnp.where(grp_index == 0, swapped, mine)
        chunk = jnp.stack([from_0, from_1], axis=2)
        per_group = EPOCHS * 2 * capacity
        chunk = chunk.reshape(group_count * per_group, antennas)
        chunk = jnp.pad(chunk, ((0, 112 - group_count * per_group), (0, 0)))
        gathered = lax.all_gather(chunk, "row")

    with jax.named_scope("planes"):
        pieces = list(make_pieces(x_index.reshape(1), inverse))
        for d in (1, 2, 3):
            pieces[d] = along_x(pieces[d], d)
        square = to_planes(jnp.stack(pieces, axis=1))
        symbol_part = jnp.einsum(
            "grc,gcs->grs", inverse, symbols.astype(f32), precision=highest
        )
        precoded = jnp.sum(to_planes(symbol_part), axis=0)

    plane_group = first_group + jnp.minimum(col_index, group_count - 1)
    slot_plane = lax.dynamic_slice_in_dim(slots, plane_group, 1, 0).reshape(1, TOTAL)
    row_ids = first_row + jnp.arange(user_rows, dtype=jnp.int32)

    cells_mine = lax.dynamic_slice_in_dim(arrival_cell, first_group, group_count, 0)[..., 0]
    slots_mine = lax.dynamic_slice_in_dim(slots, first_group, group_count, 0)
    slots_mine = slots_mine.reshape(group_count, 1, TOTAL)
    cell_table = (cells_mine[..., None] == jnp.arange(cell_count, dtype=jnp.int32)).astype(
        jnp.int32
    )
    owners = jnp.sum(cell_table * cell_owner, axis=-1)
    arrival_order = jnp.arange(ARRIVE, dtype=jnp.int32)
    earlier = (cells_mine[..., :, None] == cells_mine[..., None, :]) & (
        arrival_order[:, None] < arrival_order[None, :]
    )
    ranking = jnp.sum(earlier.astype(jnp.int32), axis=-2)
    with jax.named_scope("places"):
        offset = jnp.arange(group_count, dtype=jnp.int32) * per_group % 16
        epoch = jnp.arange(EPOCHS, dtype=jnp.int32)
        inside = offset[:, None] + epoch[None, :] * 2 * capacity
        inside = inside[:, :, None] + owners // 16 * capacity + ranking
        place = (owners % 16 * WINDOW + inside).reshape(group_count, 1, TOTAL)
        plane_place = lax.dynamic_slice_in_dim(
            place, jnp.minimum(col_index, group_count - 1), 1, 0
        ).reshape(1, TOTAL)

    with jax.named_scope("columns"):
        gathered, square, precoded = lax.optimization_barrier((gathered, square, precoded))
        both = make_columns(row_index.reshape(1), gathered, channels, place)
        both = lax.all_to_all(both, "col", 0, 0, tiled=True)
        summed = jnp.sum(both.astype(f32), axis=0)
        own = summed[:user_rows].astype(bf16)
        by_row = [own] + [along_x(own, d) for d in (1, 2, 3)]
        by_col = [own] + [along_y(own, -d) for d in (1, 2, 3)]

    with jax.named_scope("schur"):
        where = jnp.stack([y_index, row_index, first_row])
        base = make_target(where, summed, precoded, slot_plane, plane_place)
        block0, block1, block2, block3, packed = make_middle(where, square, by_row, by_col, base)
        weighted = block0
        for d, block in ((1, block1), (2, block2), (3, block3)):
            weighted = weighted + along_x(block, -d).astype(f32)
        weighted_all = lax.all_gather(weighted.astype(bf16), "row")
        packed = packed.reshape(16, SHARE, TOTAL + STREAMS)
        shared = lax.all_to_all(packed, "row", 0, 0, tiled=True)
        shared = jnp.sum(shared.astype(f32), axis=0)
        share_ids = row_index * SHARE + jnp.arange(SHARE, dtype=jnp.int32)
        identity = loading * (
            share_ids[:, None] == jnp.arange(TOTAL, dtype=jnp.int32)[None, :]
        ).astype(f32)
        schur_rows = identity - shared[:, :TOTAL]
        ready = jnp.concatenate([schur_rows, shared[:, TOTAL:]], axis=1)
        ready = jnp.broadcast_to(ready[None], (16, SHARE, TOTAL + STREAMS))
        whole = lax.all_to_all(ready, "row", 0, 0, tiled=True).reshape(TOTAL, TOTAL + STREAMS)

    with jax.named_scope("users"):
        channel = make_channel(first_arg, gathered, channels, place, slots_mine)
        whole, channel = lax.optimization_barrier((whole, channel))
        pivots, users = make_solve(first_arg, whole, weighted, precoded, slot_plane)
        users_side = lax.all_to_all(users, "col", 0, 0, tiled=True)

    with jax.named_scope("update"):
        changes = make_update(
            jnp.stack([first_row, col_index]), weighted, whole, pivots, weighted_all, slot_plane
        )
        changes = [changes[0]] + [along_z(changes[d], d) for d in (1, 2, 3)]

    with jax.named_scope("signal"):
        signal_part = make_signal(users_side, channel)
        received = lax.all_to_all(signal_part, "row", 0, 0, tiled=True)
        signal, power = make_total(received)
        power, changes = lax.optimization_barrier((power, changes))
        power = lax.all_to_all(power, ("row", "col"), 0, 0, tiled=True)
        total_power = jnp.sum(power, axis=0)[:group_count] / (8 * STREAMS * ANTENNAS)
        transmit = signal * lax.rsqrt(total_power + epsilon)[:, None, None]
        transmit = jnp.swapaxes(transmit, 0, 1)

    with jax.named_scope("final"):
        col_ids = col_index * user_cols + jnp.arange(user_cols, dtype=jnp.int32)
        diagonal = row_ids[:, None] == col_ids[None, :]
        full = jnp.any(slots_mine == row_ids[None, :, None], axis=2)
        gone = jnp.where(diagonal[None] & full[:, :, None], 1.0 / loading, 0.0)
        updated = []
        for g in range(group_count):
            step = (col_index - g) % 4
            add = changes[0]
            for d in (1, 2, 3):
                add = jnp.where(step == d, changes[d], add)
            updated.append(inverse[g] - gone[g] + add.astype(f32))
        updated = jnp.stack(updated, axis=0)
    return (updated, transmit)


def solution(mesh):
    placed = (
        P("grp", "row", "col"),
        P("grp", "row", "col"),
        P(None, None, ("grp", "row"), "col"),
        P(),
        P(),
        P(),
        P("grp", "col", None),
    )
    return jax.shard_map(
        local,
        mesh=mesh,
        in_specs=placed,
        out_specs=(P("grp", "row", "col"), P("row", "grp", "col")),
        check_vma=False,
    )
```

```python
import jax
import jax.numpy as jnp
from jax import lax
from jax.experimental import pallas as pl
from jax.experimental.pallas import tpu as pltpu
from jax.sharding import PartitionSpec as P

ANTENNAS = 8192
ARRIVE = 128
EPOCHS = 3
STREAMS = 256
TOTAL = ARRIVE * EPOCHS
BLOCK = 128
PANEL = 8
WINDOW = 48
SHARE = TOTAL // 16
FIRST = 1536

loading = 1.0
epsilon = 1e-06
highest = lax.Precision.HIGHEST
f32 = jnp.float32
bf16 = jnp.bfloat16
VMEM = pl.BlockSpec(memory_space=pltpu.VMEM)
SMEM = pl.BlockSpec(memory_space=pltpu.SMEM)
HBM = pl.BlockSpec(memory_space=pltpu.HBM)


def params(mib=40):
    return pltpu.CompilerParams(vmem_limit_bytes=mib * 1024 * 1024)


def cost(flops, nbytes):
    return pl.CostEstimate(flops=flops, bytes_accessed=nbytes, transcendentals=0)


def dot(a, b):
    return jnp.dot(a, b, preferred_element_type=f32)


def dot_t(a, b):
    return lax.dot_general(a, b, (((1,), (1,)), ((), ())), preferred_element_type=f32)


def t_dot(a, b):
    return lax.dot_general(a, b, (((0,), (0,)), ((), ())), preferred_element_type=f32)


def halves(a):
    high = a.astype(bf16)
    return high, (a - high.astype(f32)).astype(bf16)


def split(product, a, b):
    a_high, a_low = halves(a)
    b_high, b_low = halves(b)
    return product(a_high, b_low) + product(a_low, b_high) + product(a_high, b_high)


def placing(slots_ref, first, rows):
    ids = first + lax.broadcasted_iota(jnp.int32, (rows, TOTAL), 0)
    return (ids == slots_ref[...].reshape(1, TOTAL)).astype(f32)


def choosing(place_ref, g):
    ids = lax.broadcasted_iota(jnp.int32, (16 * WINDOW, TOTAL), 0)
    return (ids == place_ref[g]).astype(f32).astype(bf16)


def start_inputs(gathered_ref, relayed_ref, channel_ref, window_ref, held_ref, sems, row=None):
    groups, user_rows = channel_ref.shape[:2]
    copies = []
    for g in range(groups):
        rows = pl.ds(g * 2 * EPOCHS * 6 // 16 * 16, WINDOW)
        pairs = [
            (channel_ref.at[g], held_ref.at[g, :user_rows]),
            (gathered_ref.at[:, rows, :], window_ref.at[g, :, :, :FIRST]),
            (relayed_ref.at[:, rows, :], window_ref.at[g, :, :, FIRST:]),
        ]
        if row is not None:
            pairs.append((gathered_ref.at[row, rows, :], held_ref.at[g, user_rows:, :FIRST]))
            pairs.append((relayed_ref.at[0, rows, :], held_ref.at[g, user_rows:, FIRST:]))
        parts = [
            pltpu.make_async_copy(source, target, sems.at[n, g])
            for n, (source, target) in enumerate(pairs)
        ]
        for part in parts:
            part.start()
        copies.append(parts)
    return copies


def input_scratch(groups, rows, antennas):
    return [
        pltpu.VMEM((groups, 16, WINDOW, antennas), bf16),
        pltpu.VMEM((groups, rows, antennas), bf16),
        pltpu.SemaphoreType.DMA((5, groups)),
    ]


def columns_kernel(
    row_ref, gathered_ref, relayed_ref, channel_ref, place_ref, relative_ref,
    out_ref, window_ref, held_ref, sems,
):
    groups = channel_ref.shape[0]
    copies = start_inputs(
        gathered_ref, relayed_ref, channel_ref, window_ref, held_ref, sems, row_ref[0]
    )
    out_ref[groups] = jnp.zeros(out_ref.shape[1:], bf16)
    for g in range(groups):
        choose = choosing(place_ref, g)
        choose_relative = choosing(relative_ref, g)
        for copy in copies[g]:
            copy.wait()
        window = window_ref[g, :, :, :FIRST].reshape(16 * WINDOW, FIRST)
        wide = dot_t(held_ref[g, :, :FIRST], window).astype(bf16)
        total = dot(wide, choose)
        window = window_ref[g, :, :, FIRST:].reshape(16 * WINDOW, -1)
        wide = dot_t(held_ref[g, :, FIRST:], window).astype(bf16)
        out_ref[g] = (total + dot(wide, choose_relative)).astype(bf16)


def make_columns(row, gathered, relayed, channels, place, relative):
    groups, user_rows, antennas = channels.shape
    return pl.pallas_call(
        columns_kernel,
        out_shape=jax.ShapeDtypeStruct((groups + 1, user_rows + WINDOW, TOTAL), bf16),
        in_specs=[SMEM, HBM, HBM, HBM, VMEM, VMEM],
        out_specs=VMEM,
        scratch_shapes=input_scratch(groups, user_rows + WINDOW, antennas),
        compiler_params=params(60),
        cost_estimate=cost(8_000_000_000, 12_000_000),
        name="columns",
    )(row, gathered, relayed, channels, place, relative)


def channel_kernel(
    first_ref, gathered_ref, relayed_ref, channel_ref, place_ref, relative_ref, slots_ref,
    out_ref, window_ref, held_ref, sems,
):
    groups, user_rows, _ = channel_ref.shape
    copies = start_inputs(gathered_ref, relayed_ref, channel_ref, window_ref, held_ref, sems)
    for g in range(groups):
        here = placing(slots_ref.at[g], first_ref[0], user_rows).astype(bf16)
        route = dot_t(here, choosing(place_ref, g)).astype(bf16)
        route_relative = dot_t(here, choosing(relative_ref, g)).astype(bf16)
        for copy in copies[g]:
            copy.wait()
        window = window_ref[g, :, :, :FIRST].reshape(16 * WINDOW, FIRST)
        out_ref[g, :, :FIRST] = held_ref[g, :, :FIRST] + dot(route, window).astype(bf16)
        window = window_ref[g, :, :, FIRST:].reshape(16 * WINDOW, -1)
        added = dot(route_relative, window).astype(bf16)
        out_ref[g, :, FIRST:] = held_ref[g, :, FIRST:] + added


def make_channel(first, gathered, relayed, channels, place, relative, slots_mine):
    groups, user_rows, antennas = channels.shape
    return pl.pallas_call(
        channel_kernel,
        out_shape=jax.ShapeDtypeStruct(channels.shape, bf16),
        in_specs=[SMEM, HBM, HBM, HBM, VMEM, VMEM, VMEM],
        out_specs=VMEM,
        scratch_shapes=input_scratch(groups, user_rows, antennas),
        compiler_params=params(60),
        cost_estimate=cost(4_000_000_000, 14_000_000),
        name="channel",
    )(first, gathered, relayed, channels, place, relative, slots_mine)


def pieces_kernel(x_ref, inverse_ref, out0, out1, out2, out3):
    size = out0.shape[-1]
    for d, out in enumerate([out0, out1, out2, out3]):
        start = pl.multiple_of((x_ref[0] + d) % 4 * size, size)
        out[...] = inverse_ref[:, :, pl.ds(start, size)].astype(bf16)


def make_pieces(x, inverse):
    groups, user_rows = inverse.shape[:2]
    shape = jax.ShapeDtypeStruct((groups, user_rows, user_rows), bf16)
    return pl.pallas_call(
        pieces_kernel,
        out_shape=(shape,) * 4,
        in_specs=[SMEM, VMEM],
        out_specs=(VMEM,) * 4,
        compiler_params=params(16),
        cost_estimate=cost(100_000_000, 5_000_000),
        name="pieces",
    )(x, inverse)


def target_kernel(where_ref, summed_ref, precoded_ref, slots_ref, place_ref, base_out):
    row, first = where_ref[1], where_ref[2]
    user_rows = precoded_ref.shape[0]
    ids = row * WINDOW + lax.broadcasted_iota(jnp.int32, (WINDOW, TOTAL), 0)
    choose = (ids == place_ref[...]).astype(f32).astype(bf16)
    base_out[:, :TOTAL] = -t_dot(choose, summed_ref[user_rows:].astype(bf16))
    border = summed_ref[:user_rows] - placing(slots_ref, first, user_rows)
    base_out[:, TOTAL:] = split(t_dot, border, precoded_ref[...])


def make_target(where, summed, precoded, slot_plane, place_plane):
    return pl.pallas_call(
        target_kernel,
        out_shape=jax.ShapeDtypeStruct((TOTAL, TOTAL + STREAMS), f32),
        in_specs=[SMEM] + [VMEM] * 4,
        out_specs=VMEM,
        compiler_params=params(16),
        cost_estimate=cost(1_000_000_000, 2_000_000),
        name="target",
    )(where, summed, precoded, slot_plane, place_plane)


def middle_kernel(
    where_ref, square_ref, own_ref, row1_ref, row2_ref, row3_ref, col1_ref, col2_ref, col3_ref,
    base_ref, first_out, block1_out, block2_out, block3_out, packed_out,
):
    y = where_ref[0]
    by_row = [own_ref, row1_ref, row2_ref, row3_ref]
    by_col = [own_ref, col1_ref, col2_ref, col3_ref]
    outs = [first_out, block1_out, block2_out, block3_out]
    schur = base_ref[:, :TOTAL]
    for d in range(4):
        block = dot(square_ref[y, d], own_ref[...])
        for e in range(1, 4):
            block += dot(square_ref[(y + e) % 4, d], by_col[e][...])
        low = block.astype(bf16)
        outs[d][...] = block if d == 0 else low
        schur += t_dot(by_row[d][...], low)
    packed_out[:, :TOTAL] = schur.astype(bf16)
    packed_out[:, TOTAL:] = base_ref[:, TOTAL:].astype(bf16)


def make_middle(where, square, by_row, by_col, base):
    shape = by_row[0].shape
    return pl.pallas_call(
        middle_kernel,
        out_shape=(
            jax.ShapeDtypeStruct(shape, f32),
            jax.ShapeDtypeStruct(shape, bf16),
            jax.ShapeDtypeStruct(shape, bf16),
            jax.ShapeDtypeStruct(shape, bf16),
            jax.ShapeDtypeStruct((TOTAL, TOTAL + STREAMS), bf16),
        ),
        in_specs=[SMEM] + [VMEM] * 9,
        out_specs=(VMEM,) * 5,
        compiler_params=params(),
        cost_estimate=cost(2_000_000_000, 8_000_000),
        name="middle",
    )(where, square, *by_row, *by_col[1:], base)


def invert_block(a):
    lane = lax.broadcasted_iota(jnp.int32, (1, BLOCK), 1)
    sub = lax.broadcasted_iota(jnp.int32, (PANEL, 1), 0)
    for k in range(0, BLOCK, PANEL):
        inside = (lane >= k) & (lane < k + PANEL)
        rows = a[k:k + PANEL, :]
        cols = [
            jnp.broadcast_to(rows[:, k + j:k + j + 1], (PANEL, BLOCK)) for j in range(PANEL)
        ]
        rows = jnp.where(inside, (lane - k == sub).astype(f32), rows)
        for i in range(PANEL):
            scale = 1.0 / cols[i][i:i + 1, :]
            factor = cols[i] - (sub == i).astype(f32)
            for j in range(i + 1, PANEL):
                cols[j] = cols[j] - factor * (cols[j][i:i + 1, :] * scale)
            rows = rows - factor * (rows[i:i + 1, :] * scale)
        rest = jnp.where(inside, 0.0, a)
        for i in range(PANEL):
            rest = rest - a[:, k + i:k + i + 1] * rows[i:i + 1, :]
        pieces = [rest[:k]] if k else []
        pieces.append(rows)
        if k + PANEL < BLOCK:
            pieces.append(rest[k + PANEL:])
        a = jnp.concatenate(pieces, axis=0)
    return a


def solve_kernel(
    first_ref, whole_ref, weighted_ref, precoded_ref, slots_ref, pivots_ref, users_ref, work_ref
):
    work_ref[...] = whole_ref[...]

    @pl.loop(0, EPOCHS)
    def _(b):
        start = pl.ds(pl.multiple_of(b * BLOCK, BLOCK), BLOCK)
        pivots_ref[b] = invert_block(work_ref[start, start])
        for k in range(EPOCHS):
            here = slice(k * BLOCK, (k + 1) * BLOCK)

            @pl.when(b == k)
            def _():
                scaled = split(dot, pivots_ref[k], work_ref[here, here.stop:])
                work_ref[here, here.stop:] = scaled
                if k + 1 < EPOCHS:
                    below = work_ref[here.stop:, here]
                    work_ref[here.stop:, here.stop:] -= split(dot, below, scaled)

    effect = work_ref[TOTAL - BLOCK:, TOTAL:]
    for b in range(EPOCHS - 2, -1, -1):
        here = slice(b * BLOCK, (b + 1) * BLOCK)
        part = work_ref[here, TOTAL:] - split(dot, work_ref[here, here.stop:TOTAL], effect)
        effect = jnp.concatenate([part, effect], axis=0)
    place = placing(slots_ref, first_ref[0], weighted_ref.shape[0])
    kept = 1.0 - jnp.sum(place, axis=1, keepdims=True)
    users = precoded_ref[...] * kept + split(dot, weighted_ref[...] - place, effect)
    for z in range(4):
        users_ref[z] = users.astype(bf16)


def make_solve(first, whole, weighted, precoded, slot_plane):
    return pl.pallas_call(
        solve_kernel,
        out_shape=(
            jax.ShapeDtypeStruct((EPOCHS, BLOCK, BLOCK), f32),
            jax.ShapeDtypeStruct((4, weighted.shape[0], STREAMS), bf16),
        ),
        in_specs=[SMEM] + [VMEM] * 4,
        out_specs=(VMEM,) * 2,
        scratch_shapes=[pltpu.VMEM(whole.shape, f32)],
        compiler_params=params(),
        cost_estimate=cost(14_000_000_000, 4_000_000),
        name="solve",
    )(first, whole, weighted, precoded, slot_plane)


def inverse_of(whole_ref, pivots_ref, inv_ref):
    inv_ref[...] = whole_ref[:, :TOTAL]
    row_id = lax.broadcasted_iota(jnp.int32, (TOTAL, BLOCK), 0)
    lane_id = lax.broadcasted_iota(jnp.int32, (TOTAL, BLOCK), 1)
    for b in range(EPOCHS):
        here = slice(b * BLOCK, (b + 1) * BLOCK)
        inside = (row_id >= here.start) & (row_id < here.stop)
        rest = jnp.where(inside, 0.0, inv_ref[:, here])
        inv_ref[:, here] = (row_id == lane_id + here.start).astype(f32)
        scaled = split(dot, pivots_ref[b], inv_ref[here, :])
        inv_ref[here, :] = jnp.zeros((BLOCK, TOTAL), f32)
        inv_ref[...] = inv_ref[...] - split(dot, rest, scaled)
        inv_ref[here, :] = scaled


def signal_kernel(users_ref, channel_ref, out_ref, held_ref, sems):
    groups, _, antennas = channel_ref.shape
    tile = antennas // 2
    copies = []
    for g in range(groups):
        for m in range(0, antennas, tile):
            part = t_dot(users_ref[g], channel_ref[g, :, m:m + tile]).astype(bf16)
            held_ref[g, :, :, m:m + tile] = part.reshape(16, STREAMS // 16, tile)
        copy = pltpu.make_async_copy(held_ref.at[g], out_ref.at[:, g], sems.at[g])
        copy.start()
        copies.append(copy)
    for copy in copies:
        copy.wait()


def make_signal(users_side, channel):
    groups, _, antennas = channel.shape
    each = STREAMS // 16
    return pl.pallas_call(
        signal_kernel,
        out_shape=jax.ShapeDtypeStruct((16, groups, each, antennas), bf16),
        in_specs=[VMEM, VMEM],
        out_specs=HBM,
        scratch_shapes=[
            pltpu.VMEM((groups, 16, each, antennas), bf16),
            pltpu.SemaphoreType.DMA((groups,)),
        ],
        compiler_params=params(),
        cost_estimate=cost(800_000_000, 7_000_000),
        name="signal",
    )(users_side, channel)


def update_kernel(
    where_ref, weighted_ref, whole_ref, pivots_ref, all_ref, slots_ref,
    out0, out1, out2, out3, inv_ref, held_ref, sems,
):
    first, plane = where_ref[0], where_ref[1]
    user_rows = weighted_ref.shape[0]
    inverse_of(whole_ref, pivots_ref, inv_ref)
    border = weighted_ref[...] - placing(slots_ref, first, user_rows)
    half = split(dot, border, inv_ref[...]).astype(bf16)
    copies = []
    for d, out in enumerate([out0, out1, out2, out3]):
        z = (plane + d) % 4
        there = all_ref[pl.ds(4 * z, 4)].reshape(4 * user_rows, TOTAL).astype(f32)
        there = there - placing(slots_ref, 4 * user_rows * z, 4 * user_rows)
        held_ref[d] = dot_t(half, there.astype(bf16)).astype(bf16)
        copy = pltpu.make_async_copy(held_ref.at[d], out, sems.at[d])
        copy.start()
        copies.append(copy)
    for copy in copies:
        copy.wait()


def make_update(where, weighted, whole, pivots, weighted_all, slot_plane):
    user_rows = weighted.shape[0]
    return pl.pallas_call(
        update_kernel,
        out_shape=(jax.ShapeDtypeStruct((user_rows, 4 * user_rows), bf16),) * 4,
        in_specs=[SMEM] + [VMEM] * 5,
        out_specs=(HBM,) * 4,
        scratch_shapes=[
            pltpu.VMEM((TOTAL, TOTAL), f32),
            pltpu.VMEM((4, user_rows, 4 * user_rows), bf16),
            pltpu.SemaphoreType.DMA((4,)),
        ],
        compiler_params=params(),
        cost_estimate=cost(1_500_000_000, 8_000_000),
        name="update",
    )(where, weighted, whole, pivots, weighted_all, slot_plane)


def local(channels, inverse, arrivals, arrival_cell, cell_owner, slots, symbols):
    group_count, user_rows, antennas = channels.shape
    user_cols = inverse.shape[2]
    capacity = arrivals.shape[2]
    cell_count = cell_owner.shape[0]
    grp_index = lax.axis_index("grp")
    row_index = lax.axis_index("row")
    col_index = lax.axis_index("col")
    y_index, x_index = row_index // 4, row_index % 4

    def along_x(value, step):
        pairs = [(4 * y + x, 4 * y + (x + step) % 4) for y in range(4) for x in range(4)]
        return lax.ppermute(value, "row", pairs)

    def along_y(value, step):
        pairs = [(4 * y + x, 4 * ((y + step) % 4) + x) for y in range(4) for x in range(4)]
        return lax.ppermute(value, "row", pairs)

    def along_z(value, step):
        return lax.ppermute(value, "col", [(z, (z + step) % 4) for z in range(4)])

    def spread(value, along):
        half = value.shape[0] // 32 * 16
        behind, ahead = along(value, 1), along(value, -1)
        return jnp.concatenate(
            [value, behind, ahead, along(behind[:half], 1), along(ahead[half:], -1)], axis=0
        )

    def to_planes(value):
        padded = jnp.concatenate([value, jnp.zeros_like(value[:1])], axis=0)
        return lax.all_to_all(padded, "col", 0, 0, tiled=True)

    first_group = grp_index * group_count
    other_first = (1 - grp_index) * group_count
    first_row = row_index * user_rows
    first_arg = first_row.reshape(1)

    with jax.named_scope("newcomers"):
        mine = lax.dynamic_slice_in_dim(arrivals, first_group, group_count, 0)
        theirs = lax.dynamic_slice_in_dim(arrivals, other_first, group_count, 0)
        swapped = lax.ppermute(theirs, "grp", [(0, 1), (1, 0)])
        from_0 = jnp.where(grp_index == 0, mine, swapped)
        from_1 = jnp.where(grp_index == 0, swapped, mine)
        chunk = jnp.stack([from_0, from_1], axis=2)
        per_group = EPOCHS * 2 * capacity
        chunk = chunk.reshape(group_count * per_group, antennas)
        chunk = jnp.pad(chunk, ((0, 112 - group_count * per_group), (0, 0)))
        chunk, state, wanted = lax.optimization_barrier((chunk, inverse, symbols))
        gathered = lax.all_gather(chunk[:, :FIRST], "row")
        relayed = spread(spread(chunk[:, FIRST:], along_x), along_y)
        relayed = relayed.reshape(16, chunk.shape[0], antennas - FIRST)

    with jax.named_scope("planes"):
        pieces = list(make_pieces(x_index.reshape(1), state))
        for d in (1, 2, 3):
            pieces[d] = along_x(pieces[d], d)
        square = to_planes(jnp.stack(pieces, axis=1))
        symbol_part = jnp.einsum(
            "grc,gcs->grs", state, wanted.astype(f32), precision=highest
        )
        precoded = jnp.sum(to_planes(symbol_part), axis=0)

    plane_group = first_group + jnp.minimum(col_index, group_count - 1)
    slot_plane = lax.dynamic_slice_in_dim(slots, plane_group, 1, 0).reshape(1, TOTAL)
    row_ids = first_row + jnp.arange(user_rows, dtype=jnp.int32)

    cells_mine = lax.dynamic_slice_in_dim(arrival_cell, first_group, group_count, 0)[..., 0]
    slots_mine = lax.dynamic_slice_in_dim(slots, first_group, group_count, 0)
    slots_mine = slots_mine.reshape(group_count, 1, TOTAL)
    cell_table = (cells_mine[..., None] == jnp.arange(cell_count, dtype=jnp.int32)).astype(
        jnp.int32
    )
    owners = jnp.sum(cell_table * cell_owner, axis=-1)
    arrival_order = jnp.arange(ARRIVE, dtype=jnp.int32)
    earlier = (cells_mine[..., :, None] == cells_mine[..., None, :]) & (
        arrival_order[:, None] < arrival_order[None, :]
    )
    ranking = jnp.sum(earlier.astype(jnp.int32), axis=-2)
    with jax.named_scope("places"):
        offset = jnp.arange(group_count, dtype=jnp.int32) * per_group % 16
        epoch = jnp.arange(EPOCHS, dtype=jnp.int32)
        inside = offset[:, None] + epoch[None, :] * 2 * capacity
        inside = inside[:, :, None] + owners // 16 * capacity + ranking
        place = (owners % 16 * WINDOW + inside).reshape(group_count, 1, TOTAL)
        away_y = (owners % 16 // 4 - y_index) % 4
        away_x = (owners % 4 - x_index) % 4
        order_y = jnp.where(away_y == 0, 0, away_y % 3 + 1)
        order_x = jnp.where(away_x == 0, 0, away_x % 3 + 1)
        relative = ((order_y * 4 + order_x) * WINDOW + inside).reshape(group_count, 1, TOTAL)
        plane_place = lax.dynamic_slice_in_dim(
            place, jnp.minimum(col_index, group_count - 1), 1, 0
        ).reshape(1, TOTAL)

    with jax.named_scope("columns"):
        gathered, relayed, square, precoded = lax.optimization_barrier(
            (gathered, relayed, square, precoded)
        )
        both = make_columns(row_index.reshape(1), gathered, relayed, channels, place, relative)
        both = lax.all_to_all(both, "col", 0, 0, tiled=True)
        summed = jnp.sum(both.astype(f32), axis=0)
        own = summed[:user_rows].astype(bf16)
        by_row = [own] + [along_x(own, d) for d in (1, 2, 3)]
        by_col = [own] + [along_y(own, -d) for d in (1, 2, 3)]

    with jax.named_scope("schur"):
        where = jnp.stack([y_index, row_index, first_row])
        base = make_target(where, summed, precoded, slot_plane, plane_place)
        block0, block1, block2, block3, packed = make_middle(where, square, by_row, by_col, base)
        weighted = block0
        for d, block in ((1, block1), (2, block2), (3, block3)):
            weighted = weighted + along_x(block, -d).astype(f32)
        weighted_all = lax.all_gather(weighted.astype(bf16), "row")
        packed = packed.reshape(16, SHARE, TOTAL + STREAMS)
        shared = lax.all_to_all(packed, "row", 0, 0, tiled=True)
        shared = jnp.sum(shared.astype(f32), axis=0)
        share_ids = row_index * SHARE + jnp.arange(SHARE, dtype=jnp.int32)
        identity = loading * (
            share_ids[:, None] == jnp.arange(TOTAL, dtype=jnp.int32)[None, :]
        ).astype(f32)
        schur_rows = identity - shared[:, :TOTAL]
        ready = jnp.concatenate([schur_rows, shared[:, TOTAL:]], axis=1)
        ready = jnp.broadcast_to(ready[None], (16, SHARE, TOTAL + STREAMS))
        whole = lax.all_to_all(ready, "row", 0, 0, tiled=True).reshape(TOTAL, TOTAL + STREAMS)

    with jax.named_scope("users"):
        channel = make_channel(
            first_arg, gathered, relayed, channels, place, relative, slots_mine
        )
        whole, channel = lax.optimization_barrier((whole, channel))
        pivots, users = make_solve(first_arg, whole, weighted, precoded, slot_plane)
        users_side = lax.all_to_all(users, "col", 0, 0, tiled=True)

    with jax.named_scope("update"):
        changes = make_update(
            jnp.stack([first_row, col_index]), weighted, whole, pivots, weighted_all, slot_plane
        )
        changes = [changes[0]] + [along_z(changes[d], d) for d in (1, 2, 3)]

    with jax.named_scope("signal"):
        signal_part = make_signal(users_side, channel)
        received = lax.all_to_all(signal_part, "row", 0, 0, tiled=True)
        signal = jnp.sum(received.astype(f32), axis=0)
        power = jnp.sum(signal * signal, axis=(1, 2))
        power, changes = lax.optimization_barrier((power, changes))
        power = jnp.broadcast_to(power[None, None, :], (64, 1, group_count))
        power = lax.all_to_all(power, ("row", "col"), 0, 0, tiled=True)
        total_power = jnp.sum(power, axis=(0, 1)) / (STREAMS * ANTENNAS)
        transmit = signal * lax.rsqrt(total_power + epsilon)[:, None, None]
        transmit = jnp.swapaxes(transmit, 0, 1)

    with jax.named_scope("final"):
        col_ids = col_index * user_cols + jnp.arange(user_cols, dtype=jnp.int32)
        diagonal = row_ids[:, None] == col_ids[None, :]
        full = jnp.any(slots_mine == row_ids[None, :, None], axis=2)
        gone = jnp.where(diagonal[None] & full[:, :, None], 1.0 / loading, 0.0)
        updated = []
        for g in range(group_count):
            step = (col_index - g) % 4
            add = changes[0]
            for d in (1, 2, 3):
                add = jnp.where(step == d, changes[d], add)
            updated.append(inverse[g] - gone[g] + add.astype(f32))
        updated = jnp.stack(updated, axis=0)
    return (updated, transmit)


def solution(mesh):
    placed = (
        P("grp", "row", "col"),
        P("grp", "row", "col"),
        P(None, None, ("grp", "row"), "col"),
        P(),
        P(),
        P(),
        P("grp", "col", None),
    )
    return jax.shard_map(
        local,
        mesh=mesh,
        in_specs=placed,
        out_specs=(P("grp", "row", "col"), P("row", "grp", "col")),
        check_vma=False,
    )
```

```python
import jax
import jax.numpy as jnp
from jax import lax
from jax.experimental import pallas as pl
from jax.experimental.pallas import tpu as pltpu
from jax.sharding import PartitionSpec as P

ANTENNAS = 8192
ARRIVE = 128
EPOCHS = 3
STREAMS = 256
TOTAL = ARRIVE * EPOCHS
BLOCK = 128
PANEL = 8
WINDOW = 48
SHARE = TOTAL // 16

loading = 1.0
epsilon = 1e-06
highest = lax.Precision.HIGHEST
f32 = jnp.float32
bf16 = jnp.bfloat16
VMEM = pl.BlockSpec(memory_space=pltpu.VMEM)
SMEM = pl.BlockSpec(memory_space=pltpu.SMEM)
HBM = pl.BlockSpec(memory_space=pltpu.HBM)


def params(mib=40):
    return pltpu.CompilerParams(vmem_limit_bytes=mib * 1024 * 1024)


def cost(flops, nbytes):
    return pl.CostEstimate(flops=flops, bytes_accessed=nbytes, transcendentals=0)


def dot(a, b):
    return jnp.dot(a, b, preferred_element_type=f32)


def dot_t(a, b):
    return lax.dot_general(a, b, (((1,), (1,)), ((), ())), preferred_element_type=f32)


def t_dot(a, b):
    return lax.dot_general(a, b, (((0,), (0,)), ((), ())), preferred_element_type=f32)


def halves(a):
    high = a.astype(bf16)
    return high, (a - high.astype(f32)).astype(bf16)


def split(product, a, b):
    a_high, a_low = halves(a)
    b_high, b_low = halves(b)
    return product(a_high, b_low) + product(a_low, b_high) + product(a_high, b_high)


def placing(slots_ref, first, rows):
    ids = first + lax.broadcasted_iota(jnp.int32, (rows, TOTAL), 0)
    return (ids == slots_ref[...].reshape(1, TOTAL)).astype(f32)


def choosing(place_ref, g):
    ids = lax.broadcasted_iota(jnp.int32, (16 * WINDOW, TOTAL), 0)
    return (ids == place_ref[g]).astype(f32).astype(bf16)


def start_inputs(gathered_ref, channel_ref, window_ref, held_ref, sems, row=None):
    groups, user_rows = channel_ref.shape[:2]
    copies = []
    for g in range(groups):
        start = g * 2 * EPOCHS * 6 // 16 * 16
        source = gathered_ref.at[:, pl.ds(start, WINDOW), :]
        parts = [
            pltpu.make_async_copy(channel_ref.at[g], held_ref.at[g, :user_rows], sems.at[0, g]),
            pltpu.make_async_copy(source, window_ref.at[g], sems.at[1, g]),
        ]
        if row is not None:
            source = gathered_ref.at[row, pl.ds(start, WINDOW), :]
            parts.append(
                pltpu.make_async_copy(source, held_ref.at[g, user_rows:], sems.at[2, g])
            )
        for part in parts:
            part.start()
        copies.append(parts)
    return copies


def input_scratch(groups, rows, antennas):
    return [
        pltpu.VMEM((groups, 16, WINDOW, antennas), bf16),
        pltpu.VMEM((groups, rows, antennas), bf16),
        pltpu.SemaphoreType.DMA((3, groups)),
    ]


def columns_kernel(
    row_ref, gathered_ref, channel_ref, place_ref, out_ref, window_ref, held_ref, sems
):
    groups, _, antennas = channel_ref.shape
    copies = start_inputs(gathered_ref, channel_ref, window_ref, held_ref, sems, row_ref[0])
    out_ref[groups] = jnp.zeros(out_ref.shape[1:], bf16)
    for g in range(groups):
        choose = choosing(place_ref, g)
        for copy in copies[g]:
            copy.wait()
        window = window_ref[g].reshape(16 * WINDOW, antennas)
        wide = dot_t(held_ref[g], window).astype(bf16)
        out_ref[g] = dot(wide, choose).astype(bf16)


def make_columns(row, gathered, channels, place):
    groups, user_rows, antennas = channels.shape
    return pl.pallas_call(
        columns_kernel,
        out_shape=jax.ShapeDtypeStruct((groups + 1, user_rows + WINDOW, TOTAL), bf16),
        in_specs=[SMEM, HBM, HBM, VMEM],
        out_specs=VMEM,
        scratch_shapes=input_scratch(groups, user_rows + WINDOW, antennas),
        compiler_params=params(60),
        cost_estimate=cost(4_000_000_000, 12_000_000),
        name="columns",
    )(row, gathered, channels, place)


def channel_kernel(
    first_ref, gathered_ref, channel_ref, place_ref, slots_ref, out_ref, window_ref, held_ref, sems
):
    groups, user_rows, antennas = channel_ref.shape
    copies = start_inputs(gathered_ref, channel_ref, window_ref, held_ref, sems)
    for g in range(groups):
        here = placing(slots_ref.at[g], first_ref[0], user_rows).astype(bf16)
        route = dot_t(here, choosing(place_ref, g)).astype(bf16)
        for copy in copies[g]:
            copy.wait()
        window = window_ref[g].reshape(16 * WINDOW, antennas)
        out_ref[g] = held_ref[g] + dot(route, window).astype(bf16)


def make_channel(first, gathered, channels, place, slots_mine):
    groups, user_rows, antennas = channels.shape
    return pl.pallas_call(
        channel_kernel,
        out_shape=jax.ShapeDtypeStruct(channels.shape, bf16),
        in_specs=[SMEM, HBM, HBM, VMEM, VMEM],
        out_specs=VMEM,
        scratch_shapes=input_scratch(groups, user_rows, antennas),
        compiler_params=params(60),
        cost_estimate=cost(4_000_000_000, 14_000_000),
        name="channel",
    )(first, gathered, channels, place, slots_mine)


def pieces_kernel(x_ref, inverse_ref, out0, out1, out2, out3):
    size = out0.shape[-1]
    for d, out in enumerate([out0, out1, out2, out3]):
        start = pl.multiple_of((x_ref[0] + d) % 4 * size, size)
        out[...] = inverse_ref[:, :, pl.ds(start, size)].astype(bf16)


def make_pieces(x, inverse):
    groups, user_rows = inverse.shape[:2]
    shape = jax.ShapeDtypeStruct((groups, user_rows, user_rows), bf16)
    return pl.pallas_call(
        pieces_kernel,
        out_shape=(shape,) * 4,
        in_specs=[SMEM, VMEM],
        out_specs=(VMEM,) * 4,
        compiler_params=params(16),
        cost_estimate=cost(100_000_000, 5_000_000),
        name="pieces",
    )(x, inverse)


def target_kernel(where_ref, summed_ref, precoded_ref, slots_ref, place_ref, base_out):
    row, first = where_ref[1], where_ref[2]
    user_rows = precoded_ref.shape[0]
    ids = row * WINDOW + lax.broadcasted_iota(jnp.int32, (WINDOW, TOTAL), 0)
    choose = (ids == place_ref[...]).astype(f32).astype(bf16)
    base_out[:, :TOTAL] = -t_dot(choose, summed_ref[user_rows:].astype(bf16))
    border = summed_ref[:user_rows] - placing(slots_ref, first, user_rows)
    base_out[:, TOTAL:] = split(t_dot, border, precoded_ref[...])


def make_target(where, summed, precoded, slot_plane, place_plane):
    return pl.pallas_call(
        target_kernel,
        out_shape=jax.ShapeDtypeStruct((TOTAL, TOTAL + STREAMS), f32),
        in_specs=[SMEM] + [VMEM] * 4,
        out_specs=VMEM,
        compiler_params=params(16),
        cost_estimate=cost(1_000_000_000, 2_000_000),
        name="target",
    )(where, summed, precoded, slot_plane, place_plane)


def middle_kernel(
    where_ref, square_ref, own_ref, row1_ref, row2_ref, row3_ref, col1_ref, col2_ref, col3_ref,
    base_ref, first_out, block1_out, block2_out, block3_out, packed_out,
):
    y = where_ref[0]
    by_row = [own_ref, row1_ref, row2_ref, row3_ref]
    by_col = [own_ref, col1_ref, col2_ref, col3_ref]
    outs = [first_out, block1_out, block2_out, block3_out]
    schur = base_ref[:, :TOTAL]
    for d in range(4):
        block = dot(square_ref[y, d], own_ref[...])
        for e in range(1, 4):
            block += dot(square_ref[(y + e) % 4, d], by_col[e][...])
        low = block.astype(bf16)
        outs[d][...] = block if d == 0 else low
        schur += t_dot(by_row[d][...], low)
    packed_out[:, :TOTAL] = schur.astype(bf16)
    packed_out[:, TOTAL:] = base_ref[:, TOTAL:].astype(bf16)


def make_middle(where, square, by_row, by_col, base):
    shape = by_row[0].shape
    return pl.pallas_call(
        middle_kernel,
        out_shape=(
            jax.ShapeDtypeStruct(shape, f32),
            jax.ShapeDtypeStruct(shape, bf16),
            jax.ShapeDtypeStruct(shape, bf16),
            jax.ShapeDtypeStruct(shape, bf16),
            jax.ShapeDtypeStruct((TOTAL, TOTAL + STREAMS), bf16),
        ),
        in_specs=[SMEM] + [VMEM] * 9,
        out_specs=(VMEM,) * 5,
        compiler_params=params(),
        cost_estimate=cost(2_000_000_000, 8_000_000),
        name="middle",
    )(where, square, *by_row, *by_col[1:], base)


def invert_block(a):
    lane = lax.broadcasted_iota(jnp.int32, (1, BLOCK), 1)
    sub = lax.broadcasted_iota(jnp.int32, (PANEL, 1), 0)
    for k in range(0, BLOCK, PANEL):
        inside = (lane >= k) & (lane < k + PANEL)
        rows = a[k:k + PANEL, :]
        cols = [
            jnp.broadcast_to(rows[:, k + j:k + j + 1], (PANEL, BLOCK)) for j in range(PANEL)
        ]
        rows = jnp.where(inside, (lane - k == sub).astype(f32), rows)
        for i in range(PANEL):
            scale = 1.0 / cols[i][i:i + 1, :]
            factor = cols[i] - (sub == i).astype(f32)
            for j in range(i + 1, PANEL):
                cols[j] = cols[j] - factor * (cols[j][i:i + 1, :] * scale)
            rows = rows - factor * (rows[i:i + 1, :] * scale)
        rest = jnp.where(inside, 0.0, a)
        for i in range(PANEL):
            rest = rest - a[:, k + i:k + i + 1] * rows[i:i + 1, :]
        pieces = [rest[:k]] if k else []
        pieces.append(rows)
        if k + PANEL < BLOCK:
            pieces.append(rest[k + PANEL:])
        a = jnp.concatenate(pieces, axis=0)
    return a


def solve_kernel(
    first_ref, whole_ref, weighted_ref, precoded_ref, slots_ref, pivots_ref, users_ref, work_ref
):
    work_ref[...] = whole_ref[...]

    @pl.loop(0, EPOCHS)
    def _(b):
        start = pl.ds(pl.multiple_of(b * BLOCK, BLOCK), BLOCK)
        pivots_ref[b] = invert_block(work_ref[start, start])
        for k in range(EPOCHS):
            here = slice(k * BLOCK, (k + 1) * BLOCK)

            @pl.when(b == k)
            def _():
                scaled = split(dot, pivots_ref[k], work_ref[here, here.stop:])
                work_ref[here, here.stop:] = scaled
                if k + 1 < EPOCHS:
                    below = work_ref[here.stop:, here]
                    work_ref[here.stop:, here.stop:] -= split(dot, below, scaled)

    effect = work_ref[TOTAL - BLOCK:, TOTAL:]
    for b in range(EPOCHS - 2, -1, -1):
        here = slice(b * BLOCK, (b + 1) * BLOCK)
        part = work_ref[here, TOTAL:] - split(dot, work_ref[here, here.stop:TOTAL], effect)
        effect = jnp.concatenate([part, effect], axis=0)
    place = placing(slots_ref, first_ref[0], weighted_ref.shape[0])
    kept = 1.0 - jnp.sum(place, axis=1, keepdims=True)
    users = precoded_ref[...] * kept + split(dot, weighted_ref[...] - place, effect)
    for z in range(4):
        users_ref[z] = users.astype(bf16)


def make_solve(first, whole, weighted, precoded, slot_plane):
    return pl.pallas_call(
        solve_kernel,
        out_shape=(
            jax.ShapeDtypeStruct((EPOCHS, BLOCK, BLOCK), f32),
            jax.ShapeDtypeStruct((4, weighted.shape[0], STREAMS), bf16),
        ),
        in_specs=[SMEM] + [VMEM] * 4,
        out_specs=(VMEM,) * 2,
        scratch_shapes=[pltpu.VMEM(whole.shape, f32)],
        compiler_params=params(),
        cost_estimate=cost(14_000_000_000, 4_000_000),
        name="solve",
    )(first, whole, weighted, precoded, slot_plane)


def inverse_of(whole_ref, pivots_ref, inv_ref):
    inv_ref[...] = whole_ref[:, :TOTAL]
    row_id = lax.broadcasted_iota(jnp.int32, (TOTAL, BLOCK), 0)
    lane_id = lax.broadcasted_iota(jnp.int32, (TOTAL, BLOCK), 1)
    for b in range(EPOCHS):
        here = slice(b * BLOCK, (b + 1) * BLOCK)
        inside = (row_id >= here.start) & (row_id < here.stop)
        rest = jnp.where(inside, 0.0, inv_ref[:, here])
        inv_ref[:, here] = (row_id == lane_id + here.start).astype(f32)
        scaled = split(dot, pivots_ref[b], inv_ref[here, :])
        inv_ref[here, :] = jnp.zeros((BLOCK, TOTAL), f32)
        inv_ref[...] = inv_ref[...] - split(dot, rest, scaled)
        inv_ref[here, :] = scaled


def signal_kernel(users_ref, channel_ref, out_ref, held_ref, sems):
    groups, _, antennas = channel_ref.shape
    tile = antennas // 2
    copies = []
    for g in range(groups):
        for m in range(0, antennas, tile):
            part = t_dot(users_ref[g], channel_ref[g, :, m:m + tile]).astype(bf16)
            held_ref[g, :, :, m:m + tile] = part.reshape(16, STREAMS // 16, tile)
        copy = pltpu.make_async_copy(held_ref.at[g], out_ref.at[:, g], sems.at[g])
        copy.start()
        copies.append(copy)
    for copy in copies:
        copy.wait()


def make_signal(users_side, channel):
    groups, _, antennas = channel.shape
    each = STREAMS // 16
    return pl.pallas_call(
        signal_kernel,
        out_shape=jax.ShapeDtypeStruct((16, groups, each, antennas), bf16),
        in_specs=[VMEM, VMEM],
        out_specs=HBM,
        scratch_shapes=[
            pltpu.VMEM((groups, 16, each, antennas), bf16),
            pltpu.SemaphoreType.DMA((groups,)),
        ],
        compiler_params=params(),
        cost_estimate=cost(800_000_000, 7_000_000),
        name="signal",
    )(users_side, channel)


def update_kernel(
    where_ref, weighted_ref, whole_ref, pivots_ref, all_ref, slots_ref,
    out0, out1, out2, out3, inv_ref, held_ref, sems,
):
    first, plane = where_ref[0], where_ref[1]
    user_rows = weighted_ref.shape[0]
    inverse_of(whole_ref, pivots_ref, inv_ref)
    border = weighted_ref[...] - placing(slots_ref, first, user_rows)
    half = split(dot, border, inv_ref[...]).astype(bf16)
    copies = []
    for d, out in enumerate([out0, out1, out2, out3]):
        z = (plane + d) % 4
        there = all_ref[pl.ds(4 * z, 4)].reshape(4 * user_rows, TOTAL).astype(f32)
        there = there - placing(slots_ref, 4 * user_rows * z, 4 * user_rows)
        held_ref[d] = dot_t(half, there.astype(bf16)).astype(bf16)
        copy = pltpu.make_async_copy(held_ref.at[d], out, sems.at[d])
        copy.start()
        copies.append(copy)
    for copy in copies:
        copy.wait()


def make_update(where, weighted, whole, pivots, weighted_all, slot_plane):
    user_rows = weighted.shape[0]
    return pl.pallas_call(
        update_kernel,
        out_shape=(jax.ShapeDtypeStruct((user_rows, 4 * user_rows), bf16),) * 4,
        in_specs=[SMEM] + [VMEM] * 5,
        out_specs=(HBM,) * 4,
        scratch_shapes=[
            pltpu.VMEM((TOTAL, TOTAL), f32),
            pltpu.VMEM((4, user_rows, 4 * user_rows), bf16),
            pltpu.SemaphoreType.DMA((4,)),
        ],
        compiler_params=params(),
        cost_estimate=cost(1_500_000_000, 8_000_000),
        name="update",
    )(where, weighted, whole, pivots, weighted_all, slot_plane)


def local(channels, inverse, arrivals, arrival_cell, cell_owner, slots, symbols):
    group_count, user_rows, antennas = channels.shape
    user_cols = inverse.shape[2]
    capacity = arrivals.shape[2]
    cell_count = cell_owner.shape[0]
    grp_index = lax.axis_index("grp")
    row_index = lax.axis_index("row")
    col_index = lax.axis_index("col")
    y_index, x_index = row_index // 4, row_index % 4

    def along_x(value, step):
        pairs = [(4 * y + x, 4 * y + (x + step) % 4) for y in range(4) for x in range(4)]
        return lax.ppermute(value, "row", pairs)

    def along_y(value, step):
        pairs = [(4 * y + x, 4 * ((y + step) % 4) + x) for y in range(4) for x in range(4)]
        return lax.ppermute(value, "row", pairs)

    def along_z(value, step):
        return lax.ppermute(value, "col", [(z, (z + step) % 4) for z in range(4)])

    def to_planes(value):
        padded = jnp.concatenate([value, jnp.zeros_like(value[:1])], axis=0)
        return lax.all_to_all(padded, "col", 0, 0, tiled=True)

    first_group = grp_index * group_count
    other_first = (1 - grp_index) * group_count
    first_row = row_index * user_rows
    first_arg = first_row.reshape(1)

    with jax.named_scope("newcomers"):
        mine = lax.dynamic_slice_in_dim(arrivals, first_group, group_count, 0)
        theirs = lax.dynamic_slice_in_dim(arrivals, other_first, group_count, 0)
        swapped = lax.ppermute(theirs, "grp", [(0, 1), (1, 0)])
        from_0 = jnp.where(grp_index == 0, mine, swapped)
        from_1 = jnp.where(grp_index == 0, swapped, mine)
        chunk = jnp.stack([from_0, from_1], axis=2)
        per_group = EPOCHS * 2 * capacity
        chunk = chunk.reshape(group_count * per_group, antennas)
        chunk = jnp.pad(chunk, ((0, 112 - group_count * per_group), (0, 0)))
        gathered = lax.all_gather(chunk, "row")

    with jax.named_scope("planes"):
        pieces = list(make_pieces(x_index.reshape(1), inverse))
        for d in (1, 2, 3):
            pieces[d] = along_x(pieces[d], d)
        square = to_planes(jnp.stack(pieces, axis=1))
        symbol_part = jnp.einsum(
            "grc,gcs->grs", inverse, symbols.astype(f32), precision=highest
        )
        precoded = jnp.sum(to_planes(symbol_part), axis=0)

    plane_group = first_group + jnp.minimum(col_index, group_count - 1)
    slot_plane = lax.dynamic_slice_in_dim(slots, plane_group, 1, 0).reshape(1, TOTAL)
    row_ids = first_row + jnp.arange(user_rows, dtype=jnp.int32)

    cells_mine = lax.dynamic_slice_in_dim(arrival_cell, first_group, group_count, 0)[..., 0]
    slots_mine = lax.dynamic_slice_in_dim(slots, first_group, group_count, 0)
    slots_mine = slots_mine.reshape(group_count, 1, TOTAL)
    cell_table = (cells_mine[..., None] == jnp.arange(cell_count, dtype=jnp.int32)).astype(
        jnp.int32
    )
    owners = jnp.sum(cell_table * cell_owner, axis=-1)
    arrival_order = jnp.arange(ARRIVE, dtype=jnp.int32)
    earlier = (cells_mine[..., :, None] == cells_mine[..., None, :]) & (
        arrival_order[:, None] < arrival_order[None, :]
    )
    ranking = jnp.sum(earlier.astype(jnp.int32), axis=-2)
    with jax.named_scope("places"):
        offset = jnp.arange(group_count, dtype=jnp.int32) * per_group % 16
        epoch = jnp.arange(EPOCHS, dtype=jnp.int32)
        inside = offset[:, None] + epoch[None, :] * 2 * capacity
        inside = inside[:, :, None] + owners // 16 * capacity + ranking
        place = (owners % 16 * WINDOW + inside).reshape(group_count, 1, TOTAL)
        plane_place = lax.dynamic_slice_in_dim(
            place, jnp.minimum(col_index, group_count - 1), 1, 0
        ).reshape(1, TOTAL)

    with jax.named_scope("columns"):
        gathered, square, precoded = lax.optimization_barrier((gathered, square, precoded))
        both = make_columns(row_index.reshape(1), gathered, channels, place)
        both = lax.all_to_all(both, "col", 0, 0, tiled=True)
        summed = jnp.sum(both.astype(f32), axis=0)
        own = summed[:user_rows].astype(bf16)
        by_row = [own] + [along_x(own, d) for d in (1, 2, 3)]
        by_col = [own] + [along_y(own, -d) for d in (1, 2, 3)]

    with jax.named_scope("schur"):
        where = jnp.stack([y_index, row_index, first_row])
        base = make_target(where, summed, precoded, slot_plane, plane_place)
        block0, block1, block2, block3, packed = make_middle(where, square, by_row, by_col, base)
        weighted = block0
        for d, block in ((1, block1), (2, block2), (3, block3)):
            weighted = weighted + along_x(block, -d).astype(f32)
        weighted_all = lax.all_gather(weighted.astype(bf16), "row")
        packed = packed.reshape(16, SHARE, TOTAL + STREAMS)
        shared = lax.all_to_all(packed, "row", 0, 0, tiled=True)
        shared = jnp.sum(shared.astype(f32), axis=0)
        share_ids = row_index * SHARE + jnp.arange(SHARE, dtype=jnp.int32)
        identity = loading * (
            share_ids[:, None] == jnp.arange(TOTAL, dtype=jnp.int32)[None, :]
        ).astype(f32)
        schur_rows = identity - shared[:, :TOTAL]
        ready = jnp.concatenate([schur_rows, shared[:, TOTAL:]], axis=1)
        ready = jnp.broadcast_to(ready[None], (16, SHARE, TOTAL + STREAMS))
        whole = lax.all_to_all(ready, "row", 0, 0, tiled=True).reshape(TOTAL, TOTAL + STREAMS)

    with jax.named_scope("users"):
        channel = make_channel(first_arg, gathered, channels, place, slots_mine)
        whole, channel = lax.optimization_barrier((whole, channel))
        pivots, users = make_solve(first_arg, whole, weighted, precoded, slot_plane)
        users_side = lax.all_to_all(users, "col", 0, 0, tiled=True)

    with jax.named_scope("update"):
        changes = make_update(
            jnp.stack([first_row, col_index]), weighted, whole, pivots, weighted_all, slot_plane
        )
        changes = [changes[0]] + [along_z(changes[d], d) for d in (1, 2, 3)]

    with jax.named_scope("signal"):
        signal_part = make_signal(users_side, channel)
        received = lax.all_to_all(signal_part, "row", 0, 0, tiled=True)
        signal = jnp.sum(received.astype(f32), axis=0)
        power = jnp.sum(signal * signal, axis=(1, 2))
        power, changes = lax.optimization_barrier((power, changes))
        power = jnp.broadcast_to(power[None, None, :], (64, 1, group_count))
        power = lax.all_to_all(power, ("row", "col"), 0, 0, tiled=True)
        total_power = jnp.sum(power, axis=(0, 1)) / (STREAMS * ANTENNAS)
        transmit = signal * lax.rsqrt(total_power + epsilon)[:, None, None]
        transmit = jnp.swapaxes(transmit, 0, 1)

    with jax.named_scope("final"):
        col_ids = col_index * user_cols + jnp.arange(user_cols, dtype=jnp.int32)
        diagonal = row_ids[:, None] == col_ids[None, :]
        full = jnp.any(slots_mine == row_ids[None, :, None], axis=2)
        gone = jnp.where(diagonal[None] & full[:, :, None], 1.0 / loading, 0.0)
        updated = []
        for g in range(group_count):
            step = (col_index - g) % 4
            add = changes[0]
            for d in (1, 2, 3):
                add = jnp.where(step == d, changes[d], add)
            updated.append(inverse[g] - gone[g] + add.astype(f32))
        updated = jnp.stack(updated, axis=0)
    return (updated, transmit)


def solution(mesh):
    placed = (
        P("grp", "row", "col"),
        P("grp", "row", "col"),
        P(None, None, ("grp", "row"), "col"),
        P(),
        P(),
        P(),
        P("grp", "col", None),
    )
    return jax.shard_map(
        local,
        mesh=mesh,
        in_specs=placed,
        out_specs=(P("grp", "row", "col"), P("row", "grp", "col")),
        check_vma=False,
    )
```

```python
import jax
import jax.numpy as jnp
from jax import lax
from jax.experimental import pallas as pl
from jax.experimental.pallas import tpu as pltpu
from jax.sharding import PartitionSpec as P

ANTENNAS = 8192
ARRIVE = 128
EPOCHS = 3
STREAMS = 256
TOTAL = ARRIVE * EPOCHS
BLOCK = 128
PANEL = 8
WINDOW = 48
SHARE = TOTAL // 16

loading = 1.0
epsilon = 1e-06
highest = lax.Precision.HIGHEST
f32 = jnp.float32
bf16 = jnp.bfloat16
VMEM = pl.BlockSpec(memory_space=pltpu.VMEM)
SMEM = pl.BlockSpec(memory_space=pltpu.SMEM)
HBM = pl.BlockSpec(memory_space=pltpu.HBM)


def params(mib=40):
    return pltpu.CompilerParams(vmem_limit_bytes=mib * 1024 * 1024)


def cost(flops, nbytes):
    return pl.CostEstimate(flops=flops, bytes_accessed=nbytes, transcendentals=0)


def dot(a, b):
    return jnp.dot(a, b, preferred_element_type=f32)


def dot_t(a, b):
    return lax.dot_general(a, b, (((1,), (1,)), ((), ())), preferred_element_type=f32)


def t_dot(a, b):
    return lax.dot_general(a, b, (((0,), (0,)), ((), ())), preferred_element_type=f32)


def halves(a):
    high = a.astype(bf16)
    return high, (a - high.astype(f32)).astype(bf16)


def split(product, a, b):
    a_high, a_low = halves(a)
    b_high, b_low = halves(b)
    return product(a_high, b_low) + product(a_low, b_high) + product(a_high, b_high)


def placing(slots_ref, first, rows):
    ids = first + lax.broadcasted_iota(jnp.int32, (rows, TOTAL), 0)
    return (ids == slots_ref[...].reshape(1, TOTAL)).astype(f32)


def choosing(place_ref, g):
    ids = lax.broadcasted_iota(jnp.int32, (16 * WINDOW, TOTAL), 0)
    return (ids == place_ref[g]).astype(f32).astype(bf16)


def start_inputs(gathered_ref, channel_ref, window_ref, held_ref, sems, row=None):
    groups, user_rows = channel_ref.shape[:2]
    copies = []
    for g in range(groups):
        start = g * 2 * EPOCHS * 6 // 16 * 16
        source = gathered_ref.at[:, pl.ds(start, WINDOW), :]
        parts = [
            pltpu.make_async_copy(channel_ref.at[g], held_ref.at[g, :user_rows], sems.at[0, g]),
            pltpu.make_async_copy(source, window_ref.at[g], sems.at[1, g]),
        ]
        if row is not None:
            source = gathered_ref.at[row, pl.ds(start, WINDOW), :]
            parts.append(
                pltpu.make_async_copy(source, held_ref.at[g, user_rows:], sems.at[2, g])
            )
        for part in parts:
            part.start()
        copies.append(parts)
    return copies


def input_scratch(groups, rows, antennas):
    return [
        pltpu.VMEM((groups, 16, WINDOW, antennas), bf16),
        pltpu.VMEM((groups, rows, antennas), bf16),
        pltpu.SemaphoreType.DMA((3, groups)),
    ]


def columns_kernel(
    row_ref, gathered_ref, channel_ref, place_ref, out_ref, window_ref, held_ref, sems
):
    groups, _, antennas = channel_ref.shape
    row, plane = row_ref[0], row_ref[1]
    copies = start_inputs(gathered_ref, channel_ref, window_ref, held_ref, sems, row)
    out_ref[(groups - plane) % 4] = jnp.zeros(out_ref.shape[1:], bf16)
    for g in range(groups):
        choose = choosing(place_ref, g)
        for copy in copies[g]:
            copy.wait()
        window = window_ref[g].reshape(16 * WINDOW, antennas)
        wide = dot_t(held_ref[g], window).astype(bf16)
        out_ref[(g - plane) % 4] = dot(wide, choose).astype(bf16)


def make_columns(row, gathered, channels, place):
    groups, user_rows, antennas = channels.shape
    return pl.pallas_call(
        columns_kernel,
        out_shape=jax.ShapeDtypeStruct((groups + 1, user_rows + WINDOW, TOTAL), bf16),
        in_specs=[SMEM, HBM, HBM, VMEM],
        out_specs=VMEM,
        scratch_shapes=input_scratch(groups, user_rows + WINDOW, antennas),
        compiler_params=params(60),
        cost_estimate=cost(4_000_000_000, 12_000_000),
        name="columns",
    )(row, gathered, channels, place)


def channel_kernel(
    first_ref, gathered_ref, channel_ref, place_ref, slots_ref, out_ref, window_ref, held_ref, sems
):
    groups, user_rows, antennas = channel_ref.shape
    copies = start_inputs(gathered_ref, channel_ref, window_ref, held_ref, sems)
    for g in range(groups):
        here = placing(slots_ref.at[g], first_ref[0], user_rows).astype(bf16)
        route = dot_t(here, choosing(place_ref, g)).astype(bf16)
        for copy in copies[g]:
            copy.wait()
        window = window_ref[g].reshape(16 * WINDOW, antennas)
        out_ref[g] = held_ref[g] + dot(route, window).astype(bf16)


def make_channel(first, gathered, channels, place, slots_mine):
    groups, user_rows, antennas = channels.shape
    return pl.pallas_call(
        channel_kernel,
        out_shape=jax.ShapeDtypeStruct(channels.shape, bf16),
        in_specs=[SMEM, HBM, HBM, VMEM, VMEM],
        out_specs=VMEM,
        scratch_shapes=input_scratch(groups, user_rows, antennas),
        compiler_params=params(60),
        cost_estimate=cost(4_000_000_000, 14_000_000),
        name="channel",
    )(first, gathered, channels, place, slots_mine)


def pieces_kernel(x_ref, inverse_ref, out0, out1, out2, out3):
    size = out0.shape[-1]
    for d, out in enumerate([out0, out1, out2, out3]):
        start = pl.multiple_of((x_ref[0] + d) % 4 * size, size)
        out[...] = inverse_ref[:, :, pl.ds(start, size)].astype(bf16)


def make_pieces(x, inverse):
    groups, user_rows = inverse.shape[:2]
    shape = jax.ShapeDtypeStruct((groups, user_rows, user_rows), bf16)
    return pl.pallas_call(
        pieces_kernel,
        out_shape=(shape,) * 4,
        in_specs=[SMEM, VMEM],
        out_specs=(VMEM,) * 4,
        compiler_params=params(16),
        cost_estimate=cost(100_000_000, 5_000_000),
        name="pieces",
    )(x, inverse)


def target_kernel(where_ref, summed_ref, precoded_ref, slots_ref, place_ref, base_out):
    row, first = where_ref[1], where_ref[2]
    user_rows = precoded_ref.shape[0]
    ids = row * WINDOW + lax.broadcasted_iota(jnp.int32, (WINDOW, TOTAL), 0)
    choose = (ids == place_ref[...]).astype(f32).astype(bf16)
    base_out[:, :TOTAL] = -t_dot(choose, summed_ref[user_rows:].astype(bf16))
    border = summed_ref[:user_rows] - placing(slots_ref, first, user_rows)
    base_out[:, TOTAL:] = split(t_dot, border, precoded_ref[...])


def make_target(where, summed, precoded, slot_plane, place_plane):
    return pl.pallas_call(
        target_kernel,
        out_shape=jax.ShapeDtypeStruct((TOTAL, TOTAL + STREAMS), f32),
        in_specs=[SMEM] + [VMEM] * 4,
        out_specs=VMEM,
        compiler_params=params(16),
        cost_estimate=cost(1_000_000_000, 2_000_000),
        name="target",
    )(where, summed, precoded, slot_plane, place_plane)


def middle_kernel(
    where_ref, square_ref, own_ref, row1_ref, row2_ref, row3_ref, col1_ref, col2_ref, col3_ref,
    base_ref, first_out, block1_out, block2_out, block3_out, packed_out,
):
    y = where_ref[0]
    by_row = [own_ref, row1_ref, row2_ref, row3_ref]
    by_col = [own_ref, col1_ref, col2_ref, col3_ref]
    outs = [first_out, block1_out, block2_out, block3_out]
    schur = base_ref[:, :TOTAL]
    for d in range(4):
        block = dot(square_ref[y, d], own_ref[...])
        for e in range(1, 4):
            block += dot(square_ref[(y + e) % 4, d], by_col[e][...])
        low = block.astype(bf16)
        outs[d][...] = block if d == 0 else low
        schur += t_dot(by_row[d][...], low)
    packed_out[:, :TOTAL] = schur.astype(bf16)
    packed_out[:, TOTAL:] = base_ref[:, TOTAL:].astype(bf16)


def make_middle(where, square, by_row, by_col, base):
    shape = by_row[0].shape
    return pl.pallas_call(
        middle_kernel,
        out_shape=(
            jax.ShapeDtypeStruct(shape, f32),
            jax.ShapeDtypeStruct(shape, bf16),
            jax.ShapeDtypeStruct(shape, bf16),
            jax.ShapeDtypeStruct(shape, bf16),
            jax.ShapeDtypeStruct((TOTAL, TOTAL + STREAMS), bf16),
        ),
        in_specs=[SMEM] + [VMEM] * 9,
        out_specs=(VMEM,) * 5,
        compiler_params=params(),
        cost_estimate=cost(2_000_000_000, 8_000_000),
        name="middle",
    )(where, square, *by_row, *by_col[1:], base)


def invert_block(a):
    lane = lax.broadcasted_iota(jnp.int32, (1, BLOCK), 1)
    sub = lax.broadcasted_iota(jnp.int32, (PANEL, 1), 0)
    for k in range(0, BLOCK, PANEL):
        inside = (lane >= k) & (lane < k + PANEL)
        rows = a[k:k + PANEL, :]
        cols = [
            jnp.broadcast_to(rows[:, k + j:k + j + 1], (PANEL, BLOCK)) for j in range(PANEL)
        ]
        rows = jnp.where(inside, (lane - k == sub).astype(f32), rows)
        for i in range(PANEL):
            scale = 1.0 / cols[i][i:i + 1, :]
            factor = cols[i] - (sub == i).astype(f32)
            for j in range(i + 1, PANEL):
                cols[j] = cols[j] - factor * (cols[j][i:i + 1, :] * scale)
            rows = rows - factor * (rows[i:i + 1, :] * scale)
        rest = jnp.where(inside, 0.0, a)
        for i in range(PANEL):
            rest = rest - a[:, k + i:k + i + 1] * rows[i:i + 1, :]
        pieces = [rest[:k]] if k else []
        pieces.append(rows)
        if k + PANEL < BLOCK:
            pieces.append(rest[k + PANEL:])
        a = jnp.concatenate(pieces, axis=0)
    return a


def solve_kernel(
    first_ref, whole_ref, weighted_ref, precoded_ref, slots_ref, pivots_ref, users_ref, work_ref
):
    work_ref[...] = whole_ref[...]

    @pl.loop(0, EPOCHS)
    def _(b):
        start = pl.ds(pl.multiple_of(b * BLOCK, BLOCK), BLOCK)
        pivots_ref[b] = invert_block(work_ref[start, start])
        for k in range(EPOCHS):
            here = slice(k * BLOCK, (k + 1) * BLOCK)

            @pl.when(b == k)
            def _():
                scaled = split(dot, pivots_ref[k], work_ref[here, here.stop:])
                work_ref[here, here.stop:] = scaled
                if k + 1 < EPOCHS:
                    below = work_ref[here.stop:, here]
                    work_ref[here.stop:, here.stop:] -= split(dot, below, scaled)

    effect = work_ref[TOTAL - BLOCK:, TOTAL:]
    for b in range(EPOCHS - 2, -1, -1):
        here = slice(b * BLOCK, (b + 1) * BLOCK)
        part = work_ref[here, TOTAL:] - split(dot, work_ref[here, here.stop:TOTAL], effect)
        effect = jnp.concatenate([part, effect], axis=0)
    place = placing(slots_ref, first_ref[0], weighted_ref.shape[0])
    kept = 1.0 - jnp.sum(place, axis=1, keepdims=True)
    users = precoded_ref[...] * kept + split(dot, weighted_ref[...] - place, effect)
    for z in range(4):
        users_ref[z] = users.astype(bf16)


def make_solve(first, whole, weighted, precoded, slot_plane):
    return pl.pallas_call(
        solve_kernel,
        out_shape=(
            jax.ShapeDtypeStruct((EPOCHS, BLOCK, BLOCK), f32),
            jax.ShapeDtypeStruct((4, weighted.shape[0], STREAMS), bf16),
        ),
        in_specs=[SMEM] + [VMEM] * 4,
        out_specs=(VMEM,) * 2,
        scratch_shapes=[pltpu.VMEM(whole.shape, f32)],
        compiler_params=params(),
        cost_estimate=cost(14_000_000_000, 4_000_000),
        name="solve",
    )(first, whole, weighted, precoded, slot_plane)


def inverse_of(whole_ref, pivots_ref, inv_ref):
    inv_ref[...] = whole_ref[:, :TOTAL]
    row_id = lax.broadcasted_iota(jnp.int32, (TOTAL, BLOCK), 0)
    lane_id = lax.broadcasted_iota(jnp.int32, (TOTAL, BLOCK), 1)
    for b in range(EPOCHS):
        here = slice(b * BLOCK, (b + 1) * BLOCK)
        inside = (row_id >= here.start) & (row_id < here.stop)
        rest = jnp.where(inside, 0.0, inv_ref[:, here])
        inv_ref[:, here] = (row_id == lane_id + here.start).astype(f32)
        scaled = split(dot, pivots_ref[b], inv_ref[here, :])
        inv_ref[here, :] = jnp.zeros((BLOCK, TOTAL), f32)
        inv_ref[...] = inv_ref[...] - split(dot, rest, scaled)
        inv_ref[here, :] = scaled


def signal_kernel(users_ref, channel_ref, out_ref, held_ref, sems):
    groups, _, antennas = channel_ref.shape
    tile = antennas // 2
    copies = []
    for g in range(groups):
        for m in range(0, antennas, tile):
            part = t_dot(users_ref[g], channel_ref[g, :, m:m + tile]).astype(bf16)
            held_ref[g, :, :, m:m + tile] = part.reshape(16, STREAMS // 16, tile)
        copy = pltpu.make_async_copy(held_ref.at[g], out_ref.at[:, g], sems.at[g])
        copy.start()
        copies.append(copy)
    for copy in copies:
        copy.wait()


def make_signal(users_side, channel):
    groups, _, antennas = channel.shape
    each = STREAMS // 16
    return pl.pallas_call(
        signal_kernel,
        out_shape=jax.ShapeDtypeStruct((16, groups, each, antennas), bf16),
        in_specs=[VMEM, VMEM],
        out_specs=HBM,
        scratch_shapes=[
            pltpu.VMEM((groups, 16, each, antennas), bf16),
            pltpu.SemaphoreType.DMA((groups,)),
        ],
        compiler_params=params(),
        cost_estimate=cost(800_000_000, 7_000_000),
        name="signal",
    )(users_side, channel)


def update_kernel(
    where_ref, weighted_ref, whole_ref, pivots_ref, all_ref, slots_ref,
    out0, out1, out2, out3, inv_ref, held_ref, sems,
):
    first, plane = where_ref[0], where_ref[1]
    user_rows = weighted_ref.shape[0]
    inverse_of(whole_ref, pivots_ref, inv_ref)
    border = weighted_ref[...] - placing(slots_ref, first, user_rows)
    half = split(dot, border, inv_ref[...]).astype(bf16)
    copies = []
    for d, out in enumerate([out0, out1, out2, out3]):
        z = (plane + d) % 4
        there = all_ref[pl.ds(4 * z, 4)].reshape(4 * user_rows, TOTAL).astype(f32)
        there = there - placing(slots_ref, 4 * user_rows * z, 4 * user_rows)
        held_ref[d] = dot_t(half, there.astype(bf16)).astype(bf16)
        copy = pltpu.make_async_copy(held_ref.at[d], out, sems.at[d])
        copy.start()
        copies.append(copy)
    for copy in copies:
        copy.wait()


def make_update(where, weighted, whole, pivots, weighted_all, slot_plane):
    user_rows = weighted.shape[0]
    return pl.pallas_call(
        update_kernel,
        out_shape=(jax.ShapeDtypeStruct((user_rows, 4 * user_rows), bf16),) * 4,
        in_specs=[SMEM] + [VMEM] * 5,
        out_specs=(HBM,) * 4,
        scratch_shapes=[
            pltpu.VMEM((TOTAL, TOTAL), f32),
            pltpu.VMEM((4, user_rows, 4 * user_rows), bf16),
            pltpu.SemaphoreType.DMA((4,)),
        ],
        compiler_params=params(),
        cost_estimate=cost(1_500_000_000, 8_000_000),
        name="update",
    )(where, weighted, whole, pivots, weighted_all, slot_plane)


def local(channels, inverse, arrivals, arrival_cell, cell_owner, slots, symbols):
    group_count, user_rows, antennas = channels.shape
    user_cols = inverse.shape[2]
    capacity = arrivals.shape[2]
    cell_count = cell_owner.shape[0]
    grp_index = lax.axis_index("grp")
    row_index = lax.axis_index("row")
    col_index = lax.axis_index("col")
    y_index, x_index = row_index // 4, row_index % 4

    def along_x(value, step):
        pairs = [(4 * y + x, 4 * y + (x + step) % 4) for y in range(4) for x in range(4)]
        return lax.ppermute(value, "row", pairs)

    def along_y(value, step):
        pairs = [(4 * y + x, 4 * ((y + step) % 4) + x) for y in range(4) for x in range(4)]
        return lax.ppermute(value, "row", pairs)

    def along_z(value, step):
        return lax.ppermute(value, "col", [(z, (z + step) % 4) for z in range(4)])

    def to_planes(value):
        padded = jnp.concatenate([value, jnp.zeros_like(value[:1])], axis=0)
        return lax.all_to_all(padded, "col", 0, 0, tiled=True)

    first_group = grp_index * group_count
    other_first = (1 - grp_index) * group_count
    first_row = row_index * user_rows
    first_arg = first_row.reshape(1)

    with jax.named_scope("newcomers"):
        mine = lax.dynamic_slice_in_dim(arrivals, first_group, group_count, 0)
        theirs = lax.dynamic_slice_in_dim(arrivals, other_first, group_count, 0)
        swapped = lax.ppermute(theirs, "grp", [(0, 1), (1, 0)])
        from_0 = jnp.where(grp_index == 0, mine, swapped)
        from_1 = jnp.where(grp_index == 0, swapped, mine)
        chunk = jnp.stack([from_0, from_1], axis=2)
        per_group = EPOCHS * 2 * capacity
        chunk = chunk.reshape(group_count * per_group, antennas)
        chunk = jnp.pad(chunk, ((0, 112 - group_count * per_group), (0, 0)))
        gathered = lax.all_gather(chunk, "row")

    with jax.named_scope("planes"):
        pieces = list(make_pieces(x_index.reshape(1), inverse))
        for d in (1, 2, 3):
            pieces[d] = along_x(pieces[d], d)
        square = to_planes(jnp.stack(pieces, axis=1))
        symbol_part = jnp.einsum(
            "grc,gcs->grs", inverse, symbols.astype(f32), precision=highest
        )
        precoded = jnp.sum(to_planes(symbol_part), axis=0)

    plane_group = first_group + jnp.minimum(col_index, group_count - 1)
    slot_plane = lax.dynamic_slice_in_dim(slots, plane_group, 1, 0).reshape(1, TOTAL)
    row_ids = first_row + jnp.arange(user_rows, dtype=jnp.int32)

    cells_mine = lax.dynamic_slice_in_dim(arrival_cell, first_group, group_count, 0)[..., 0]
    slots_mine = lax.dynamic_slice_in_dim(slots, first_group, group_count, 0)
    slots_mine = slots_mine.reshape(group_count, 1, TOTAL)
    cell_table = (cells_mine[..., None] == jnp.arange(cell_count, dtype=jnp.int32)).astype(
        jnp.int32
    )
    owners = jnp.sum(cell_table * cell_owner, axis=-1)
    arrival_order = jnp.arange(ARRIVE, dtype=jnp.int32)
    earlier = (cells_mine[..., :, None] == cells_mine[..., None, :]) & (
        arrival_order[:, None] < arrival_order[None, :]
    )
    ranking = jnp.sum(earlier.astype(jnp.int32), axis=-2)
    with jax.named_scope("places"):
        offset = jnp.arange(group_count, dtype=jnp.int32) * per_group % 16
        epoch = jnp.arange(EPOCHS, dtype=jnp.int32)
        inside = offset[:, None] + epoch[None, :] * 2 * capacity
        inside = inside[:, :, None] + owners // 16 * capacity + ranking
        place = (owners % 16 * WINDOW + inside).reshape(group_count, 1, TOTAL)
        plane_place = lax.dynamic_slice_in_dim(
            place, jnp.minimum(col_index, group_count - 1), 1, 0
        ).reshape(1, TOTAL)

    with jax.named_scope("columns"):
        gathered, square, precoded = lax.optimization_barrier((gathered, square, precoded))
        both = make_columns(jnp.stack([row_index, col_index]), gathered, channels, place)
        summed = both[0].astype(f32)
        for d in (1, 2, 3):
            summed = summed + along_z(both[d], d).astype(f32)
        own = summed[:user_rows].astype(bf16)
        by_row = [own] + [along_x(own, d) for d in (1, 2, 3)]
        by_col = [own] + [along_y(own, -d) for d in (1, 2, 3)]

    with jax.named_scope("schur"):
        where = jnp.stack([y_index, row_index, first_row])
        base = make_target(where, summed, precoded, slot_plane, plane_place)
        block0, block1, block2, block3, packed = make_middle(where, square, by_row, by_col, base)
        weighted = block0
        for d, block in ((1, block1), (2, block2), (3, block3)):
            weighted = weighted + along_x(block, -d).astype(f32)
        weighted_all = lax.all_gather(weighted.astype(bf16), "row")
        packed = packed.reshape(16, SHARE, TOTAL + STREAMS)
        shared = lax.all_to_all(packed, "row", 0, 0, tiled=True)
        shared = jnp.sum(shared.astype(f32), axis=0)
        share_ids = row_index * SHARE + jnp.arange(SHARE, dtype=jnp.int32)
        identity = loading * (
            share_ids[:, None] == jnp.arange(TOTAL, dtype=jnp.int32)[None, :]
        ).astype(f32)
        schur_rows = identity - shared[:, :TOTAL]
        ready = jnp.concatenate([schur_rows, shared[:, TOTAL:]], axis=1)
        ready = jnp.broadcast_to(ready[None], (16, SHARE, TOTAL + STREAMS))
        whole = lax.all_to_all(ready, "row", 0, 0, tiled=True).reshape(TOTAL, TOTAL + STREAMS)

    with jax.named_scope("users"):
        channel = make_channel(first_arg, gathered, channels, place, slots_mine)
        whole, channel = lax.optimization_barrier((whole, channel))
        pivots, users = make_solve(first_arg, whole, weighted, precoded, slot_plane)
        users_side = lax.all_to_all(users, "col", 0, 0, tiled=True)

    with jax.named_scope("update"):
        changes = make_update(
            jnp.stack([first_row, col_index]), weighted, whole, pivots, weighted_all, slot_plane
        )
        changes = [changes[0]] + [along_z(changes[d], d) for d in (1, 2, 3)]

    with jax.named_scope("signal"):
        signal_part = make_signal(users_side, channel)
        received = lax.all_to_all(signal_part, "row", 0, 0, tiled=True)
        signal = jnp.sum(received.astype(f32), axis=0)
        power = jnp.sum(signal * signal, axis=(1, 2))
        power, changes = lax.optimization_barrier((power, changes))
        power = jnp.broadcast_to(power[None, None, :], (64, 1, group_count))
        power = lax.all_to_all(power, ("row", "col"), 0, 0, tiled=True)
        total_power = jnp.sum(power, axis=(0, 1)) / (STREAMS * ANTENNAS)
        transmit = signal * lax.rsqrt(total_power + epsilon)[:, None, None]
        transmit = jnp.swapaxes(transmit, 0, 1)

    with jax.named_scope("final"):
        col_ids = col_index * user_cols + jnp.arange(user_cols, dtype=jnp.int32)
        diagonal = row_ids[:, None] == col_ids[None, :]
        full = jnp.any(slots_mine == row_ids[None, :, None], axis=2)
        gone = jnp.where(diagonal[None] & full[:, :, None], 1.0 / loading, 0.0)
        updated = []
        for g in range(group_count):
            step = (col_index - g) % 4
            add = changes[0]
            for d in (1, 2, 3):
                add = jnp.where(step == d, changes[d], add)
            updated.append(inverse[g] - gone[g] + add.astype(f32))
        updated = jnp.stack(updated, axis=0)
    return (updated, transmit)


def solution(mesh):
    placed = (
        P("grp", "row", "col"),
        P("grp", "row", "col"),
        P(None, None, ("grp", "row"), "col"),
        P(),
        P(),
        P(),
        P("grp", "col", None),
    )
    return jax.shard_map(
        local,
        mesh=mesh,
        in_specs=placed,
        out_specs=(P("grp", "row", "col"), P("row", "grp", "col")),
        check_vma=False,
    )
```

```python
import jax
import jax.numpy as jnp
from jax import lax
from jax.experimental import pallas as pl
from jax.experimental.pallas import tpu as pltpu
from jax.sharding import PartitionSpec as P

ANTENNAS = 8192
ARRIVE = 128
EPOCHS = 3
STREAMS = 256
TOTAL = ARRIVE * EPOCHS
BLOCK = 128
PANEL = 16
WINDOW = 48
SHARE = TOTAL // 16

loading = 1.0
epsilon = 1e-06
highest = lax.Precision.HIGHEST
f32 = jnp.float32
bf16 = jnp.bfloat16
VMEM = pl.BlockSpec(memory_space=pltpu.VMEM)
SMEM = pl.BlockSpec(memory_space=pltpu.SMEM)
HBM = pl.BlockSpec(memory_space=pltpu.HBM)


def params(mib=40):
    return pltpu.CompilerParams(vmem_limit_bytes=mib * 1024 * 1024)


def cost(flops, nbytes):
    return pl.CostEstimate(flops=flops, bytes_accessed=nbytes, transcendentals=0)


def dot(a, b):
    return jnp.dot(a, b, preferred_element_type=f32)


def dot_t(a, b):
    return lax.dot_general(a, b, (((1,), (1,)), ((), ())), preferred_element_type=f32)


def t_dot(a, b):
    return lax.dot_general(a, b, (((0,), (0,)), ((), ())), preferred_element_type=f32)


def halves(a):
    high = a.astype(bf16)
    return high, (a - high.astype(f32)).astype(bf16)


def split(product, a, b):
    a_high, a_low = halves(a)
    b_high, b_low = halves(b)
    return product(a_high, b_low) + product(a_low, b_high) + product(a_high, b_high)


def placing(slots_ref, first, rows):
    ids = first + lax.broadcasted_iota(jnp.int32, (rows, TOTAL), 0)
    return (ids == slots_ref[...].reshape(1, TOTAL)).astype(f32)


def choosing(place_ref, g):
    ids = lax.broadcasted_iota(jnp.int32, (16 * WINDOW, TOTAL), 0)
    return (ids == place_ref[g]).astype(f32).astype(bf16)


def start_inputs(gathered_ref, channel_ref, window_ref, held_ref, sems, row=None):
    groups, user_rows = channel_ref.shape[:2]
    copies = []
    for g in range(groups):
        start = g * 2 * EPOCHS * 6 // 16 * 16
        source = gathered_ref.at[:, pl.ds(start, WINDOW), :]
        parts = [
            pltpu.make_async_copy(channel_ref.at[g], held_ref.at[g, :user_rows], sems.at[0, g]),
            pltpu.make_async_copy(source, window_ref.at[g], sems.at[1, g]),
        ]
        if row is not None:
            source = gathered_ref.at[row, pl.ds(start, WINDOW), :]
            parts.append(
                pltpu.make_async_copy(source, held_ref.at[g, user_rows:], sems.at[2, g])
            )
        for part in parts:
            part.start()
        copies.append(parts)
    return copies


def input_scratch(groups, rows, antennas):
    return [
        pltpu.VMEM((groups, 16, WINDOW, antennas), bf16),
        pltpu.VMEM((groups, rows, antennas), bf16),
        pltpu.SemaphoreType.DMA((3, groups)),
    ]


def columns_kernel(
    row_ref, gathered_ref, channel_ref, place_ref, out_ref, window_ref, held_ref, sems
):
    groups, _, antennas = channel_ref.shape
    copies = start_inputs(gathered_ref, channel_ref, window_ref, held_ref, sems, row_ref[0])
    out_ref[groups] = jnp.zeros(out_ref.shape[1:], bf16)
    for g in range(groups):
        choose = choosing(place_ref, g)
        for copy in copies[g]:
            copy.wait()
        window = window_ref[g].reshape(16 * WINDOW, antennas)
        wide = dot_t(held_ref[g], window).astype(bf16)
        out_ref[g] = dot(wide, choose).astype(bf16)


def make_columns(row, gathered, channels, place):
    groups, user_rows, antennas = channels.shape
    return pl.pallas_call(
        columns_kernel,
        out_shape=jax.ShapeDtypeStruct((groups + 1, user_rows + WINDOW, TOTAL), bf16),
        in_specs=[SMEM, HBM, HBM, VMEM],
        out_specs=VMEM,
        scratch_shapes=input_scratch(groups, user_rows + WINDOW, antennas),
        compiler_params=params(60),
        cost_estimate=cost(4_000_000_000, 12_000_000),
        name="columns",
    )(row, gathered, channels, place)


def channel_kernel(
    first_ref, gathered_ref, channel_ref, place_ref, slots_ref, out_ref, window_ref, held_ref, sems
):
    groups, user_rows, antennas = channel_ref.shape
    copies = start_inputs(gathered_ref, channel_ref, window_ref, held_ref, sems)
    for g in range(groups):
        here = placing(slots_ref.at[g], first_ref[0], user_rows).astype(bf16)
        route = dot_t(here, choosing(place_ref, g)).astype(bf16)
        for copy in copies[g]:
            copy.wait()
        window = window_ref[g].reshape(16 * WINDOW, antennas)
        out_ref[g] = held_ref[g] + dot(route, window).astype(bf16)


def make_channel(first, gathered, channels, place, slots_mine):
    groups, user_rows, antennas = channels.shape
    return pl.pallas_call(
        channel_kernel,
        out_shape=jax.ShapeDtypeStruct(channels.shape, bf16),
        in_specs=[SMEM, HBM, HBM, VMEM, VMEM],
        out_specs=VMEM,
        scratch_shapes=input_scratch(groups, user_rows, antennas),
        compiler_params=params(60),
        cost_estimate=cost(4_000_000_000, 14_000_000),
        name="channel",
    )(first, gathered, channels, place, slots_mine)


def pieces_kernel(x_ref, inverse_ref, out0, out1, out2, out3):
    size = out0.shape[-1]
    for d, out in enumerate([out0, out1, out2, out3]):
        start = pl.multiple_of((x_ref[0] + d) % 4 * size, size)
        out[...] = inverse_ref[:, :, pl.ds(start, size)].astype(bf16)


def make_pieces(x, inverse):
    groups, user_rows = inverse.shape[:2]
    shape = jax.ShapeDtypeStruct((groups, user_rows, user_rows), bf16)
    return pl.pallas_call(
        pieces_kernel,
        out_shape=(shape,) * 4,
        in_specs=[SMEM, VMEM],
        out_specs=(VMEM,) * 4,
        compiler_params=params(16),
        cost_estimate=cost(100_000_000, 5_000_000),
        name="pieces",
    )(x, inverse)


def target_kernel(where_ref, summed_ref, precoded_ref, slots_ref, place_ref, base_out):
    row, first = where_ref[1], where_ref[2]
    user_rows = precoded_ref.shape[0]
    ids = row * WINDOW + lax.broadcasted_iota(jnp.int32, (WINDOW, TOTAL), 0)
    choose = (ids == place_ref[...]).astype(f32).astype(bf16)
    base_out[:, :TOTAL] = -t_dot(choose, summed_ref[user_rows:].astype(bf16))
    border = summed_ref[:user_rows] - placing(slots_ref, first, user_rows)
    base_out[:, TOTAL:] = split(t_dot, border, precoded_ref[...])


def make_target(where, summed, precoded, slot_plane, place_plane):
    return pl.pallas_call(
        target_kernel,
        out_shape=jax.ShapeDtypeStruct((TOTAL, TOTAL + STREAMS), f32),
        in_specs=[SMEM] + [VMEM] * 4,
        out_specs=VMEM,
        compiler_params=params(16),
        cost_estimate=cost(1_000_000_000, 2_000_000),
        name="target",
    )(where, summed, precoded, slot_plane, place_plane)


def middle_kernel(
    where_ref, square_ref, own_ref, row1_ref, row2_ref, row3_ref, col1_ref, col2_ref, col3_ref,
    base_ref, first_out, block1_out, block2_out, block3_out, packed_out,
):
    y = where_ref[0]
    by_row = [own_ref, row1_ref, row2_ref, row3_ref]
    by_col = [own_ref, col1_ref, col2_ref, col3_ref]
    outs = [first_out, block1_out, block2_out, block3_out]
    schur = base_ref[:, :TOTAL]
    for d in range(4):
        block = dot(square_ref[y, d], own_ref[...])
        for e in range(1, 4):
            block += dot(square_ref[(y + e) % 4, d], by_col[e][...])
        low = block.astype(bf16)
        outs[d][...] = block if d == 0 else low
        schur += t_dot(by_row[d][...], low)
    packed_out[:, :TOTAL] = schur.astype(bf16)
    packed_out[:, TOTAL:] = base_ref[:, TOTAL:].astype(bf16)


def make_middle(where, square, by_row, by_col, base):
    shape = by_row[0].shape
    return pl.pallas_call(
        middle_kernel,
        out_shape=(
            jax.ShapeDtypeStruct(shape, f32),
            jax.ShapeDtypeStruct(shape, bf16),
            jax.ShapeDtypeStruct(shape, bf16),
            jax.ShapeDtypeStruct(shape, bf16),
            jax.ShapeDtypeStruct((TOTAL, TOTAL + STREAMS), bf16),
        ),
        in_specs=[SMEM] + [VMEM] * 9,
        out_specs=(VMEM,) * 5,
        compiler_params=params(),
        cost_estimate=cost(2_000_000_000, 8_000_000),
        name="middle",
    )(where, square, *by_row, *by_col[1:], base)


def ready_kernel(row_ref, shared_ref, out_ref):
    total = jnp.sum(shared_ref[...].astype(f32), axis=0)
    ids = row_ref[0] * SHARE + lax.broadcasted_iota(jnp.int32, (SHARE, TOTAL), 0)
    lanes = lax.broadcasted_iota(jnp.int32, (SHARE, TOTAL), 1)
    schur = loading * (ids == lanes).astype(f32) - total[:, :TOTAL]
    for n in range(out_ref.shape[0]):
        out_ref[n, :, :TOTAL] = schur
        out_ref[n, :, TOTAL:] = total[:, TOTAL:]


def make_ready(row, shared):
    return pl.pallas_call(
        ready_kernel,
        out_shape=jax.ShapeDtypeStruct(shared.shape, f32),
        in_specs=[SMEM, VMEM],
        out_specs=VMEM,
        compiler_params=params(16),
        cost_estimate=cost(500_000_000, 2_000_000),
        name="ready",
    )(row, shared)


def invert_block(a):
    lane = lax.broadcasted_iota(jnp.int32, (1, BLOCK), 1)
    sub = lax.broadcasted_iota(jnp.int32, (PANEL, 1), 0)
    for k in range(0, BLOCK, PANEL):
        inside = (lane >= k) & (lane < k + PANEL)
        rows = a[k:k + PANEL, :]
        cols = [
            jnp.broadcast_to(rows[:, k + j:k + j + 1], (PANEL, BLOCK)) for j in range(PANEL)
        ]
        rows = jnp.where(inside, (lane - k == sub).astype(f32), rows)
        for i in range(PANEL):
            scale = 1.0 / cols[i][i:i + 1, :]
            factor = cols[i] - (sub == i).astype(f32)
            for j in range(i + 1, PANEL):
                cols[j] = cols[j] - factor * (cols[j][i:i + 1, :] * scale)
            rows = rows - factor * (rows[i:i + 1, :] * scale)
        rest = jnp.where(inside, 0.0, a)
        for i in range(PANEL):
            rest = rest - a[:, k + i:k + i + 1] * rows[i:i + 1, :]
        pieces = [rest[:k]] if k else []
        pieces.append(rows)
        if k + PANEL < BLOCK:
            pieces.append(rest[k + PANEL:])
        a = jnp.concatenate(pieces, axis=0)
    return a


def solve_kernel(
    first_ref, whole_ref, weighted_ref, precoded_ref, slots_ref, pivots_ref, users_ref, work_ref
):
    work_ref[...] = whole_ref[...]

    @pl.loop(0, EPOCHS)
    def _(b):
        start = pl.ds(pl.multiple_of(b * BLOCK, BLOCK), BLOCK)
        pivots_ref[b] = invert_block(work_ref[start, start])
        for k in range(EPOCHS):
            here = slice(k * BLOCK, (k + 1) * BLOCK)

            @pl.when(b == k)
            def _():
                scaled = split(dot, pivots_ref[k], work_ref[here, here.stop:])
                work_ref[here, here.stop:] = scaled
                if k + 1 < EPOCHS:
                    below = work_ref[here.stop:, here]
                    work_ref[here.stop:, here.stop:] -= split(dot, below, scaled)

    effect = work_ref[TOTAL - BLOCK:, TOTAL:]
    for b in range(EPOCHS - 2, -1, -1):
        here = slice(b * BLOCK, (b + 1) * BLOCK)
        part = work_ref[here, TOTAL:] - split(dot, work_ref[here, here.stop:TOTAL], effect)
        effect = jnp.concatenate([part, effect], axis=0)
    place = placing(slots_ref, first_ref[0], weighted_ref.shape[0])
    kept = 1.0 - jnp.sum(place, axis=1, keepdims=True)
    users = precoded_ref[...] * kept + split(dot, weighted_ref[...] - place, effect)
    for z in range(4):
        users_ref[z] = users.astype(bf16)


def make_solve(first, whole, weighted, precoded, slot_plane):
    return pl.pallas_call(
        solve_kernel,
        out_shape=(
            jax.ShapeDtypeStruct((EPOCHS, BLOCK, BLOCK), f32),
            jax.ShapeDtypeStruct((4, weighted.shape[0], STREAMS), bf16),
        ),
        in_specs=[SMEM] + [VMEM] * 4,
        out_specs=(VMEM,) * 2,
        scratch_shapes=[pltpu.VMEM(whole.shape, f32)],
        compiler_params=params(),
        cost_estimate=cost(14_000_000_000, 4_000_000),
        name="solve",
    )(first, whole, weighted, precoded, slot_plane)


def inverse_of(whole_ref, pivots_ref, inv_ref):
    inv_ref[...] = whole_ref[:, :TOTAL]
    row_id = lax.broadcasted_iota(jnp.int32, (TOTAL, BLOCK), 0)
    lane_id = lax.broadcasted_iota(jnp.int32, (TOTAL, BLOCK), 1)
    for b in range(EPOCHS):
        here = slice(b * BLOCK, (b + 1) * BLOCK)
        inside = (row_id >= here.start) & (row_id < here.stop)
        rest = jnp.where(inside, 0.0, inv_ref[:, here])
        inv_ref[:, here] = (row_id == lane_id + here.start).astype(f32)
        scaled = split(dot, pivots_ref[b], inv_ref[here, :])
        inv_ref[here, :] = jnp.zeros((BLOCK, TOTAL), f32)
        inv_ref[...] = inv_ref[...] - split(dot, rest, scaled)
        inv_ref[here, :] = scaled


def signal_kernel(users_ref, channel_ref, out_ref, held_ref, sems):
    groups, _, antennas = channel_ref.shape
    tile = antennas // 2
    copies = []
    for g in range(groups):
        for m in range(0, antennas, tile):
            part = t_dot(users_ref[g], channel_ref[g, :, m:m + tile]).astype(bf16)
            held_ref[g, :, :, m:m + tile] = part.reshape(16, STREAMS // 16, tile)
        copy = pltpu.make_async_copy(held_ref.at[g], out_ref.at[:, g], sems.at[g])
        copy.start()
        copies.append(copy)
    for copy in copies:
        copy.wait()


def make_signal(users_side, channel):
    groups, _, antennas = channel.shape
    each = STREAMS // 16
    return pl.pallas_call(
        signal_kernel,
        out_shape=jax.ShapeDtypeStruct((16, groups, each, antennas), bf16),
        in_specs=[VMEM, VMEM],
        out_specs=HBM,
        scratch_shapes=[
            pltpu.VMEM((groups, 16, each, antennas), bf16),
            pltpu.SemaphoreType.DMA((groups,)),
        ],
        compiler_params=params(),
        cost_estimate=cost(800_000_000, 7_000_000),
        name="signal",
    )(users_side, channel)


def update_kernel(
    where_ref, weighted_ref, whole_ref, pivots_ref, all_ref, slots_ref,
    out0, out1, out2, out3, inv_ref, held_ref, sems,
):
    first, plane = where_ref[0], where_ref[1]
    user_rows = weighted_ref.shape[0]
    inverse_of(whole_ref, pivots_ref, inv_ref)
    border = weighted_ref[...] - placing(slots_ref, first, user_rows)
    half = split(dot, border, inv_ref[...]).astype(bf16)
    copies = []
    for d, out in enumerate([out0, out1, out2, out3]):
        z = (plane + d) % 4
        there = all_ref[pl.ds(4 * z, 4)].reshape(4 * user_rows, TOTAL).astype(f32)
        there = there - placing(slots_ref, 4 * user_rows * z, 4 * user_rows)
        held_ref[d] = dot_t(half, there.astype(bf16)).astype(bf16)
        copy = pltpu.make_async_copy(held_ref.at[d], out, sems.at[d])
        copy.start()
        copies.append(copy)
    for copy in copies:
        copy.wait()


def make_update(where, weighted, whole, pivots, weighted_all, slot_plane):
    user_rows = weighted.shape[0]
    return pl.pallas_call(
        update_kernel,
        out_shape=(jax.ShapeDtypeStruct((user_rows, 4 * user_rows), bf16),) * 4,
        in_specs=[SMEM] + [VMEM] * 5,
        out_specs=(HBM,) * 4,
        scratch_shapes=[
            pltpu.VMEM((TOTAL, TOTAL), f32),
            pltpu.VMEM((4, user_rows, 4 * user_rows), bf16),
            pltpu.SemaphoreType.DMA((4,)),
        ],
        compiler_params=params(),
        cost_estimate=cost(1_500_000_000, 8_000_000),
        name="update",
    )(where, weighted, whole, pivots, weighted_all, slot_plane)


def local(channels, inverse, arrivals, arrival_cell, cell_owner, slots, symbols):
    group_count, user_rows, antennas = channels.shape
    user_cols = inverse.shape[2]
    capacity = arrivals.shape[2]
    cell_count = cell_owner.shape[0]
    grp_index = lax.axis_index("grp")
    row_index = lax.axis_index("row")
    col_index = lax.axis_index("col")
    y_index, x_index = row_index // 4, row_index % 4

    def along_x(value, step):
        pairs = [(4 * y + x, 4 * y + (x + step) % 4) for y in range(4) for x in range(4)]
        return lax.ppermute(value, "row", pairs)

    def along_y(value, step):
        pairs = [(4 * y + x, 4 * ((y + step) % 4) + x) for y in range(4) for x in range(4)]
        return lax.ppermute(value, "row", pairs)

    def along_z(value, step):
        return lax.ppermute(value, "col", [(z, (z + step) % 4) for z in range(4)])

    def to_planes(value):
        padded = jnp.concatenate([value, jnp.zeros_like(value[:1])], axis=0)
        return lax.all_to_all(padded, "col", 0, 0, tiled=True)

    first_group = grp_index * group_count
    other_first = (1 - grp_index) * group_count
    first_row = row_index * user_rows
    first_arg = first_row.reshape(1)

    with jax.named_scope("newcomers"):
        mine = lax.dynamic_slice_in_dim(arrivals, first_group, group_count, 0)
        theirs = lax.dynamic_slice_in_dim(arrivals, other_first, group_count, 0)
        swapped = lax.ppermute(theirs, "grp", [(0, 1), (1, 0)])
        from_0 = jnp.where(grp_index == 0, mine, swapped)
        from_1 = jnp.where(grp_index == 0, swapped, mine)
        chunk = jnp.stack([from_0, from_1], axis=2)
        per_group = EPOCHS * 2 * capacity
        chunk = chunk.reshape(group_count * per_group, antennas)
        chunk = jnp.pad(chunk, ((0, 112 - group_count * per_group), (0, 0)))
        gathered = lax.all_gather(chunk, "row")

    with jax.named_scope("planes"):
        pieces = list(make_pieces(x_index.reshape(1), inverse))
        for d in (1, 2, 3):
            pieces[d] = along_x(pieces[d], d)
        square = to_planes(jnp.stack(pieces, axis=1))
        symbol_part = jnp.einsum(
            "grc,gcs->grs", inverse, symbols.astype(f32), precision=highest
        )
        precoded = jnp.sum(to_planes(symbol_part), axis=0)

    plane_group = first_group + jnp.minimum(col_index, group_count - 1)
    slot_plane = lax.dynamic_slice_in_dim(slots, plane_group, 1, 0).reshape(1, TOTAL)
    row_ids = first_row + jnp.arange(user_rows, dtype=jnp.int32)

    cells_mine = lax.dynamic_slice_in_dim(arrival_cell, first_group, group_count, 0)[..., 0]
    slots_mine = lax.dynamic_slice_in_dim(slots, first_group, group_count, 0)
    slots_mine = slots_mine.reshape(group_count, 1, TOTAL)
    cell_table = (cells_mine[..., None] == jnp.arange(cell_count, dtype=jnp.int32)).astype(
        jnp.int32
    )
    owners = jnp.sum(cell_table * cell_owner, axis=-1)
    arrival_order = jnp.arange(ARRIVE, dtype=jnp.int32)
    earlier = (cells_mine[..., :, None] == cells_mine[..., None, :]) & (
        arrival_order[:, None] < arrival_order[None, :]
    )
    ranking = jnp.sum(earlier.astype(jnp.int32), axis=-2)
    with jax.named_scope("places"):
        offset = jnp.arange(group_count, dtype=jnp.int32) * per_group % 16
        epoch = jnp.arange(EPOCHS, dtype=jnp.int32)
        inside = offset[:, None] + epoch[None, :] * 2 * capacity
        inside = inside[:, :, None] + owners // 16 * capacity + ranking
        place = (owners % 16 * WINDOW + inside).reshape(group_count, 1, TOTAL)
        plane_place = lax.dynamic_slice_in_dim(
            place, jnp.minimum(col_index, group_count - 1), 1, 0
        ).reshape(1, TOTAL)

    with jax.named_scope("columns"):
        gathered, square, precoded = lax.optimization_barrier((gathered, square, precoded))
        both = make_columns(row_index.reshape(1), gathered, channels, place)
        both = lax.all_to_all(both, "col", 0, 0, tiled=True)
        summed = jnp.sum(both.astype(f32), axis=0)
        own = summed[:user_rows].astype(bf16)
        by_row = [own] + [along_x(own, d) for d in (1, 2, 3)]
        by_col = [own] + [along_y(own, -d) for d in (1, 2, 3)]

    with jax.named_scope("schur"):
        where = jnp.stack([y_index, row_index, first_row])
        base = make_target(where, summed, precoded, slot_plane, plane_place)
        block0, block1, block2, block3, packed = make_middle(where, square, by_row, by_col, base)
        weighted = block0
        for d, block in ((1, block1), (2, block2), (3, block3)):
            weighted = weighted + along_x(block, -d).astype(f32)
        weighted_all = lax.all_gather(weighted.astype(bf16), "row")
        packed = packed.reshape(16, SHARE, TOTAL + STREAMS)
        shared = lax.all_to_all(packed, "row", 0, 0, tiled=True)
        ready = make_ready(row_index.reshape(1), shared)
        whole = lax.all_to_all(ready, "row", 0, 0, tiled=True).reshape(TOTAL, TOTAL + STREAMS)

    with jax.named_scope("users"):
        channel = make_channel(first_arg, gathered, channels, place, slots_mine)
        whole, channel = lax.optimization_barrier((whole, channel))
        pivots, users = make_solve(first_arg, whole, weighted, precoded, slot_plane)
        users_side = lax.all_to_all(users, "col", 0, 0, tiled=True)

    with jax.named_scope("update"):
        changes = make_update(
            jnp.stack([first_row, col_index]), weighted, whole, pivots, weighted_all, slot_plane
        )
        changes = [changes[0]] + [along_z(changes[d], d) for d in (1, 2, 3)]

    with jax.named_scope("signal"):
        signal_part = make_signal(users_side, channel)
        received = lax.all_to_all(signal_part, "row", 0, 0, tiled=True)
        signal = jnp.sum(received.astype(f32), axis=0)
        power = jnp.sum(signal * signal, axis=(1, 2))
        power, changes = lax.optimization_barrier((power, changes))
        power = jnp.broadcast_to(power[None, None, :], (64, 1, group_count))
        power = lax.all_to_all(power, ("row", "col"), 0, 0, tiled=True)
        total_power = jnp.sum(power, axis=(0, 1)) / (STREAMS * ANTENNAS)
        transmit = signal * lax.rsqrt(total_power + epsilon)[:, None, None]
        transmit = jnp.swapaxes(transmit, 0, 1)

    with jax.named_scope("final"):
        col_ids = col_index * user_cols + jnp.arange(user_cols, dtype=jnp.int32)
        diagonal = row_ids[:, None] == col_ids[None, :]
        full = jnp.any(slots_mine == row_ids[None, :, None], axis=2)
        gone = jnp.where(diagonal[None] & full[:, :, None], 1.0 / loading, 0.0)
        updated = []
        for g in range(group_count):
            step = (col_index - g) % 4
            add = changes[0]
            for d in (1, 2, 3):
                add = jnp.where(step == d, changes[d], add)
            updated.append(inverse[g] - gone[g] + add.astype(f32))
        updated = jnp.stack(updated, axis=0)
    return (updated, transmit)


def solution(mesh):
    placed = (
        P("grp", "row", "col"),
        P("grp", "row", "col"),
        P(None, None, ("grp", "row"), "col"),
        P(),
        P(),
        P(),
        P("grp", "col", None),
    )
    return jax.shard_map(
        local,
        mesh=mesh,
        in_specs=placed,
        out_specs=(P("grp", "row", "col"), P("row", "grp", "col")),
        check_vma=False,
    )
```

```python
import jax
import jax.numpy as jnp
from jax import lax
from jax.experimental import pallas as pl
from jax.experimental.pallas import tpu as pltpu
from jax.sharding import PartitionSpec as P

ANTENNAS = 8192
ARRIVE = 128
EPOCHS = 3
STREAMS = 256
TOTAL = ARRIVE * EPOCHS
BLOCK = 128
PANEL = 16
WINDOW = 48
SHARE = TOTAL // 16

loading = 1.0
epsilon = 1e-06
highest = lax.Precision.HIGHEST
f32 = jnp.float32
bf16 = jnp.bfloat16
VMEM = pl.BlockSpec(memory_space=pltpu.VMEM)
SMEM = pl.BlockSpec(memory_space=pltpu.SMEM)
HBM = pl.BlockSpec(memory_space=pltpu.HBM)


def params(mib=40):
    return pltpu.CompilerParams(vmem_limit_bytes=mib * 1024 * 1024)


def cost(flops, nbytes):
    return pl.CostEstimate(flops=flops, bytes_accessed=nbytes, transcendentals=0)


def dot(a, b):
    return jnp.dot(a, b, preferred_element_type=f32)


def dot_t(a, b):
    return lax.dot_general(a, b, (((1,), (1,)), ((), ())), preferred_element_type=f32)


def t_dot(a, b):
    return lax.dot_general(a, b, (((0,), (0,)), ((), ())), preferred_element_type=f32)


def halves(a):
    high = a.astype(bf16)
    return high, (a - high.astype(f32)).astype(bf16)


def split(product, a, b):
    a_high, a_low = halves(a)
    b_high, b_low = halves(b)
    return product(a_high, b_low) + product(a_low, b_high) + product(a_high, b_high)


def placing(slots_ref, first, rows):
    ids = first + lax.broadcasted_iota(jnp.int32, (rows, TOTAL), 0)
    return (ids == slots_ref[...].reshape(1, TOTAL)).astype(f32)


def choosing(place_ref, g):
    ids = lax.broadcasted_iota(jnp.int32, (16 * WINDOW, TOTAL), 0)
    return (ids == place_ref[g]).astype(f32).astype(bf16)


def start_inputs(gathered_ref, channel_ref, window_ref, held_ref, sems, row=None):
    groups, user_rows = channel_ref.shape[:2]
    copies = []
    for g in range(groups):
        start = g * 2 * EPOCHS * 6 // 16 * 16
        source = gathered_ref.at[:, pl.ds(start, WINDOW), :]
        parts = [
            pltpu.make_async_copy(channel_ref.at[g], held_ref.at[g, :user_rows], sems.at[0, g]),
            pltpu.make_async_copy(source, window_ref.at[g], sems.at[1, g]),
        ]
        if row is not None:
            source = gathered_ref.at[row, pl.ds(start, WINDOW), :]
            parts.append(
                pltpu.make_async_copy(source, held_ref.at[g, user_rows:], sems.at[2, g])
            )
        for part in parts:
            part.start()
        copies.append(parts)
    return copies


def input_scratch(groups, rows, antennas):
    return [
        pltpu.VMEM((groups, 16, WINDOW, antennas), bf16),
        pltpu.VMEM((groups, rows, antennas), bf16),
        pltpu.SemaphoreType.DMA((3, groups)),
    ]


def columns_kernel(
    row_ref, gathered_ref, channel_ref, place_ref, out_ref, window_ref, held_ref, sems
):
    groups, _, antennas = channel_ref.shape
    copies = start_inputs(gathered_ref, channel_ref, window_ref, held_ref, sems, row_ref[0])
    out_ref[groups] = jnp.zeros(out_ref.shape[1:], bf16)
    for g in range(groups):
        choose = choosing(place_ref, g)
        for copy in copies[g]:
            copy.wait()
        window = window_ref[g].reshape(16 * WINDOW, antennas)
        wide = dot_t(held_ref[g], window).astype(bf16)
        out_ref[g] = dot(wide, choose).astype(bf16)


def make_columns(row, gathered, channels, place):
    groups, user_rows, antennas = channels.shape
    return pl.pallas_call(
        columns_kernel,
        out_shape=jax.ShapeDtypeStruct((groups + 1, user_rows + WINDOW, TOTAL), bf16),
        in_specs=[SMEM, HBM, HBM, VMEM],
        out_specs=VMEM,
        scratch_shapes=input_scratch(groups, user_rows + WINDOW, antennas),
        compiler_params=params(60),
        cost_estimate=cost(4_000_000_000, 12_000_000),
        name="columns",
    )(row, gathered, channels, place)


def channel_kernel(
    first_ref, gathered_ref, channel_ref, place_ref, slots_ref, out_ref, window_ref, held_ref, sems
):
    groups, user_rows, antennas = channel_ref.shape
    copies = start_inputs(gathered_ref, channel_ref, window_ref, held_ref, sems)
    for g in range(groups):
        here = placing(slots_ref.at[g], first_ref[0], user_rows).astype(bf16)
        route = dot_t(here, choosing(place_ref, g)).astype(bf16)
        for copy in copies[g]:
            copy.wait()
        window = window_ref[g].reshape(16 * WINDOW, antennas)
        out_ref[g] = held_ref[g] + dot(route, window).astype(bf16)


def make_channel(first, gathered, channels, place, slots_mine):
    groups, user_rows, antennas = channels.shape
    return pl.pallas_call(
        channel_kernel,
        out_shape=jax.ShapeDtypeStruct(channels.shape, bf16),
        in_specs=[SMEM, HBM, HBM, VMEM, VMEM],
        out_specs=VMEM,
        scratch_shapes=input_scratch(groups, user_rows, antennas),
        compiler_params=params(60),
        cost_estimate=cost(4_000_000_000, 14_000_000),
        name="channel",
    )(first, gathered, channels, place, slots_mine)


def pieces_kernel(x_ref, inverse_ref, out0, out1, out2, out3):
    size = out0.shape[-1]
    for d, out in enumerate([out0, out1, out2, out3]):
        start = pl.multiple_of((x_ref[0] + d) % 4 * size, size)
        out[...] = inverse_ref[:, :, pl.ds(start, size)].astype(bf16)


def make_pieces(x, inverse):
    groups, user_rows = inverse.shape[:2]
    shape = jax.ShapeDtypeStruct((groups, user_rows, user_rows), bf16)
    return pl.pallas_call(
        pieces_kernel,
        out_shape=(shape,) * 4,
        in_specs=[SMEM, VMEM],
        out_specs=(VMEM,) * 4,
        compiler_params=params(16),
        cost_estimate=cost(100_000_000, 5_000_000),
        name="pieces",
    )(x, inverse)


def target_kernel(where_ref, summed_ref, precoded_ref, slots_ref, place_ref, base_out):
    row, first = where_ref[1], where_ref[2]
    user_rows = precoded_ref.shape[0]
    ids = row * WINDOW + lax.broadcasted_iota(jnp.int32, (WINDOW, TOTAL), 0)
    choose = (ids == place_ref[...]).astype(f32).astype(bf16)
    base_out[:, :TOTAL] = -t_dot(choose, summed_ref[user_rows:].astype(bf16))
    border = summed_ref[:user_rows] - placing(slots_ref, first, user_rows)
    base_out[:, TOTAL:] = split(t_dot, border, precoded_ref[...])


def make_target(where, summed, precoded, slot_plane, place_plane):
    return pl.pallas_call(
        target_kernel,
        out_shape=jax.ShapeDtypeStruct((TOTAL, TOTAL + STREAMS), f32),
        in_specs=[SMEM] + [VMEM] * 4,
        out_specs=VMEM,
        compiler_params=params(16),
        cost_estimate=cost(1_000_000_000, 2_000_000),
        name="target",
    )(where, summed, precoded, slot_plane, place_plane)


def middle_kernel(
    where_ref, square_ref, own_ref, row1_ref, row2_ref, row3_ref, col1_ref, col2_ref, col3_ref,
    base_ref, first_out, block1_out, block2_out, block3_out, packed_out,
):
    y = where_ref[0]
    by_row = [own_ref, row1_ref, row2_ref, row3_ref]
    by_col = [own_ref, col1_ref, col2_ref, col3_ref]
    outs = [first_out, block1_out, block2_out, block3_out]
    schur = base_ref[:, :TOTAL]
    for d in range(4):
        block = dot(square_ref[y, d], own_ref[...])
        for e in range(1, 4):
            block += dot(square_ref[(y + e) % 4, d], by_col[e][...])
        low = block.astype(bf16)
        outs[d][...] = block if d == 0 else low
        schur += t_dot(by_row[d][...], low)
    packed_out[:, :TOTAL] = schur.astype(bf16)
    packed_out[:, TOTAL:] = base_ref[:, TOTAL:].astype(bf16)


def make_middle(where, square, by_row, by_col, base):
    shape = by_row[0].shape
    return pl.pallas_call(
        middle_kernel,
        out_shape=(
            jax.ShapeDtypeStruct(shape, f32),
            jax.ShapeDtypeStruct(shape, bf16),
            jax.ShapeDtypeStruct(shape, bf16),
            jax.ShapeDtypeStruct(shape, bf16),
            jax.ShapeDtypeStruct((TOTAL, TOTAL + STREAMS), bf16),
        ),
        in_specs=[SMEM] + [VMEM] * 9,
        out_specs=(VMEM,) * 5,
        compiler_params=params(),
        cost_estimate=cost(2_000_000_000, 8_000_000),
        name="middle",
    )(where, square, *by_row, *by_col[1:], base)


def invert_block(a):
    lane = lax.broadcasted_iota(jnp.int32, (1, BLOCK), 1)
    sub = lax.broadcasted_iota(jnp.int32, (PANEL, 1), 0)
    for k in range(0, BLOCK, PANEL):
        inside = (lane >= k) & (lane < k + PANEL)
        rows = a[k:k + PANEL, :]
        cols = [
            jnp.broadcast_to(rows[:, k + j:k + j + 1], (PANEL, BLOCK)) for j in range(PANEL)
        ]
        rows = jnp.where(inside, (lane - k == sub).astype(f32), rows)
        for i in range(PANEL):
            scale = 1.0 / cols[i][i:i + 1, :]
            factor = cols[i] - (sub == i).astype(f32)
            for j in range(i + 1, PANEL):
                cols[j] = cols[j] - factor * (cols[j][i:i + 1, :] * scale)
            rows = rows - factor * (rows[i:i + 1, :] * scale)
        rest = jnp.where(inside, 0.0, a)
        for i in range(PANEL):
            rest = rest - a[:, k + i:k + i + 1] * rows[i:i + 1, :]
        pieces = [rest[:k]] if k else []
        pieces.append(rows)
        if k + PANEL < BLOCK:
            pieces.append(rest[k + PANEL:])
        a = jnp.concatenate(pieces, axis=0)
    return a


def solve_kernel(
    first_ref, whole_ref, weighted_ref, precoded_ref, slots_ref, pivots_ref, users_ref, work_ref
):
    work_ref[...] = whole_ref[...]

    @pl.loop(0, EPOCHS)
    def _(b):
        start = pl.ds(pl.multiple_of(b * BLOCK, BLOCK), BLOCK)
        pivots_ref[b] = invert_block(work_ref[start, start])
        for k in range(EPOCHS):
            here = slice(k * BLOCK, (k + 1) * BLOCK)

            @pl.when(b == k)
            def _():
                scaled = split(dot, pivots_ref[k], work_ref[here, here.stop:])
                work_ref[here, here.stop:] = scaled
                if k + 1 < EPOCHS:
                    below = work_ref[here.stop:, here]
                    work_ref[here.stop:, here.stop:] -= split(dot, below, scaled)

    effect = work_ref[TOTAL - BLOCK:, TOTAL:]
    for b in range(EPOCHS - 2, -1, -1):
        here = slice(b * BLOCK, (b + 1) * BLOCK)
        part = work_ref[here, TOTAL:] - split(dot, work_ref[here, here.stop:TOTAL], effect)
        effect = jnp.concatenate([part, effect], axis=0)
    place = placing(slots_ref, first_ref[0], weighted_ref.shape[0])
    kept = 1.0 - jnp.sum(place, axis=1, keepdims=True)
    users = precoded_ref[...] * kept + split(dot, weighted_ref[...] - place, effect)
    for z in range(4):
        users_ref[z] = users.astype(bf16)


def make_solve(first, whole, weighted, precoded, slot_plane):
    return pl.pallas_call(
        solve_kernel,
        out_shape=(
            jax.ShapeDtypeStruct((EPOCHS, BLOCK, BLOCK), f32),
            jax.ShapeDtypeStruct((4, weighted.shape[0], STREAMS), bf16),
        ),
        in_specs=[SMEM] + [VMEM] * 4,
        out_specs=(VMEM,) * 2,
        scratch_shapes=[pltpu.VMEM(whole.shape, f32)],
        compiler_params=params(),
        cost_estimate=cost(14_000_000_000, 4_000_000),
        name="solve",
    )(first, whole, weighted, precoded, slot_plane)


def inverse_of(whole_ref, pivots_ref, inv_ref):
    inv_ref[...] = whole_ref[:, :TOTAL]
    row_id = lax.broadcasted_iota(jnp.int32, (TOTAL, BLOCK), 0)
    lane_id = lax.broadcasted_iota(jnp.int32, (TOTAL, BLOCK), 1)
    for b in range(EPOCHS):
        here = slice(b * BLOCK, (b + 1) * BLOCK)
        inside = (row_id >= here.start) & (row_id < here.stop)
        rest = jnp.where(inside, 0.0, inv_ref[:, here])
        inv_ref[:, here] = (row_id == lane_id + here.start).astype(f32)
        scaled = split(dot, pivots_ref[b], inv_ref[here, :])
        inv_ref[here, :] = jnp.zeros((BLOCK, TOTAL), f32)
        inv_ref[...] = inv_ref[...] - split(dot, rest, scaled)
        inv_ref[here, :] = scaled


def signal_kernel(users_ref, channel_ref, out_ref, held_ref, sems):
    groups, _, antennas = channel_ref.shape
    tile = antennas // 2
    copies = []
    for g in range(groups):
        for m in range(0, antennas, tile):
            part = t_dot(users_ref[g], channel_ref[g, :, m:m + tile]).astype(bf16)
            held_ref[g, :, :, m:m + tile] = part.reshape(16, STREAMS // 16, tile)
        copy = pltpu.make_async_copy(held_ref.at[g], out_ref.at[:, g], sems.at[g])
        copy.start()
        copies.append(copy)
    for copy in copies:
        copy.wait()


def make_signal(users_side, channel):
    groups, _, antennas = channel.shape
    each = STREAMS // 16
    return pl.pallas_call(
        signal_kernel,
        out_shape=jax.ShapeDtypeStruct((16, groups, each, antennas), bf16),
        in_specs=[VMEM, VMEM],
        out_specs=HBM,
        scratch_shapes=[
            pltpu.VMEM((groups, 16, each, antennas), bf16),
            pltpu.SemaphoreType.DMA((groups,)),
        ],
        compiler_params=params(),
        cost_estimate=cost(800_000_000, 7_000_000),
        name="signal",
    )(users_side, channel)


def update_kernel(
    where_ref, weighted_ref, whole_ref, pivots_ref, all_ref, slots_ref,
    out0, out1, out2, out3, inv_ref, held_ref, sems,
):
    first, plane = where_ref[0], where_ref[1]
    user_rows = weighted_ref.shape[0]
    inverse_of(whole_ref, pivots_ref, inv_ref)
    border = weighted_ref[...] - placing(slots_ref, first, user_rows)
    half = split(dot, border, inv_ref[...]).astype(bf16)
    copies = []
    for d, out in enumerate([out0, out1, out2, out3]):
        z = (plane + d) % 4
        there = all_ref[pl.ds(4 * z, 4)].reshape(4 * user_rows, TOTAL).astype(f32)
        there = there - placing(slots_ref, 4 * user_rows * z, 4 * user_rows)
        held_ref[d] = dot_t(half, there.astype(bf16)).astype(bf16)
        copy = pltpu.make_async_copy(held_ref.at[d], out, sems.at[d])
        copy.start()
        copies.append(copy)
    for copy in copies:
        copy.wait()


def make_update(where, weighted, whole, pivots, weighted_all, slot_plane):
    user_rows = weighted.shape[0]
    return pl.pallas_call(
        update_kernel,
        out_shape=(jax.ShapeDtypeStruct((user_rows, 4 * user_rows), bf16),) * 4,
        in_specs=[SMEM] + [VMEM] * 5,
        out_specs=(HBM,) * 4,
        scratch_shapes=[
            pltpu.VMEM((TOTAL, TOTAL), f32),
            pltpu.VMEM((4, user_rows, 4 * user_rows), bf16),
            pltpu.SemaphoreType.DMA((4,)),
        ],
        compiler_params=params(),
        cost_estimate=cost(1_500_000_000, 8_000_000),
        name="update",
    )(where, weighted, whole, pivots, weighted_all, slot_plane)


def local(channels, inverse, arrivals, arrival_cell, cell_owner, slots, symbols):
    group_count, user_rows, antennas = channels.shape
    user_cols = inverse.shape[2]
    capacity = arrivals.shape[2]
    cell_count = cell_owner.shape[0]
    grp_index = lax.axis_index("grp")
    row_index = lax.axis_index("row")
    col_index = lax.axis_index("col")
    y_index, x_index = row_index // 4, row_index % 4

    def along_x(value, step):
        pairs = [(4 * y + x, 4 * y + (x + step) % 4) for y in range(4) for x in range(4)]
        return lax.ppermute(value, "row", pairs)

    def along_y(value, step):
        pairs = [(4 * y + x, 4 * ((y + step) % 4) + x) for y in range(4) for x in range(4)]
        return lax.ppermute(value, "row", pairs)

    def along_z(value, step):
        return lax.ppermute(value, "col", [(z, (z + step) % 4) for z in range(4)])

    def to_planes(value):
        padded = jnp.concatenate([value, jnp.zeros_like(value[:1])], axis=0)
        return lax.all_to_all(padded, "col", 0, 0, tiled=True)

    first_group = grp_index * group_count
    other_first = (1 - grp_index) * group_count
    first_row = row_index * user_rows
    first_arg = first_row.reshape(1)

    with jax.named_scope("newcomers"):
        mine = lax.dynamic_slice_in_dim(arrivals, first_group, group_count, 0)
        theirs = lax.dynamic_slice_in_dim(arrivals, other_first, group_count, 0)
        swapped = lax.ppermute(theirs, "grp", [(0, 1), (1, 0)])
        from_0 = jnp.where(grp_index == 0, mine, swapped)
        from_1 = jnp.where(grp_index == 0, swapped, mine)
        chunk = jnp.stack([from_0, from_1], axis=2)
        per_group = EPOCHS * 2 * capacity
        chunk = chunk.reshape(group_count * per_group, antennas)
        chunk = jnp.pad(chunk, ((0, 112 - group_count * per_group), (0, 0)))
        gathered = lax.all_gather(chunk, "row")

    with jax.named_scope("planes"):
        pieces = list(make_pieces(x_index.reshape(1), inverse))
        for d in (1, 2, 3):
            pieces[d] = along_x(pieces[d], d)
        square = to_planes(jnp.stack(pieces, axis=1))
        symbol_part = jnp.einsum(
            "grc,gcs->grs", inverse, symbols.astype(f32), precision=highest
        )
        precoded = jnp.sum(to_planes(symbol_part), axis=0)

    plane_group = first_group + jnp.minimum(col_index, group_count - 1)
    slot_plane = lax.dynamic_slice_in_dim(slots, plane_group, 1, 0).reshape(1, TOTAL)
    row_ids = first_row + jnp.arange(user_rows, dtype=jnp.int32)

    cells_mine = lax.dynamic_slice_in_dim(arrival_cell, first_group, group_count, 0)[..., 0]
    slots_mine = lax.dynamic_slice_in_dim(slots, first_group, group_count, 0)
    slots_mine = slots_mine.reshape(group_count, 1, TOTAL)
    cell_table = (cells_mine[..., None] == jnp.arange(cell_count, dtype=jnp.int32)).astype(
        jnp.int32
    )
    owners = jnp.sum(cell_table * cell_owner, axis=-1)
    arrival_order = jnp.arange(ARRIVE, dtype=jnp.int32)
    earlier = (cells_mine[..., :, None] == cells_mine[..., None, :]) & (
        arrival_order[:, None] < arrival_order[None, :]
    )
    ranking = jnp.sum(earlier.astype(jnp.int32), axis=-2)
    with jax.named_scope("places"):
        offset = jnp.arange(group_count, dtype=jnp.int32) * per_group % 16
        epoch = jnp.arange(EPOCHS, dtype=jnp.int32)
        inside = offset[:, None] + epoch[None, :] * 2 * capacity
        inside = inside[:, :, None] + owners // 16 * capacity + ranking
        place = (owners % 16 * WINDOW + inside).reshape(group_count, 1, TOTAL)
        plane_place = lax.dynamic_slice_in_dim(
            place, jnp.minimum(col_index, group_count - 1), 1, 0
        ).reshape(1, TOTAL)

    with jax.named_scope("columns"):
        gathered, square, precoded = lax.optimization_barrier((gathered, square, precoded))
        both = make_columns(row_index.reshape(1), gathered, channels, place)
        both = lax.all_to_all(both, "col", 0, 0, tiled=True)
        summed = jnp.sum(both.astype(f32), axis=0)
        own = summed[:user_rows].astype(bf16)
        by_row = [own] + [along_x(own, d) for d in (1, 2, 3)]
        by_col = [own] + [along_y(own, -d) for d in (1, 2, 3)]

    with jax.named_scope("schur"):
        where = jnp.stack([y_index, row_index, first_row])
        base = make_target(where, summed, precoded, slot_plane, plane_place)
        block0, block1, block2, block3, packed = make_middle(where, square, by_row, by_col, base)
        weighted = block0
        for d, block in ((1, block1), (2, block2), (3, block3)):
            weighted = weighted + along_x(block, -d).astype(f32)
        weighted_all = lax.all_gather(weighted.astype(bf16), "row")
        packed = packed.reshape(16, SHARE, TOTAL + STREAMS)
        shared = lax.all_to_all(packed, "row", 0, 0, tiled=True)
        shared = jnp.sum(shared.astype(f32), axis=0)
        share_ids = row_index * SHARE + jnp.arange(SHARE, dtype=jnp.int32)
        identity = loading * (
            share_ids[:, None] == jnp.arange(TOTAL, dtype=jnp.int32)[None, :]
        ).astype(f32)
        schur_rows = identity - shared[:, :TOTAL]
        ready = jnp.concatenate([schur_rows, shared[:, TOTAL:]], axis=1)
        ready = jnp.broadcast_to(ready[None], (16, SHARE, TOTAL + STREAMS))
        whole = lax.all_to_all(ready, "row", 0, 0, tiled=True).reshape(TOTAL, TOTAL + STREAMS)

    with jax.named_scope("users"):
        channel = make_channel(first_arg, gathered, channels, place, slots_mine)
        whole, channel = lax.optimization_barrier((whole, channel))
        pivots, users = make_solve(first_arg, whole, weighted, precoded, slot_plane)
        users_side = lax.all_to_all(users, "col", 0, 0, tiled=True)

    with jax.named_scope("update"):
        changes = make_update(
            jnp.stack([first_row, col_index]), weighted, whole, pivots, weighted_all, slot_plane
        )
        changes = [changes[0]] + [along_z(changes[d], d) for d in (1, 2, 3)]

    with jax.named_scope("signal"):
        signal_part = make_signal(users_side, channel)
        received = lax.all_to_all(signal_part, "row", 0, 0, tiled=True)
        signal = jnp.sum(received.astype(f32), axis=0)
        power = jnp.sum(signal * signal, axis=(1, 2))
        power, changes = lax.optimization_barrier((power, changes))
        power = jnp.broadcast_to(power[None, None, :], (64, 1, group_count))
        power = lax.all_to_all(power, ("row", "col"), 0, 0, tiled=True)
        total_power = jnp.sum(power, axis=(0, 1)) / (STREAMS * ANTENNAS)
        transmit = signal * lax.rsqrt(total_power + epsilon)[:, None, None]
        transmit = jnp.swapaxes(transmit, 0, 1)

    with jax.named_scope("final"):
        col_ids = col_index * user_cols + jnp.arange(user_cols, dtype=jnp.int32)
        diagonal = row_ids[:, None] == col_ids[None, :]
        full = jnp.any(slots_mine == row_ids[None, :, None], axis=2)
        gone = jnp.where(diagonal[None] & full[:, :, None], 1.0 / loading, 0.0)
        updated = []
        for g in range(group_count):
            step = (col_index - g) % 4
            add = changes[0]
            for d in (1, 2, 3):
                add = jnp.where(step == d, changes[d], add)
            updated.append(inverse[g] - gone[g] + add.astype(f32))
        updated = jnp.stack(updated, axis=0)
    return (updated, transmit)


def solution(mesh):
    placed = (
        P("grp", "row", "col"),
        P("grp", "row", "col"),
        P(None, None, ("grp", "row"), "col"),
        P(),
        P(),
        P(),
        P("grp", "col", None),
    )
    return jax.shard_map(
        local,
        mesh=mesh,
        in_specs=placed,
        out_specs=(P("grp", "row", "col"), P("row", "grp", "col")),
        check_vma=False,
    )
```
